128 devices in a mesh: seq: 16 (over z, x), head: 8 (over y, core).
Axes of the slice: x: 4, y: 4, z: 4, core: 2. Of those that a mesh axis runs over, the one named last changes fastest.
Arguments:
- queries: float32 [16384, 4096], P('seq', 'head'), may hold values from -8 to 8
- key_rows: float32 [16384, 1024], P('seq', 'head'), may hold values from -8 to 8
- value_vectors: float32 [16384, 1024], P('seq', 'head'), may hold values from -6 to 6
- vertical_blocks: int32 [32, 8], replicated, may hold values from 0 to 255, all different within a row
- slash_offsets: int32 [32, 3], replicated, may hold values from 0 to 31, all different within a row
- prompt_length: int32 [1], replicated, may hold values from 4096 to 8191
- out_weight: float32 [4096, 4096], P('head'), may hold values from -0.09375 to 0.09375
Outputs:
- projected: float32 [16384, 4096], P('seq', 'head')
The draws below stay inside these ranges and needn't reach their ends.
Inputs may be any that keep to these rules, and one draw needn't show every extreme that they name: `vertical_blocks`: each head's 8 blocks are all different, and every block of the slab is named by some head. `slash_offsets`: each head's 3 values are all different.
All inputs are finite; a program needn't handle non-finite values.
Results may differ from the reference program's by a relative error of at most 0.0003.
Values sent between devices are 32-bit elements; how exact they have to be, the bound alone decides.
No kernel may reach another device: no remote copies, remote signals or barrier semaphores. Data moves between devices by JAX's collectives and lax.ppermute only.
A program may use at most 128 MiB of HBM per device.

```python
import math
import jax
import jax.numpy as jnp
from jax import lax

QUERY_HEADS = 32
KEY_VALUE_HEADS = 8
HEAD_SIZE = 128
D = 4096
TOK_DEV = 1024
NV = 8
NS = 3
SLAB_TOKENS = 16384


def draw_queries(key, part):
    key = jax.random.fold_in(key, 1)
    return jnp.clip(jax.random.normal(key, (SLAB_TOKENS, QUERY_HEADS * HEAD_SIZE), jnp.float32), -4.0, 4.0)


def draw_key_rows(key, part):
    key = jax.random.fold_in(key, 2)
    return jnp.clip(jax.random.normal(key, (SLAB_TOKENS, KEY_VALUE_HEADS * HEAD_SIZE), jnp.float32), -4.0, 4.0)


def level_of(own_key, dims, cuts, low, top_value):
    loudness = 1.0
    for dim, parts in cuts:
        draws = jax.random.uniform(jax.random.fold_in(jax.random.fold_in(own_key, 6), dim), (parts,), jnp.float32, low / len(cuts), top_value / len(cuts))
        loudness = loudness * jnp.repeat(jnp.exp(draws), dims[dim] // parts).reshape((-1,) + (1,) * (len(dims) - 1 - dim))
    return loudness


def choose_distinct(key, rows, amount, top, lift):
    order = jax.random.permutation(jax.random.fold_in(key, 1), amount)
    favour = order
    for power in range(3):
        favour = favour * favour // amount
    favour = favour * lift // amount
    chance = jax.random.randint(jax.random.fold_in(key, 2), (rows, amount), 0, 4096) + favour
    fixed_rows = jax.random.permutation(jax.random.fold_in(key, 3), rows)[jnp.arange(amount) % rows]
    chance = jnp.where(jnp.arange(rows)[:, None] == fixed_rows[None, :], 1 << 14, chance)
    merit = chance * amount + jnp.arange(amount)
    return lax.top_k(merit.astype(jnp.int32), top)[1].astype(jnp.int32)


def bell_draw(stream_key, dims, width, most, pieces=(), kind=jnp.bfloat16):
    level = level_of(stream_key, dims, pieces, -0.22, 0.18) if pieces else 1.0
    result = jax.random.normal(stream_key, dims, jnp.float32) * width * level
    return jnp.minimum(jnp.maximum(result, -most), most).astype(kind)


def setup_inputs(seed: int = 0) -> dict:
    arg_keys = jax.random.split(jax.random.key(seed), 8)
    queries = draw_queries(jax.random.fold_in(arg_keys[7], 71), 0)
    key_rows = draw_key_rows(jax.random.fold_in(arg_keys[7], 71), 0)
    value_vectors = bell_draw(arg_keys[2], (SLAB_TOKENS, KEY_VALUE_HEADS * HEAD_SIZE), 1.0, 6.0, ((0, 16), (1, 8)), jnp.float32)
    vertical_blocks = choose_distinct(arg_keys[3], QUERY_HEADS, SLAB_TOKENS // 64, NV, 256)
    slash_offsets = choose_distinct(arg_keys[4], QUERY_HEADS, 2 * TOK_DEV // 64, NS, 0)
    prompt_length = jax.random.randint(arg_keys[5], (1,), SLAB_TOKENS // 4, SLAB_TOKENS // 2).astype(jnp.int32)
    out_weight = bell_draw(arg_keys[6], (QUERY_HEADS * HEAD_SIZE, D), (QUERY_HEADS * HEAD_SIZE) ** -0.5, 0.09375, ((0, 8),), jnp.float32)
    return dict(queries=queries, key_rows=key_rows, value_vectors=value_vectors, vertical_blocks=vertical_blocks, slash_offsets=slash_offsets, prompt_length=prompt_length, out_weight=out_weight)


def attend_head(query_head, key_head, value_head, vert_row, slash_row, prompt_end):
    blocks = SLAB_TOKENS // 64
    score_scale = 1.0 / math.sqrt(HEAD_SIZE)
    query_blocks = query_head.reshape(blocks, 64, HEAD_SIZE)
    key_blocks = key_head.reshape(blocks, 64, HEAD_SIZE)
    value_blocks = value_head.reshape(blocks, 64, HEAD_SIZE)
    inside = jnp.arange(64, dtype=jnp.int32)
    query_pos = jnp.arange(blocks, dtype=jnp.int32)[:, None] * 64 + inside[None, :]
    vert_keys = key_blocks[vert_row].reshape(NV * 64, HEAD_SIZE)
    vert_values = value_blocks[vert_row].reshape(NV * 64, HEAD_SIZE)
    vert_pos = (vert_row[:, None] * 64 + inside[None, :]).reshape(NV * 64)
    vert_scores = jnp.einsum('brd,kd->brk', query_blocks, vert_keys, precision=lax.Precision.HIGHEST) * score_scale
    vert_seen = (vert_pos[None, None, :] <= query_pos[:, :, None]) | (vert_pos[None, None, :] < prompt_end)
    offsets = jnp.concatenate([jnp.zeros((1,), jnp.int32), slash_row + 1])
    slash_block = jnp.arange(blocks, dtype=jnp.int32)[:, None] - offsets[None, :]
    repeated = jnp.any(slash_block[:, :, None] == vert_row[None, None, :], axis=-1)
    usable = (slash_block >= 0) & jnp.logical_not(repeated)
    clipped = jnp.maximum(slash_block, 0)
    slash_keys = key_blocks[clipped]
    slash_values = value_blocks[clipped]
    slash_scores = jnp.einsum('brd,bnkd->brnk', query_blocks, slash_keys, precision=lax.Precision.HIGHEST) * score_scale
    slash_pos = clipped[:, None, :, None] * 64 + inside[None, None, None, :]
    slash_seen = usable[:, None, :, None] & ((slash_pos <= query_pos[:, :, None, None]) | (slash_pos < prompt_end))
    vert_scores = jnp.where(vert_seen, vert_scores, -jnp.inf)
    slash_scores = jnp.where(slash_seen, slash_scores, -jnp.inf)
    row_max = jnp.maximum(lax.optimization_barrier(jnp.max(vert_scores, axis=-1)), lax.optimization_barrier(jnp.max(slash_scores, axis=(-2, -1))))
    vert_weights = jnp.exp(vert_scores - row_max[:, :, None])
    slash_weights = jnp.exp(slash_scores - row_max[:, :, None, None])
    row_total = lax.optimization_barrier(jnp.sum(vert_weights, axis=-1)) + lax.optimization_barrier(jnp.sum(slash_weights, axis=(-2, -1)))
    mixed_rows = jnp.einsum('brk,kd->brd', vert_weights, vert_values, precision=lax.Precision.HIGHEST)
    mixed_rows = mixed_rows + jnp.einsum('brnk,bnkd->brd', slash_weights, slash_values, precision=lax.Precision.HIGHEST)
    return (mixed_rows / row_total[:, :, None]).reshape(SLAB_TOKENS, HEAD_SIZE)

def reference(queries, key_rows, value_vectors, vertical_blocks, slash_offsets, prompt_length, out_weight):
    query_group_width = QUERY_HEADS // KEY_VALUE_HEADS

    def one_head(head):
        query_head = lax.dynamic_slice_in_dim(queries, head * HEAD_SIZE, HEAD_SIZE, 1)
        kv_head = head // query_group_width
        key_head = lax.dynamic_slice_in_dim(key_rows, kv_head * HEAD_SIZE, HEAD_SIZE, 1)
        value_head = lax.dynamic_slice_in_dim(value_vectors, kv_head * HEAD_SIZE, HEAD_SIZE, 1)
        return attend_head(query_head, key_head, value_head, vertical_blocks[head], slash_offsets[head], prompt_length[0])
    heads_out = lax.map(one_head, jnp.arange(QUERY_HEADS, dtype=jnp.int32))
    joined = heads_out.transpose(1, 0, 2).reshape(SLAB_TOKENS, QUERY_HEADS * HEAD_SIZE)
    return jnp.dot(joined, out_weight, precision=lax.Precision.HIGHEST, preferred_element_type=jnp.float32)
```

```python
import functools
import math

import jax
import jax.numpy as jnp
from jax import lax
from jax.experimental import pallas as pl
from jax.experimental.pallas import tpu as pltpu
from jax.sharding import PartitionSpec as P

HEAD_SIZE = 128
BLOCK = 64
TILE = 256
FAR = 1 << 30
LOW = -1e30
SMALL = pl.CostEstimate(flops=1024, bytes_accessed=1024, transcendentals=0)


def pick_kernel(place, held, keys, values, both, picked):
    both[:, 0:HEAD_SIZE] = keys[...]
    both[:, HEAD_SIZE:] = values[...]
    for slot in range(picked.shape[0] // BLOCK):
        rows = pl.ds(slot * BLOCK, BLOCK)

        @pl.when(held[slot] == 1)
        def _():
            source = pl.ds(pl.multiple_of(place[slot] * BLOCK, BLOCK), BLOCK)
            picked[rows, 0:HEAD_SIZE] = keys[source, :]
            picked[rows, HEAD_SIZE:] = values[source, :]

        @pl.when(held[slot] == 0)
        def _():
            picked[rows, :] = jnp.zeros((BLOCK, 2 * HEAD_SIZE), jnp.float32)


def pick_blocks(place, held, keys, values):
    slots = place.shape[0]
    smem = pl.BlockSpec(memory_space=pltpu.SMEM)
    vmem = pl.BlockSpec(memory_space=pltpu.VMEM)
    return pl.pallas_call(
        pick_kernel,
        out_shape=[
            jax.ShapeDtypeStruct((keys.shape[0], 2 * HEAD_SIZE), jnp.float32),
            jax.ShapeDtypeStruct((slots * BLOCK, 2 * HEAD_SIZE), jnp.float32),
        ],
        in_specs=[smem, smem, vmem, vmem],
        out_specs=[vmem, vmem],
        compiler_params=pltpu.CompilerParams(vmem_limit_bytes=16 << 20),
    )(place, held, keys, values)


def split(x):
    high = x.astype(jnp.bfloat16)
    return high, (x - high.astype(jnp.float32)).astype(jnp.bfloat16)


def attend_kernel(
    first_row, scale, back, start, q, kv2, kv1, kv0, named, vert_pos, slash_pos, out,
    near_k, near_v, vert_k, vert_v,
):
    tile = pl.program_id(0)
    head = pl.program_id(1)

    def put_key(target, at, x):
        high, low = split(x)
        target[at, 0:128] = high
        target[at, 128:256] = high
        target[at, 256:384] = low

    def put_value(target, at, x):
        high, low = split(x)
        target[at, 0:128] = high
        target[at, 128:256] = low

    @pl.when((tile == 0) & (head == 0))
    def _():
        rows = kv0.shape[0]
        for part, kv in enumerate((kv2, kv1, kv0)):
            for step in range(rows // TILE):
                at = pl.ds(part * rows + step * TILE, TILE)
                put_key(near_k, at, kv[pl.ds(step * TILE, TILE), 0:HEAD_SIZE])
                put_value(near_v, at, kv[pl.ds(step * TILE, TILE), HEAD_SIZE:])
        for step in range(named.shape[0] // TILE):
            at = pl.ds(step * TILE, TILE)
            put_key(vert_k, at, named[at, 0:HEAD_SIZE])
            put_value(vert_v, at, named[at, HEAD_SIZE:])

    dot = functools.partial(lax.dot_general, preferred_element_type=jnp.float32)
    rows_by_rows = (((1,), (1,)), ((), ()))
    plain = (((1,), (0,)), ((), ()))
    q_high, q_low = split(q[...] * scale)
    q_parts = jnp.concatenate([q_high, q_low, q_high], axis=1)
    vert = vert_k.shape[0] // 4
    vert_rows = pl.ds(pl.multiple_of(head * vert, vert), vert)
    vert_scores = dot(q_parts, vert_k[vert_rows, :], rows_by_rows)
    place = first_row[0] + start + tile * TILE
    q_pos = place + lax.broadcasted_iota(jnp.int32, (TILE, 1), 0)
    vert_scores = jnp.where(vert_pos[head] <= q_pos, vert_scores, LOW)

    local = start // BLOCK + tile * (TILE // BLOCK)
    slash_scores = []
    near = []
    for j in range(TILE // BLOCK):
        spots = [
            pl.ds(pl.multiple_of((local + j + back[head, n]) * BLOCK, BLOCK), BLOCK)
            for n in range(4)
        ]
        near.append(spots)
        keys = jnp.concatenate([near_k[s, :] for s in spots], axis=0)
        score = dot(q_parts[j * BLOCK : (j + 1) * BLOCK], keys, rows_by_rows)
        seen = slash_pos[head, local + j] <= q_pos[j * BLOCK : (j + 1) * BLOCK]
        slash_scores.append(jnp.where(seen, score, LOW))
    slash_scores = jnp.concatenate(slash_scores, axis=0)

    top = jnp.maximum(
        jnp.max(vert_scores, axis=1, keepdims=True), jnp.max(slash_scores, axis=1, keepdims=True)
    )
    vert_w = jnp.exp(vert_scores - top)
    slash_w = jnp.exp(slash_scores - top)
    total = jnp.sum(vert_w, axis=1, keepdims=True) + jnp.sum(slash_w, axis=1, keepdims=True)
    vert_high, vert_low = split(vert_w)
    slash_high, slash_low = split(slash_w)
    wide = dot(vert_high, vert_v[vert_rows, :], plain)
    mixed = wide[:, :128] + wide[:, 128:] + dot(vert_low, vert_v[vert_rows, 0:128], plain)
    parts = []
    for j in range(TILE // BLOCK):
        values = jnp.concatenate([near_v[s, :] for s in near[j]], axis=0)
        mine = slice(j * BLOCK, (j + 1) * BLOCK)
        wide = dot(slash_high[mine], values, plain)
        parts.append(wide[:, :128] + wide[:, 128:] + dot(slash_low[mine], values[:, :128], plain))
    out[...] = (mixed + jnp.concatenate(parts, axis=0)) / total


def attend(q, start, rows, first_row, back, near, named, vert_pos, slash_pos):
    heads = q.shape[1] // HEAD_SIZE
    smem = pl.BlockSpec(memory_space=pltpu.SMEM)
    vmem = pl.BlockSpec(memory_space=pltpu.VMEM)
    window = sum(kv.shape[0] for kv in near)
    kernel = lambda first, back_ref, *refs: attend_kernel(
        first, 1.0 / math.sqrt(HEAD_SIZE), back_ref, start, *refs
    )
    base = start // TILE
    return pl.pallas_call(
        kernel,
        grid=(rows // TILE, heads),
        out_shape=jax.ShapeDtypeStruct((rows, heads * HEAD_SIZE), jnp.float32),
        in_specs=[smem, smem, pl.BlockSpec((TILE, HEAD_SIZE), lambda t, h: (base + t, h))]
        + [vmem] * 6,
        out_specs=pl.BlockSpec((TILE, HEAD_SIZE), lambda t, h: (t, h)),
        scratch_shapes=[
            pltpu.VMEM((window, 384), jnp.bfloat16),
            pltpu.VMEM((window, 256), jnp.bfloat16),
            pltpu.VMEM((named.shape[0], 384), jnp.bfloat16),
            pltpu.VMEM((named.shape[0], 256), jnp.bfloat16),
        ],
        compiler_params=pltpu.CompilerParams(vmem_limit_bytes=40 << 20),
        cost_estimate=SMALL,
    )(first_row, back, q, *near, named, vert_pos, slash_pos)


def take_kernel(core, w, out):
    out[...] = w[...]


def take_columns(weight, core, width):
    rows, columns = weight.shape
    count = columns // (2 * width)
    return pl.pallas_call(
        take_kernel,
        out_shape=jax.ShapeDtypeStruct((rows, count * width), jnp.float32),
        grid_spec=pltpu.PrefetchScalarGridSpec(
            num_scalar_prefetch=1,
            grid=(count,),
            in_specs=[pl.BlockSpec((rows, width), lambda i, c: (0, 2 * i + c[0]))],
            out_specs=pl.BlockSpec((rows, width), lambda i, c: (0, i)),
        ),
        compiler_params=pltpu.CompilerParams(vmem_limit_bytes=16 << 20),
        cost_estimate=SMALL,
    )(core, weight)


def halves_kernel(core, own, other, high, low):
    rows = own.shape[0]
    for first, ref in ((0, own), (rows, other)):
        high[0, first : first + rows], low[0, first : first + rows] = split(ref[...])


def weight_halves(own, other, core, width):
    rows = own.shape[0]
    count = other.shape[1] // width
    shape = jax.ShapeDtypeStruct((count, 2 * rows, width), jnp.bfloat16)
    spec = pl.BlockSpec((1, 2 * rows, width), lambda i, c: (i, 0, 0))
    return pl.pallas_call(
        halves_kernel,
        out_shape=[shape, shape],
        grid_spec=pltpu.PrefetchScalarGridSpec(
            num_scalar_prefetch=1,
            grid=(count,),
            in_specs=[
                pl.BlockSpec((rows, width), lambda i, c: (0, 2 * i + c[0])),
                pl.BlockSpec((rows, width), lambda i, c: (0, i)),
            ],
            out_specs=[spec, spec],
        ),
        compiler_params=pltpu.CompilerParams(vmem_limit_bytes=24 << 20),
        cost_estimate=SMALL,
    )(core, own, other)


def project_kernel(order, own, other, high, low, first, rest, x_high, x_low):
    depth = own.shape[1]

    @pl.when(pl.program_id(0) == 0)
    def _():
        x_high[:, :depth], x_low[:, :depth] = split(own[...])
        x_high[:, depth:], x_low[:, depth:] = split(other[...])

    dot = functools.partial(jnp.dot, preferred_element_type=jnp.float32)
    term = dot(x_high[...], high[0]) + (dot(x_high[...], low[0]) + dot(x_low[...], high[0]))

    @pl.when(pl.program_id(0) == 0)
    def _():
        first[...] = term

    @pl.when(pl.program_id(0) > 0)
    def _():
        rest[0] = term


def project(own, other, high, low, order):
    rows, depth = own.shape
    count, _, width = high.shape
    x_spec = pl.BlockSpec((rows, depth), lambda i, o: (0, 0))
    w_spec = pl.BlockSpec((1, 2 * depth, width), lambda i, o: (o[i], 0, 0))
    return pl.pallas_call(
        project_kernel,
        out_shape=[
            jax.ShapeDtypeStruct((rows, width), jnp.float32),
            jax.ShapeDtypeStruct((count - 1, rows, width), jnp.float32),
        ],
        grid_spec=pltpu.PrefetchScalarGridSpec(
            num_scalar_prefetch=1,
            grid=(count,),
            in_specs=[x_spec, x_spec, w_spec, w_spec],
            out_specs=[
                pl.BlockSpec((rows, width), lambda i, o: (0, 0)),
                pl.BlockSpec((1, rows, width), lambda i, o: (jnp.maximum(i - 1, 0), 0, 0)),
            ],
            scratch_shapes=[pltpu.VMEM((rows, 2 * depth), jnp.bfloat16)] * 2,
        ),
        compiler_params=pltpu.CompilerParams(vmem_limit_bytes=24 << 20),
        cost_estimate=SMALL,
    )(order, own, other, high, low)


def body(
    queries, key_rows, value_vectors, vertical_blocks, slash_offsets, prompt_length, out_weight
):
    rows = queries.shape[0]
    blocks = rows // BLOCK
    heads = queries.shape[1] // HEAD_SIZE
    seq_size = lax.axis_size("seq")
    seq_index = lax.axis_index("seq")
    head_index = lax.axis_index("head")
    vert = lax.dynamic_slice_in_dim(vertical_blocks, head_index * heads, heads, 0)
    slash = lax.dynamic_slice_in_dim(slash_offsets, head_index * heads, heads, 0)
    prompt = prompt_length[0]

    def shift(x, far):
        return lax.ppermute(x, "seq", [(i, i + far) for i in range(seq_size - far)])

    named = vert.reshape(-1)
    held = (named // blocks == seq_index).astype(jnp.int32)
    both, part = pick_blocks(named % blocks, held, key_rows, value_vectors)
    near = (shift(both, 2), shift(both, 1), both)
    part = part.reshape(seq_size, part.shape[0] // seq_size, part.shape[1])
    share = jnp.sum(lax.all_to_all(part, "seq", 0, 0), axis=0)
    copies = jnp.broadcast_to(share[None], part.shape)
    named_rows = lax.all_to_all(copies, "seq", 0, 0).reshape(-1, part.shape[2])

    head_size = lax.axis_size("head")
    swap = [(i, i ^ 1) for i in range(head_size)]
    core = (head_index % 2).reshape(1)
    width = out_weight.shape[1] // head_size
    other_weight = lax.ppermute(take_columns(out_weight, 1 - core, width), "head", swap)
    high, low = weight_halves(out_weight, other_weight, core, width)

    inside = jnp.arange(BLOCK, dtype=jnp.int32)
    vert_pos = vert[:, :, None] * BLOCK + inside
    vert_pos = jnp.where(vert_pos < prompt, -1, vert_pos).reshape(heads, 1, -1)
    offsets = jnp.concatenate([jnp.zeros((heads, 1), jnp.int32), slash + 1], axis=1)
    ids = seq_index * blocks + jnp.arange(blocks, dtype=jnp.int32)
    slash_block = ids[None, :, None] - offsets[:, None, :]
    repeated = jnp.any(slash_block[:, :, :, None] == vert[:, None, None, :], axis=-1)
    usable = (slash_block >= 0) & jnp.logical_not(repeated)
    slash_pos = slash_block[..., None] * BLOCK + inside
    slash_pos = jnp.where(slash_pos < prompt, -1, slash_pos)
    slash_pos = jnp.where(usable[..., None], slash_pos, FAR).reshape(heads, blocks, 1, -1)
    first_row = (seq_index * rows).reshape(1)
    back = 2 * blocks - offsets

    chips = head_size // 2
    chip = head_index // 2
    steps = jnp.arange(chips, dtype=jnp.int32)
    orders = ((chip + 2 * chips - 1 - steps) % chips, (chip + 1 + steps) % chips)
    rings = (
        [(i, (i + 2) % head_size) for i in range(head_size)],
        [(i, (i + head_size - 2) % head_size) for i in range(head_size)],
    )
    piece = rows // 4
    sums, terms = [], []
    q, high, low = lax.optimization_barrier((queries, high, low))
    for part in range(4):
        own = attend(
            q, part * piece, piece, first_row, back, near, named_rows, vert_pos, slash_pos
        )
        other = lax.ppermute(own, "head", swap)
        first, rest = project(own, other, high, low, orders[part % 2])
        sums.append(first)
        terms.append(rest)
        if part == 1:
            q, *sums = lax.optimization_barrier((q, *sums))
    for step in range(chips - 1):
        for part in range(4):
            moved = lax.ppermute(sums[part], "head", rings[part % 2])
            sums[part] = moved + terms[part][step]
    return jnp.concatenate(sums, axis=0)


def solution(mesh):
    placed = (P("seq", "head"), P("seq", "head"), P("seq", "head"), P(), P(), P(), P("head", None))
    return jax.shard_map(
        body, mesh=mesh, in_specs=placed, out_specs=P("seq", "head"), check_vma=False
    )
```

```python
import functools
import math

import jax
import jax.numpy as jnp
from jax import lax
from jax.experimental import pallas as pl
from jax.experimental.pallas import tpu as pltpu
from jax.sharding import PartitionSpec as P

HEAD_SIZE = 128
BLOCK = 64
TILE = 256
FAR = 1 << 30
LOW = -1e30
SMALL = pl.CostEstimate(flops=1024, bytes_accessed=1024, transcendentals=0)


def pick_kernel(place, held, *refs):
    *pieces, first, second, rows = refs
    size = pieces[0].shape[0]
    for at, piece in enumerate(pieces):
        rows[at * size : (at + 1) * size, :] = piece[...]
    slots = first.shape[0] // BLOCK
    for slot in range(2 * slots):
        out = first if slot < slots else second
        target = pl.ds(slot % slots * BLOCK, BLOCK)

        @pl.when(held[slot] == 1)
        def _():
            start = pl.multiple_of(place[slot] * BLOCK, BLOCK)
            out[target, :] = rows[pl.ds(start, BLOCK), :]

        @pl.when(held[slot] == 0)
        def _():
            out[target, :] = jnp.zeros((BLOCK, HEAD_SIZE), jnp.float32)


def pick_blocks(place, held, pieces):
    half = place.shape[0] // 2 * BLOCK
    smem = pl.BlockSpec(memory_space=pltpu.SMEM)
    vmem = pl.BlockSpec(memory_space=pltpu.VMEM)
    out = jax.ShapeDtypeStruct((half, HEAD_SIZE), jnp.float32)
    size = pieces[0].shape[0]
    return pl.pallas_call(
        pick_kernel,
        out_shape=[out, out],
        in_specs=[smem, smem] + [vmem] * len(pieces),
        out_specs=[vmem] * 2,
        scratch_shapes=[pltpu.VMEM((len(pieces) * size, HEAD_SIZE), jnp.float32)],
        compiler_params=pltpu.CompilerParams(vmem_limit_bytes=16 << 20),
        cost_estimate=SMALL,
    )(place, held, *pieces)


def split(x):
    high = x.astype(jnp.bfloat16)
    return high, (x - high.astype(jnp.float32)).astype(jnp.bfloat16)


def fold(x):
    half = x.shape[0] // 2
    return x[:half] + x[half:]


def attend_kernel(
    start, first_row, back, wraps, q, k_far, k_far_wrap, k_left, k_left_wrap, k_own,
    v_far_a, v_far_b, v_left, v_own, k_a, k_b, v_a, v_b, vert_pos, slash_pos, out,
    near_k, near_v, vert_k, vert_v,
):
    turn = pl.program_id(0)
    scale = 1.0 / math.sqrt(HEAD_SIZE)

    def put(target, first, pieces):
        for piece in pieces:
            count = piece.shape[0]
            high, low = split(piece[...])
            target[first : first + count, 0:HEAD_SIZE] = high
            target[first : first + count, HEAD_SIZE:] = low
            first += count

    @pl.when((turn == 0) & (pl.program_id(1) == 0))
    def _():
        rows = k_own.shape[0]
        for at, (plain, wrapped) in enumerate(((k_far, k_far_wrap), (k_left, k_left_wrap))):

            @pl.when(wraps[at] == 0)
            def _():
                put(near_k, at * rows, (plain,))

            @pl.when(wraps[at] == 1)
            def _():
                put(near_k, at * rows, (wrapped,))

        put(near_k, 2 * rows, (k_own,))
        put(near_v, 0, (v_far_a, v_far_b, v_left, v_own))
        put(vert_k, 0, (k_a, k_b))
        put(vert_v, 0, (v_a, v_b))

    dot = functools.partial(lax.dot_general, preferred_element_type=jnp.float32)
    across = (((1,), (1,)), ((), ()))
    down = (((1,), (0,)), ((), ()))
    q_pos = first_row[0] + start + turn * TILE + lax.broadcasted_iota(jnp.int32, (TILE, 1), 0)
    local = start // BLOCK + turn * (TILE // BLOCK)
    per_block = TILE // BLOCK
    vert = vert_pos.shape[2]
    pair = q.shape[1] // HEAD_SIZE
    for part in range(pair):
        head = pl.program_id(1) * pair + part
        columns = slice(part * HEAD_SIZE, (part + 1) * HEAD_SIZE)
        high, low = split(q[:, columns] * scale)
        high, low = (jnp.concatenate([x, x], axis=1) for x in (high, low))
        rows = pl.ds(pl.multiple_of(head * vert, vert), vert)
        both = jnp.concatenate([high, low], axis=0)
        vert_scores = fold(dot(both, vert_k[rows, :], across))
        vert_scores = jnp.where(vert_pos[head] <= q_pos, vert_scores, LOW)

        slash_scores, near = [], []
        for j in range(per_block):
            spots = [
                pl.ds(pl.multiple_of((local + j + back[head, n]) * BLOCK, BLOCK), BLOCK)
                for n in range(4)
            ]
            near.append(spots)
            keys = jnp.concatenate([near_k[s, :] for s in spots], axis=0)
            mine = slice(j * BLOCK, (j + 1) * BLOCK)
            score = fold(dot(jnp.concatenate([high[mine], low[mine]], axis=0), keys, across))
            slash_scores.append(jnp.where(slash_pos[head, local + j] <= q_pos[mine], score, LOW))
        slash_scores = jnp.concatenate(slash_scores, axis=0)

        top = jnp.maximum(
            jnp.max(vert_scores, axis=1, keepdims=True),
            jnp.max(slash_scores, axis=1, keepdims=True),
        )
        vert_w = jnp.exp(vert_scores - top)
        slash_w = jnp.exp(slash_scores - top)
        total = jnp.sum(vert_w, axis=1, keepdims=True) + jnp.sum(slash_w, axis=1, keepdims=True)
        mixed = fold(dot(jnp.concatenate(split(vert_w), axis=0), vert_v[rows, :], down))
        slash_high, slash_low = split(slash_w)
        parts = []
        for j in range(per_block):
            values = jnp.concatenate([near_v[s, :] for s in near[j]], axis=0)
            mine = slice(j * BLOCK, (j + 1) * BLOCK)
            weights = jnp.concatenate([slash_high[mine], slash_low[mine]], axis=0)
            parts.append(fold(dot(weights, values, down)))
        mixed = mixed + jnp.concatenate(parts, axis=0)
        out[:, columns] = (mixed[:, :HEAD_SIZE] + mixed[:, HEAD_SIZE:]) / total


def attend(q, start, rows, first_row, back, wraps, arrays):
    heads = q.shape[1] // HEAD_SIZE
    pair = 2
    smem = pl.BlockSpec(memory_space=pltpu.SMEM)
    vmem = pl.BlockSpec(memory_space=pltpu.VMEM)
    near, vert = 3 * q.shape[0], heads * 8 * BLOCK
    base = start // TILE
    return pl.pallas_call(
        functools.partial(attend_kernel, start),
        grid=(rows // TILE, heads // pair),
        out_shape=jax.ShapeDtypeStruct((rows, heads * HEAD_SIZE), jnp.float32),
        in_specs=[smem, smem, smem]
        + [pl.BlockSpec((TILE, pair * HEAD_SIZE), lambda t, h: (base + t, h))]
        + [vmem] * len(arrays),
        out_specs=pl.BlockSpec((TILE, pair * HEAD_SIZE), lambda t, h: (t, h)),
        scratch_shapes=[
            pltpu.VMEM((n, 2 * HEAD_SIZE), jnp.bfloat16) for n in (near, near, vert, vert)
        ],
        compiler_params=pltpu.CompilerParams(vmem_limit_bytes=40 << 20),
        cost_estimate=SMALL,
    )(first_row, back, wraps, q, *arrays)


def project_kernel(order, own, other, w_own, w_other, first_a, rest_a, first_b, rest_b, x, w):
    rows, depth = own.shape
    half = first_a.shape[0]
    step = pl.program_id(0)

    @pl.when(step == 0)
    def _():
        for at, ref in ((0, own), (depth, other)):
            x[0:rows, at : at + depth], x[rows:, at : at + depth] = split(ref[...])

    for at, ref in ((0, w_own), (depth, w_other)):
        w[0, at : at + depth, :], w[1, at : at + depth, :] = split(ref[...])
    dot = functools.partial(jnp.dot, preferred_element_type=jnp.float32)
    term = fold(dot(x[...], w[0])) + dot(x[0:rows, :], w[1])

    @pl.when(step == 0)
    def _():
        first_a[...] = term[:half]

    @pl.when(step > 0)
    def _():
        rest_a[0] = term[:half]

    @pl.when(step == 2)
    def _():
        first_b[...] = term[half:]

    @pl.when(step != 2)
    def _():
        rest_b[0] = term[half:]


def project(own, other, part, rows, w_own, w_other, order):
    depth = own.shape[1]
    half = rows // 2
    count = order.shape[0]
    width = w_own.shape[1] // (2 * count)
    x_spec = pl.BlockSpec((rows, depth), lambda i, o: (part, 0))
    w_spec = pl.BlockSpec((depth, width), lambda i, o: (0, o[i]))
    first = jax.ShapeDtypeStruct((half, width), jnp.float32)
    rest = jax.ShapeDtypeStruct((count - 1, half, width), jnp.float32)
    first_spec = pl.BlockSpec((half, width), lambda i, o: (0, 0))
    back_step = lambda i: jnp.where(i == 0, 1, jnp.where(i == 3, 2, 0))
    return pl.pallas_call(
        project_kernel,
        out_shape=[first, rest, first, rest],
        grid_spec=pltpu.PrefetchScalarGridSpec(
            num_scalar_prefetch=1,
            grid=(count,),
            in_specs=[x_spec, x_spec, w_spec, w_spec],
            out_specs=[
                first_spec,
                pl.BlockSpec((1, half, width), lambda i, o: (jnp.maximum(i - 1, 0), 0, 0)),
                first_spec,
                pl.BlockSpec((1, half, width), lambda i, o: (back_step(i), 0, 0)),
            ],
            scratch_shapes=[
                pltpu.VMEM((2 * rows, 2 * depth), jnp.bfloat16),
                pltpu.VMEM((2, 2 * depth, width), jnp.bfloat16),
            ],
        ),
        compiler_params=pltpu.CompilerParams(vmem_limit_bytes=48 << 20),
        cost_estimate=SMALL,
    )(order, own, other, w_own, w_other)


def body(
    queries, key_rows, value_vectors, vertical_blocks, slash_offsets, prompt_length, out_weight
):
    rows = queries.shape[0]
    blocks = rows // BLOCK
    heads = queries.shape[1] // HEAD_SIZE
    seq_index = lax.axis_index("seq")
    head_index = lax.axis_index("head")
    head_size = lax.axis_size("head")
    core = head_index % 2
    chips = head_size // 2

    x, z = seq_index % 4, seq_index // 4
    ids = range(lax.axis_size("seq"))
    right = [(i, i // 4 * 4 + (i + 1) % 4) for i in ids]
    left = [(i, i // 4 * 4 + (i + 3) % 4) for i in ids]
    over = [(i, i // 4 * 4 + (i + 2) % 4) for i in ids]
    up = [(i, (i + 4) % 16) for i in ids]
    down = [(i, (i + 12) % 16) for i in ids]
    send = lambda a, pairs: lax.ppermute(a, "seq", pairs)
    swapped = lambda a, bits: send(a, [(i, i ^ bits) for i in ids])

    k_left = send(key_rows, right)
    k_right = send(key_rows, left)
    v_below = send(value_vectors, up)
    v_above = send(value_vectors, down)
    swap = [(i, i ^ 1) for i in range(head_size)]
    w_other = lax.ppermute(out_weight, "head", swap)

    vert = lax.dynamic_slice_in_dim(vertical_blocks, head_index * heads, heads, 0)
    slash = lax.dynamic_slice_in_dim(slash_offsets, head_index * heads, heads, 0)
    prompt = prompt_length[0]
    named = vert.reshape(-1)
    inside = jnp.arange(BLOCK, dtype=jnp.int32)
    vert_pos = vert[:, :, None] * BLOCK + inside
    vert_pos = jnp.where(vert_pos < prompt, -1, vert_pos).reshape(heads, 1, -1)
    offsets = jnp.concatenate([jnp.zeros((heads, 1), jnp.int32), slash + 1], axis=1)
    block_ids = seq_index * blocks + jnp.arange(blocks, dtype=jnp.int32)
    slash_block = block_ids[None, :, None] - offsets[:, None, :]
    repeated = jnp.any(slash_block[:, :, :, None] == vert[:, None, None, :], axis=-1)
    usable = (slash_block >= 0) & jnp.logical_not(repeated)
    slash_pos = slash_block[..., None] * BLOCK + inside
    slash_pos = jnp.where(slash_pos < prompt, -1, slash_pos)
    slash_pos = jnp.where(usable[..., None], slash_pos, FAR).reshape(heads, blocks, 1, -1)
    first_row = (seq_index * rows).reshape(1)
    back = 2 * blocks - offsets
    wraps = jnp.stack([x < 2, x == 0]).astype(jnp.int32)
    order = (head_index // 2 + 2 * chips - 1 - jnp.arange(chips, dtype=jnp.int32)) % chips
    order = 2 * order + core
    owner = named // blocks
    at = named % blocks
    k_place, k_held = (owner % 4 - x) % 4 * blocks + at, (owner // 4 == z).astype(jnp.int32)
    v_place, v_held = (owner // 4 - z) % 4 * blocks + at, (owner % 4 == x).astype(jnp.int32)
    small = (vert_pos, slash_pos, first_row, back, wraps, order, k_place, k_held, v_place, v_held)

    (k_left, k_right, v_below, v_above), small = lax.optimization_barrier(
        ((k_left, k_right, v_below, v_above), small)
    )
    vert_pos, slash_pos, first_row, back, wraps, order, k_place, k_held, v_place, v_held = small
    k_far = send(k_right, left)
    v_beyond = send(v_above, down)
    v_left = send(jnp.where(x == 3, v_below, value_vectors), right)
    source = jnp.where(x >= 2, v_below, value_vectors)
    half = rows // 2
    k_far, v_beyond, v_left = lax.optimization_barrier((k_far, v_beyond, v_left))
    v_far_a = send(source[:half], over)
    v_far_b = send(source[half:], left)
    k_left_wrap = send(k_left, [(i, i + 4) for i in ids if i % 4 == 0 and i + 4 in ids])

    k_named = pick_blocks(k_place, k_held, (key_rows, k_right, k_far, k_left))
    v_named = pick_blocks(v_place, v_held, (value_vectors, v_above, v_beyond, v_below))
    named = [*k_named, *v_named]
    one, two = (4, 12, 1, 3), (12, 4, 3, 1)
    named = [a + swapped(a, bits) for a, bits in zip(named, one)]
    v_far_a, v_far_b, k_left_wrap, *named = lax.optimization_barrier(
        (v_far_a, v_far_b, k_left_wrap, *named)
    )
    v_far_b = send(v_far_b, left)
    k_far_wrap = send(k_far, [(i, i + 4) for i in ids if i % 4 < 2 and i + 4 in ids])
    more = [swapped(a, bits) for a, bits in zip(named, two)]
    v_far_b, k_far_wrap, *more = lax.optimization_barrier((v_far_b, k_far_wrap, *more))
    named = [a + b for a, b in zip(named, more)]

    arrays = (k_far, k_far_wrap, k_left, k_left_wrap, key_rows, v_far_a, v_far_b, v_left)
    arrays = (*arrays, value_vectors, *named, vert_pos, slash_pos)

    rings = [[(i, (i + d) % head_size) for i in range(head_size)] for d in (2, head_size - 2)]
    q = queries
    pairs = []
    for start in (0, half):
        own = attend(q, start, half, first_row, back, wraps, arrays)
        q, own = lax.optimization_barrier((q, own))
        pairs.append((own, lax.ppermute(own, "head", swap)))
    sums, terms = [], []
    for which, part, count in ((0, 0, half // 2), (0, 1, half // 2), (1, 0, half)):
        own, other = pairs[which]
        first_a, rest_a, first_b, rest_b = project(
            own, other, part, count, out_weight, w_other, order
        )
        order, first_a, first_b = lax.optimization_barrier((order, first_a, first_b))
        sums.append([first_a, first_b])
        terms.append([rest_a, rest_b])
    for step in range(chips - 1):
        for part in range(len(sums)):
            for way in range(2):
                moved = lax.ppermute(sums[part][way], "head", rings[way])
                sums[part][way] = moved + terms[part][way][step]
    return jnp.concatenate(sums[0] + sums[1] + sums[2], axis=0)


def solution(mesh):
    placed = (P("seq", "head"), P("seq", "head"), P("seq", "head"), P(), P(), P(), P("head", None))
    return jax.shard_map(
        body, mesh=mesh, in_specs=placed, out_specs=P("seq", "head"), check_vma=False
    )
```

```python
import functools
import math

import jax
import jax.numpy as jnp
from jax import lax
from jax.experimental import pallas as pl
from jax.experimental.pallas import tpu as pltpu
from jax.sharding import PartitionSpec as P

HEAD_SIZE = 128
BLOCK = 64
TILE = 256
FAR = 1 << 30
LOW = -1e30
LARGE = pl.CostEstimate(flops=12 << 30, bytes_accessed=16 << 20, transcendentals=0)
SMALL = pl.CostEstimate(flops=1024, bytes_accessed=1024, transcendentals=0)


def pick_kernel(place, held, *refs):
    *pieces, first, second, rows = refs
    size = pieces[0].shape[0]
    for at, piece in enumerate(pieces):
        rows[at * size : (at + 1) * size, :] = piece[...]
    slots = first.shape[0] // BLOCK
    for slot in range(2 * slots):
        out = first if slot < slots else second
        target = pl.ds(slot % slots * BLOCK, BLOCK)

        @pl.when(held[slot] == 1)
        def _():
            start = pl.multiple_of(place[slot] * BLOCK, BLOCK)
            out[target, :] = rows[pl.ds(start, BLOCK), :]

        @pl.when(held[slot] == 0)
        def _():
            out[target, :] = jnp.zeros((BLOCK, HEAD_SIZE), jnp.float32)


def pick_blocks(place, held, pieces):
    half = place.shape[0] // 2 * BLOCK
    smem = pl.BlockSpec(memory_space=pltpu.SMEM)
    vmem = pl.BlockSpec(memory_space=pltpu.VMEM)
    out = jax.ShapeDtypeStruct((half, HEAD_SIZE), jnp.float32)
    size = pieces[0].shape[0]
    return pl.pallas_call(
        pick_kernel,
        out_shape=[out, out],
        in_specs=[smem, smem] + [vmem] * len(pieces),
        out_specs=[vmem] * 2,
        scratch_shapes=[pltpu.VMEM((len(pieces) * size, HEAD_SIZE), jnp.float32)],
        compiler_params=pltpu.CompilerParams(vmem_limit_bytes=16 << 20),
        cost_estimate=SMALL,
    )(place, held, *pieces)


def split(x):
    high = x.astype(jnp.bfloat16)
    return high, (x - high.astype(jnp.float32)).astype(jnp.bfloat16)


def fold(x):
    half = x.shape[0] // 2
    return x[:half] + x[half:]


def attend_kernel(
    start, first_row, back, wraps, q, k_far, k_far_wrap, k_left, k_left_wrap, k_own,
    v_far_a, v_far_b, v_left, v_own, k_a, k_b, v_a, v_b, vert_pos, slash_pos, out,
    near_k, near_v, vert_k, vert_v,
):
    turn = pl.program_id(0)
    scale = 1.0 / math.sqrt(HEAD_SIZE)

    def put(target, first, pieces):
        for piece in pieces:
            count = piece.shape[0]
            high, low = split(piece[...])
            target[first : first + count, 0:HEAD_SIZE] = high
            target[first : first + count, HEAD_SIZE:] = low
            first += count

    @pl.when((turn == 0) & (pl.program_id(1) == 0))
    def _():
        rows = k_own.shape[0]
        for at, (plain, wrapped) in enumerate(((k_far, k_far_wrap), (k_left, k_left_wrap))):

            @pl.when(wraps[at] == 0)
            def _():
                put(near_k, at * rows, (plain,))

            @pl.when(wraps[at] == 1)
            def _():
                put(near_k, at * rows, (wrapped,))

        put(near_k, 2 * rows, (k_own,))
        put(near_v, 0, (v_far_a, v_far_b, v_left, v_own))
        put(vert_k, 0, (k_a, k_b))
        put(vert_v, 0, (v_a, v_b))

    dot = functools.partial(lax.dot_general, preferred_element_type=jnp.float32)
    across = (((1,), (1,)), ((), ()))
    down = (((1,), (0,)), ((), ()))
    q_pos = first_row[0] + start + turn * TILE + lax.broadcasted_iota(jnp.int32, (TILE, 1), 0)
    local = start // BLOCK + turn * (TILE // BLOCK)
    per_block = TILE // BLOCK
    vert = vert_pos.shape[2]
    pair = q.shape[1] // HEAD_SIZE
    for part in range(pair):
        head = pl.program_id(1) * pair + part
        columns = slice(part * HEAD_SIZE, (part + 1) * HEAD_SIZE)
        high, low = split(q[:, columns] * scale)
        high, low = (jnp.concatenate([x, x], axis=1) for x in (high, low))
        rows = pl.ds(pl.multiple_of(head * vert, vert), vert)
        both = jnp.concatenate([high, low], axis=0)
        vert_scores = fold(dot(both, vert_k[rows, :], across))
        vert_scores = jnp.where(vert_pos[head] <= q_pos, vert_scores, LOW)

        slash_scores, near = [], []
        for j in range(per_block):
            spots = [
                pl.ds(pl.multiple_of((local + j + back[head, n]) * BLOCK, BLOCK), BLOCK)
                for n in range(4)
            ]
            near.append(spots)
            keys = jnp.concatenate([near_k[s, :] for s in spots], axis=0)
            mine = slice(j * BLOCK, (j + 1) * BLOCK)
            score = fold(dot(jnp.concatenate([high[mine], low[mine]], axis=0), keys, across))
            slash_scores.append(jnp.where(slash_pos[head, local + j] <= q_pos[mine], score, LOW))
        slash_scores = jnp.concatenate(slash_scores, axis=0)

        top = jnp.maximum(
            jnp.max(vert_scores, axis=1, keepdims=True),
            jnp.max(slash_scores, axis=1, keepdims=True),
        )
        vert_w = jnp.exp(vert_scores - top)
        slash_w = jnp.exp(slash_scores - top)
        total = jnp.sum(vert_w, axis=1, keepdims=True) + jnp.sum(slash_w, axis=1, keepdims=True)
        mixed = fold(dot(jnp.concatenate(split(vert_w), axis=0), vert_v[rows, :], down))
        slash_high, slash_low = split(slash_w)
        parts = []
        for j in range(per_block):
            values = jnp.concatenate([near_v[s, :] for s in near[j]], axis=0)
            mine = slice(j * BLOCK, (j + 1) * BLOCK)
            weights = jnp.concatenate([slash_high[mine], slash_low[mine]], axis=0)
            parts.append(fold(dot(weights, values, down)))
        mixed = mixed + jnp.concatenate(parts, axis=0)
        out[:, columns] = (mixed[:, :HEAD_SIZE] + mixed[:, HEAD_SIZE:]) / total


def attend(q, start, rows, first_row, back, wraps, arrays):
    heads = q.shape[1] // HEAD_SIZE
    pair = 2
    smem = pl.BlockSpec(memory_space=pltpu.SMEM)
    vmem = pl.BlockSpec(memory_space=pltpu.VMEM)
    near, vert = 3 * q.shape[0], heads * 8 * BLOCK
    base = start // TILE
    return pl.pallas_call(
        functools.partial(attend_kernel, start),
        grid=(rows // TILE, heads // pair),
        out_shape=jax.ShapeDtypeStruct((rows, heads * HEAD_SIZE), jnp.float32),
        in_specs=[smem, smem, smem]
        + [pl.BlockSpec((TILE, pair * HEAD_SIZE), lambda t, h: (base + t, h))]
        + [vmem] * len(arrays),
        out_specs=pl.BlockSpec((TILE, pair * HEAD_SIZE), lambda t, h: (t, h)),
        scratch_shapes=[
            pltpu.VMEM((n, 2 * HEAD_SIZE), jnp.bfloat16) for n in (near, near, vert, vert)
        ],
        compiler_params=pltpu.CompilerParams(vmem_limit_bytes=40 << 20),
        cost_estimate=LARGE,
    )(first_row, back, wraps, q, *arrays)


def project_kernel(order, own, other, w_own, w_other, first_a, rest_a, first_b, rest_b, x, w):
    rows, depth = own.shape
    half = first_a.shape[0]
    step = pl.program_id(0)

    @pl.when(step == 0)
    def _():
        for at, ref in ((0, own), (depth, other)):
            x[0:rows, at : at + depth], x[rows:, at : at + depth] = split(ref[...])

    for at, ref in ((0, w_own), (depth, w_other)):
        w[0, at : at + depth, :], w[1, at : at + depth, :] = split(ref[...])
    dot = functools.partial(jnp.dot, preferred_element_type=jnp.float32)
    term = fold(dot(x[...], w[0])) + dot(x[0:rows, :], w[1])

    @pl.when(step == 0)
    def _():
        first_a[...] = term[:half]

    @pl.when(step > 0)
    def _():
        rest_a[0] = term[:half]

    @pl.when(step == 2)
    def _():
        first_b[...] = term[half:]

    @pl.when(step != 2)
    def _():
        rest_b[0] = term[half:]


def project(own, other, w_own, w_other, order):
    rows, depth = own.shape
    half = rows // 2
    count = order.shape[0]
    width = w_own.shape[1] // (2 * count)
    x_spec = pl.BlockSpec((rows, depth), lambda i, o: (0, 0))
    w_spec = pl.BlockSpec((depth, width), lambda i, o: (0, o[i]))
    first = jax.ShapeDtypeStruct((half, width), jnp.float32)
    rest = jax.ShapeDtypeStruct((count - 1, half, width), jnp.float32)
    first_spec = pl.BlockSpec((half, width), lambda i, o: (0, 0))
    back_step = lambda i: jnp.where(i == 0, 1, jnp.where(i == 3, 2, 0))
    first_a, rest_a, first_b, rest_b = pl.pallas_call(
        project_kernel,
        out_shape=[first, rest, first, rest],
        grid_spec=pltpu.PrefetchScalarGridSpec(
            num_scalar_prefetch=1,
            grid=(count,),
            in_specs=[x_spec, x_spec, w_spec, w_spec],
            out_specs=[
                first_spec,
                pl.BlockSpec((1, half, width), lambda i, o: (jnp.maximum(i - 1, 0), 0, 0)),
                first_spec,
                pl.BlockSpec((1, half, width), lambda i, o: (back_step(i), 0, 0)),
            ],
            scratch_shapes=[
                pltpu.VMEM((2 * rows, 2 * depth), jnp.bfloat16),
                pltpu.VMEM((2, 2 * depth, width), jnp.bfloat16),
            ],
        ),
        compiler_params=pltpu.CompilerParams(vmem_limit_bytes=48 << 20),
        cost_estimate=LARGE,
    )(order, own, other, w_own, w_other)
    return (first_a, first_b), (rest_a, rest_b)


def body(
    queries, key_rows, value_vectors, vertical_blocks, slash_offsets, prompt_length, out_weight
):
    rows = queries.shape[0]
    blocks = rows // BLOCK
    heads = queries.shape[1] // HEAD_SIZE
    seq_index = lax.axis_index("seq")
    head_index = lax.axis_index("head")
    head_size = lax.axis_size("head")
    core = head_index % 2
    chips = head_size // 2

    x, z = seq_index % 4, seq_index // 4
    ids = range(lax.axis_size("seq"))
    right = [(i, i // 4 * 4 + (i + 1) % 4) for i in ids]
    left = [(i, i // 4 * 4 + (i + 3) % 4) for i in ids]
    over = [(i, i // 4 * 4 + (i + 2) % 4) for i in ids]
    up = [(i, (i + 4) % 16) for i in ids]
    down = [(i, (i + 12) % 16) for i in ids]
    send = lambda a, pairs: lax.ppermute(a, "seq", pairs)
    swapped = lambda a, bits: send(a, [(i, i ^ bits) for i in ids])

    k_left = send(key_rows, right)
    k_right = send(key_rows, left)
    v_below = send(value_vectors, up)
    v_above = send(value_vectors, down)
    swap = [(i, i ^ 1) for i in range(head_size)]
    w_other = lax.ppermute(out_weight, "head", swap)

    vert = lax.dynamic_slice_in_dim(vertical_blocks, head_index * heads, heads, 0)
    slash = lax.dynamic_slice_in_dim(slash_offsets, head_index * heads, heads, 0)
    prompt = prompt_length[0]
    named = vert.reshape(-1)
    inside = jnp.arange(BLOCK, dtype=jnp.int32)
    vert_pos = vert[:, :, None] * BLOCK + inside
    vert_pos = jnp.where(vert_pos < prompt, -1, vert_pos).reshape(heads, 1, -1)
    offsets = jnp.concatenate([jnp.zeros((heads, 1), jnp.int32), slash + 1], axis=1)
    block_ids = seq_index * blocks + jnp.arange(blocks, dtype=jnp.int32)
    slash_block = block_ids[None, :, None] - offsets[:, None, :]
    repeated = jnp.any(slash_block[:, :, :, None] == vert[:, None, None, :], axis=-1)
    usable = (slash_block >= 0) & jnp.logical_not(repeated)
    slash_pos = slash_block[..., None] * BLOCK + inside
    slash_pos = jnp.where(slash_pos < prompt, -1, slash_pos)
    slash_pos = jnp.where(usable[..., None], slash_pos, FAR).reshape(heads, blocks, 1, -1)
    first_row = (seq_index * rows).reshape(1)
    back = 2 * blocks - offsets
    wraps = jnp.stack([x < 2, x == 0]).astype(jnp.int32)
    order = (head_index // 2 + 2 * chips - 1 - jnp.arange(chips, dtype=jnp.int32)) % chips
    order = 2 * order + core
    owner = named // blocks
    at = named % blocks
    k_place, k_held = (owner % 4 - x) % 4 * blocks + at, (owner // 4 == z).astype(jnp.int32)
    v_place, v_held = (owner // 4 - z) % 4 * blocks + at, (owner % 4 == x).astype(jnp.int32)
    small = (vert_pos, slash_pos, first_row, back, wraps, order, k_place, k_held, v_place, v_held)

    (k_left, k_right, v_below, v_above), small = lax.optimization_barrier(
        ((k_left, k_right, v_below, v_above), small)
    )
    vert_pos, slash_pos, first_row, back, wraps, order, k_place, k_held, v_place, v_held = small
    half = rows // 2
    source = jnp.where(x >= 2, v_below, value_vectors)
    v_left = jnp.where(x == 3, v_below, value_vectors)
    moved_left = send(jnp.concatenate([k_right, source[half:]]), left)
    v_beyond = send(v_above, down)
    moved_right = send(jnp.concatenate([v_left, source[:half]]), right)
    k_left_wrap = send(k_left, [(i, i + 4) for i in ids if i % 4 == 0 and i + 4 in ids])
    moved_left, v_beyond, moved_right, k_left_wrap = lax.optimization_barrier(
        (moved_left, v_beyond, moved_right, k_left_wrap)
    )
    k_far, v_far_b = moved_left[:rows], moved_left[rows:]
    v_left, v_far_a = moved_right[:rows], moved_right[rows:]

    k_named = pick_blocks(k_place, k_held, (key_rows, k_right, k_far, k_left))
    v_named = pick_blocks(v_place, v_held, (value_vectors, v_above, v_beyond, v_below))
    v_far_a = send(v_far_a, right)
    v_far_b = send(v_far_b, left)
    k_far_wrap = send(k_far, [(i, i + 4) for i in ids if i % 4 < 2 and i + 4 in ids])
    named = [*k_named, *v_named]
    one, two = (4, 12, 1, 3), (12, 4, 3, 1)
    named = [a + swapped(a, bits) for a, bits in zip(named, one)]
    v_far_a, v_far_b, k_far_wrap, *named = lax.optimization_barrier(
        (v_far_a, v_far_b, k_far_wrap, *named)
    )
    named = [a + swapped(a, bits) for a, bits in zip(named, two)]

    arrays = (k_far, k_far_wrap, k_left, k_left_wrap, key_rows, v_far_a, v_far_b, v_left)
    arrays = (*arrays, value_vectors, *named, vert_pos, slash_pos)

    rings = [[(i, (i + d) % head_size) for i in range(head_size)] for d in (2, head_size - 2)]
    ring = lambda parts: [lax.ppermute(p, "head", r) for p, r in zip(parts, rings)]
    add = lambda parts, terms, step: [p + t[step] for p, t in zip(parts, terms)]

    own = attend(queries, 0, half, first_row, back, wraps, arrays)
    other = lax.ppermute(own, "head", swap)
    first, terms = project(own, other, out_weight, w_other, order)
    q, *first = lax.optimization_barrier((queries, *first))
    moved = ring(first)
    own = attend(q, half, half, first_row, back, wraps, arrays)
    own, *moved = lax.optimization_barrier((own, *moved))
    other = lax.ppermute(own, "head", swap)
    sums = add(moved, terms, 0)
    order, *sums = lax.optimization_barrier((order, *sums))
    moved = ring(sums)
    later, later_terms = project(own, other, out_weight, w_other, order)
    *moved, later_a, later_b = lax.optimization_barrier((*moved, *later))
    sums, later = add(moved, terms, 1), (later_a, later_b)
    sums, later = add(ring(sums), terms, 2), add(ring(later), later_terms, 0)
    later = add(ring(later), later_terms, 1)
    later = add(ring(later), later_terms, 2)
    return jnp.concatenate([*sums, *later], axis=0)


def solution(mesh):
    placed = (P("seq", "head"), P("seq", "head"), P("seq", "head"), P(), P(), P(), P("head", None))
    return jax.shard_map(
        body, mesh=mesh, in_specs=placed, out_specs=P("seq", "head"), check_vma=False
    )
```

```python
import functools
import math

import jax
import jax.numpy as jnp
from jax import lax
from jax.experimental import pallas as pl
from jax.experimental.pallas import tpu as pltpu
from jax.sharding import PartitionSpec as P

HEAD_SIZE = 128
BLOCK = 64
TILE = 256
FAR = 1 << 30
LOW = -1e30
LARGE = pl.CostEstimate(flops=12 << 30, bytes_accessed=16 << 20, transcendentals=0)
SMALL = pl.CostEstimate(flops=1024, bytes_accessed=1024, transcendentals=0)


def pick_kernel(place, held, *refs):
    *pieces, first, second, rows = refs
    size = pieces[0].shape[0]
    for at, piece in enumerate(pieces):
        rows[at * size : (at + 1) * size, :] = piece[...]
    slots = first.shape[0] // BLOCK
    for slot in range(2 * slots):
        out = first if slot < slots else second
        target = pl.ds(slot % slots * BLOCK, BLOCK)

        @pl.when(held[slot] == 1)
        def _():
            start = pl.multiple_of(place[slot] * BLOCK, BLOCK)
            out[target, :] = rows[pl.ds(start, BLOCK), :]

        @pl.when(held[slot] == 0)
        def _():
            out[target, :] = jnp.zeros((BLOCK, HEAD_SIZE), jnp.float32)


def pick_blocks(place, held, pieces):
    half = place.shape[0] // 2 * BLOCK
    smem = pl.BlockSpec(memory_space=pltpu.SMEM)
    vmem = pl.BlockSpec(memory_space=pltpu.VMEM)
    out = jax.ShapeDtypeStruct((half, HEAD_SIZE), jnp.float32)
    size = pieces[0].shape[0]
    return pl.pallas_call(
        pick_kernel,
        out_shape=[out, out],
        in_specs=[smem, smem] + [vmem] * len(pieces),
        out_specs=[vmem] * 2,
        scratch_shapes=[pltpu.VMEM((len(pieces) * size, HEAD_SIZE), jnp.float32)],
        compiler_params=pltpu.CompilerParams(vmem_limit_bytes=16 << 20),
        cost_estimate=SMALL,
    )(place, held, *pieces)


def split(x):
    high = x.astype(jnp.bfloat16)
    return high, (x - high.astype(jnp.float32)).astype(jnp.bfloat16)


def fold(x):
    half = x.shape[0] // 2
    return x[:half] + x[half:]


def put_parts(target, first, pieces):
    for piece in pieces:
        count = piece.shape[0]
        high, low = split(piece[...])
        target[first : first + count, 0:HEAD_SIZE] = high
        target[first : first + count, HEAD_SIZE:] = low
        first += count


dot = functools.partial(lax.dot_general, preferred_element_type=jnp.float32)
ACROSS = (((1,), (1,)), ((), ()))
DOWN = (((1,), (0,)), ((), ()))
SCALE = math.log2(math.e) / math.sqrt(HEAD_SIZE)


def query_parts(q):
    return (jnp.concatenate([x, x], axis=1) for x in split(q * SCALE))


def weights_of(scores, top):
    weights = jnp.exp2(scores - top)
    return weights, jnp.sum(weights, axis=1, keepdims=True)


def near_kernel(
    first_row, back, wraps, q, k_far, k_far_wrap, k_left, k_left_wrap, k_own,
    v_far_a, v_far_b, v_left, v_own, slash_pos, out, stats, near_k, near_v,
):
    turn = pl.program_id(0)

    @pl.when((turn == 0) & (pl.program_id(1) == 0))
    def _():
        rows = k_own.shape[0]
        for at, (plain, wrapped) in enumerate(((k_far, k_far_wrap), (k_left, k_left_wrap))):

            @pl.when(wraps[at] == 0)
            def _():
                put_parts(near_k, at * rows, (plain,))

            @pl.when(wraps[at] == 1)
            def _():
                put_parts(near_k, at * rows, (wrapped,))

        put_parts(near_k, 2 * rows, (k_own,))
        put_parts(near_v, 0, (v_far_a, v_far_b, v_left, v_own))

    q_pos = first_row[0] + turn * TILE + lax.broadcasted_iota(jnp.int32, (TILE, 1), 0)
    per_block = TILE // BLOCK
    pair = q.shape[1] // HEAD_SIZE
    lane = lax.broadcasted_iota(jnp.int32, (TILE, HEAD_SIZE), 1)
    known = jnp.zeros((TILE, HEAD_SIZE), jnp.float32)
    for part in range(pair):
        head = pl.program_id(1) * pair + part
        columns = slice(part * HEAD_SIZE, (part + 1) * HEAD_SIZE)
        high, low = query_parts(q[:, columns])
        scores, near = [], []
        for j in range(per_block):
            block = turn * per_block + j
            spots = [
                pl.ds(pl.multiple_of((block + back[head, n]) * BLOCK, BLOCK), BLOCK)
                for n in range(4)
            ]
            near.append(spots)
            keys = jnp.concatenate([near_k[s, :] for s in spots], axis=0)
            mine = slice(j * BLOCK, (j + 1) * BLOCK)
            score = fold(dot(jnp.concatenate([high[mine], low[mine]], axis=0), keys, ACROSS))
            scores.append(jnp.where(slash_pos[head, block] <= q_pos[mine], score, LOW))
        scores = jnp.concatenate(scores, axis=0)
        top = jnp.max(scores, axis=1, keepdims=True)
        weights, total = weights_of(scores, top)
        w_high, w_low = split(weights)
        parts = []
        for j in range(per_block):
            values = jnp.concatenate([near_v[s, :] for s in near[j]], axis=0)
            mine = slice(j * BLOCK, (j + 1) * BLOCK)
            stacked = jnp.concatenate([w_high[mine], w_low[mine]], axis=0)
            parts.append(fold(dot(stacked, values, DOWN)))
        mixed = jnp.concatenate(parts, axis=0)
        out[:, columns] = mixed[:, :HEAD_SIZE] + mixed[:, HEAD_SIZE:]
        known = jnp.where(lane == 2 * part, top, known)
        known = jnp.where(lane == 2 * part + 1, total, known)
    stats[...] = known


def attend_near(q, first_row, back, wraps, arrays):
    rows, width = q.shape
    pair = 2
    count = width // (pair * HEAD_SIZE)
    smem = pl.BlockSpec(memory_space=pltpu.SMEM)
    vmem = pl.BlockSpec(memory_space=pltpu.VMEM)
    wide = pl.BlockSpec((TILE, pair * HEAD_SIZE), lambda t, h: (t, h))
    return pl.pallas_call(
        near_kernel,
        grid=(rows // TILE, count),
        out_shape=[
            jax.ShapeDtypeStruct((rows, width), jnp.float32),
            jax.ShapeDtypeStruct((rows, count * HEAD_SIZE), jnp.float32),
        ],
        in_specs=[smem, smem, smem, wide] + [vmem] * len(arrays),
        out_specs=[wide, pl.BlockSpec((TILE, HEAD_SIZE), lambda t, h: (t, h))],
        scratch_shapes=[pltpu.VMEM((3 * rows, 2 * HEAD_SIZE), jnp.bfloat16)] * 2,
        compiler_params=pltpu.CompilerParams(vmem_limit_bytes=40 << 20),
        cost_estimate=LARGE,
    )(first_row, back, wraps, q, *arrays)


def attend_kernel(
    start, first_row, q, near, stats, k_a, k_b, v_a, v_b, vert_pos, out, vert_k, vert_v
):
    turn = pl.program_id(0)

    @pl.when((turn == 0) & (pl.program_id(1) == 0))
    def _():
        put_parts(vert_k, 0, (k_a, k_b))
        put_parts(vert_v, 0, (v_a, v_b))

    q_pos = first_row[0] + start + turn * TILE + lax.broadcasted_iota(jnp.int32, (TILE, 1), 0)
    vert = vert_pos.shape[2]
    pair = q.shape[1] // HEAD_SIZE
    for part in range(pair):
        head = pl.program_id(1) * pair + part
        columns = slice(part * HEAD_SIZE, (part + 1) * HEAD_SIZE)
        rows = pl.ds(pl.multiple_of(head * vert, vert), vert)
        both = jnp.concatenate(list(query_parts(q[:, columns])), axis=0)
        scores = fold(dot(both, vert_k[rows, :], ACROSS))
        scores = jnp.where(vert_pos[head] <= q_pos, scores, LOW)
        near_top = stats[:, 2 * part : 2 * part + 1]
        top = jnp.maximum(jnp.max(scores, axis=1, keepdims=True), near_top)
        weights, total = weights_of(scores, top)
        keep = jnp.exp2(near_top - top)
        total = total + keep * stats[:, 2 * part + 1 : 2 * part + 2]
        mixed = fold(dot(jnp.concatenate(split(weights), axis=0), vert_v[rows, :], DOWN))
        mixed = mixed[:, :HEAD_SIZE] + mixed[:, HEAD_SIZE:] + keep * near[:, columns]
        out[:, columns] = mixed / total


def attend(q, near, stats, start, rows, first_row, arrays):
    width = q.shape[1]
    heads = width // HEAD_SIZE
    pair = 2
    smem = pl.BlockSpec(memory_space=pltpu.SMEM)
    vmem = pl.BlockSpec(memory_space=pltpu.VMEM)
    base = start // TILE
    wide = pl.BlockSpec((TILE, pair * HEAD_SIZE), lambda t, h: (base + t, h))
    return pl.pallas_call(
        functools.partial(attend_kernel, start),
        grid=(rows // TILE, heads // pair),
        out_shape=jax.ShapeDtypeStruct((rows, width), jnp.float32),
        in_specs=[smem, wide, wide, pl.BlockSpec((TILE, HEAD_SIZE), lambda t, h: (base + t, h))]
        + [vmem] * len(arrays),
        out_specs=pl.BlockSpec((TILE, pair * HEAD_SIZE), lambda t, h: (t, h)),
        scratch_shapes=[pltpu.VMEM((heads * 8 * BLOCK, 2 * HEAD_SIZE), jnp.bfloat16)] * 2,
        compiler_params=pltpu.CompilerParams(vmem_limit_bytes=40 << 20),
        cost_estimate=LARGE,
    )(first_row, q, near, stats, *arrays)


def halves_kernel(order, own, other, out):
    rows = own.shape[0]
    for first, ref in ((0, own), (rows, other)):
        high, low = split(ref[...])
        out[0, first : first + rows] = high
        out[0, first + 2 * rows : first + 3 * rows] = low


def weight_halves(own, other, order):
    rows = own.shape[0]
    count = order.shape[0]
    width = own.shape[1] // (2 * count)
    w_spec = pl.BlockSpec((rows, width), lambda i, o: (0, o[i]))
    return pl.pallas_call(
        halves_kernel,
        out_shape=jax.ShapeDtypeStruct((count, 4 * rows, width), jnp.bfloat16),
        grid_spec=pltpu.PrefetchScalarGridSpec(
            num_scalar_prefetch=1,
            grid=(count,),
            in_specs=[w_spec, w_spec],
            out_specs=pl.BlockSpec((1, 4 * rows, width), lambda i, o: (i, 0, 0)),
        ),
        compiler_params=pltpu.CompilerParams(vmem_limit_bytes=24 << 20),
        cost_estimate=LARGE,
    )(order, own, other)


def project_kernel(own, other, w, first_a, rest_a, first_b, rest_b, x):
    depth = own.shape[1]
    half = first_a.shape[0]
    step = pl.program_id(0)

    @pl.when(step == 0)
    def _():
        for at, ref in ((0, own), (depth, other)):
            high, low = split(ref[...])
            x[:, at : at + depth] = high
            x[:, at + 2 * depth : at + 3 * depth] = high
            x[:, at + 4 * depth : at + 5 * depth] = low

    term = dot(x[:, : 4 * depth], w[0], DOWN) + dot(x[:, 4 * depth :], w[0, : 2 * depth], DOWN)

    @pl.when(step == 0)
    def _():
        first_a[...] = term[:half]

    @pl.when(step > 0)
    def _():
        rest_a[0] = term[:half]

    @pl.when(step == 2)
    def _():
        first_b[...] = term[half:]

    @pl.when(step != 2)
    def _():
        rest_b[0] = term[half:]


def project(own, other, weights):
    rows, depth = own.shape
    half = rows // 2
    count, _, width = weights.shape
    x_spec = pl.BlockSpec((rows, depth), lambda i: (0, 0))
    first = jax.ShapeDtypeStruct((half, width), jnp.float32)
    rest = jax.ShapeDtypeStruct((count - 1, half, width), jnp.float32)
    first_spec = pl.BlockSpec((half, width), lambda i: (0, 0))
    back_step = lambda i: jnp.where(i == 0, 1, jnp.where(i == 3, 2, 0))
    first_a, rest_a, first_b, rest_b = pl.pallas_call(
        project_kernel,
        grid=(count,),
        out_shape=[first, rest, first, rest],
        in_specs=[x_spec, x_spec, pl.BlockSpec((1, 4 * depth, width), lambda i: (i, 0, 0))],
        out_specs=[
            first_spec,
            pl.BlockSpec((1, half, width), lambda i: (jnp.maximum(i - 1, 0), 0, 0)),
            first_spec,
            pl.BlockSpec((1, half, width), lambda i: (back_step(i), 0, 0)),
        ],
        scratch_shapes=[pltpu.VMEM((rows, 6 * depth), jnp.bfloat16)],
        compiler_params=pltpu.CompilerParams(vmem_limit_bytes=48 << 20),
        cost_estimate=LARGE,
    )(own, other, weights)
    return (first_a, first_b), (rest_a, rest_b)


def body(
    queries, key_rows, value_vectors, vertical_blocks, slash_offsets, prompt_length, out_weight
):
    rows = queries.shape[0]
    blocks = rows // BLOCK
    heads = queries.shape[1] // HEAD_SIZE
    seq_index = lax.axis_index("seq")
    head_index = lax.axis_index("head")
    head_size = lax.axis_size("head")
    core = head_index % 2
    chips = head_size // 2

    x, z = seq_index % 4, seq_index // 4
    ids = range(lax.axis_size("seq"))
    right = [(i, i // 4 * 4 + (i + 1) % 4) for i in ids]
    left = [(i, i // 4 * 4 + (i + 3) % 4) for i in ids]
    over = [(i, i // 4 * 4 + (i + 2) % 4) for i in ids]
    up = [(i, (i + 4) % 16) for i in ids]
    down = [(i, (i + 12) % 16) for i in ids]
    send = lambda a, pairs: lax.ppermute(a, "seq", pairs)
    swapped = lambda a, bits: send(a, [(i, i ^ bits) for i in ids])

    k_left = send(key_rows, right)
    k_right = send(key_rows, left)
    v_below = send(value_vectors, up)
    v_above = send(value_vectors, down)
    swap = [(i, i ^ 1) for i in range(head_size)]
    w_other = lax.ppermute(out_weight, "head", swap)

    vert = lax.dynamic_slice_in_dim(vertical_blocks, head_index * heads, heads, 0)
    slash = lax.dynamic_slice_in_dim(slash_offsets, head_index * heads, heads, 0)
    prompt = prompt_length[0]
    named = vert.reshape(-1)
    inside = jnp.arange(BLOCK, dtype=jnp.int32)
    vert_pos = vert[:, :, None] * BLOCK + inside
    vert_pos = jnp.where(vert_pos < prompt, -1, vert_pos).reshape(heads, 1, -1)
    offsets = jnp.concatenate([jnp.zeros((heads, 1), jnp.int32), slash + 1], axis=1)
    block_ids = seq_index * blocks + jnp.arange(blocks, dtype=jnp.int32)
    slash_block = block_ids[None, :, None] - offsets[:, None, :]
    repeated = jnp.any(slash_block[:, :, :, None] == vert[:, None, None, :], axis=-1)
    usable = (slash_block >= 0) & jnp.logical_not(repeated)
    slash_pos = slash_block[..., None] * BLOCK + inside
    slash_pos = jnp.where(slash_pos < prompt, -1, slash_pos)
    slash_pos = jnp.where(usable[..., None], slash_pos, FAR).reshape(heads, blocks, 1, -1)
    first_row = (seq_index * rows).reshape(1)
    back = 2 * blocks - offsets
    wraps = jnp.stack([x < 2, x == 0]).astype(jnp.int32)
    order = (head_index // 2 + 2 * chips - 1 - jnp.arange(chips, dtype=jnp.int32)) % chips
    order = 2 * order + core
    owner = named // blocks
    at = named % blocks
    k_place, k_held = (owner % 4 - x) % 4 * blocks + at, (owner // 4 == z).astype(jnp.int32)
    v_place, v_held = (owner // 4 - z) % 4 * blocks + at, (owner % 4 == x).astype(jnp.int32)
    small = (vert_pos, slash_pos, first_row, back, wraps, order, k_place, k_held, v_place, v_held)

    (k_left, k_right, v_below, v_above), small = lax.optimization_barrier(
        ((k_left, k_right, v_below, v_above), small)
    )
    vert_pos, slash_pos, first_row, back, wraps, order, k_place, k_held, v_place, v_held = small
    half = rows // 2
    source = jnp.where(x >= 2, v_below, value_vectors)
    v_left = jnp.where(x == 3, v_below, value_vectors)
    moved_left = send(jnp.concatenate([k_right, source[half:]]), left)
    v_beyond = send(v_above, down)
    moved_right = send(jnp.concatenate([v_left, source[:half]]), right)
    k_left_wrap = send(k_left, [(i, i + 4) for i in ids if i % 4 == 0 and i + 4 in ids])
    moved_left, v_beyond, moved_right, k_left_wrap = lax.optimization_barrier(
        (moved_left, v_beyond, moved_right, k_left_wrap)
    )
    k_far, v_far_b = moved_left[:rows], moved_left[rows:]
    v_left, v_far_a = moved_right[:rows], moved_right[rows:]

    k_named = pick_blocks(k_place, k_held, (key_rows, k_right, k_far, k_left))
    v_named = pick_blocks(v_place, v_held, (value_vectors, v_above, v_beyond, v_below))
    v_far_a = send(v_far_a, right)
    v_far_b = send(v_far_b, left)
    k_far_wrap = send(k_far, [(i, i + 4) for i in ids if i % 4 < 2 and i + 4 in ids])
    named = [*k_named, *v_named]
    one, two = (4, 12, 1, 3), (12, 4, 3, 1)
    more = [swapped(a, bits) for a, bits in zip(named, one)]
    weights = weight_halves(out_weight, w_other, order)
    weights, v_far_a, v_far_b, k_far_wrap, *more = lax.optimization_barrier(
        (weights, v_far_a, v_far_b, k_far_wrap, *more)
    )
    named = [a + b for a, b in zip(named, more)]
    arrays = (k_far, k_far_wrap, k_left, k_left_wrap, key_rows, v_far_a, v_far_b, v_left)
    arrays = (*arrays, value_vectors, slash_pos)
    near, stats = attend_near(queries, first_row, back, wraps, arrays)
    more = [swapped(a, bits) for a, bits in zip(named, two)]
    near, stats, *more = lax.optimization_barrier((near, stats, *more))
    arrays = (*(a + b for a, b in zip(named, more)), vert_pos)

    rings = [[(i, (i + d) % head_size) for i in range(head_size)] for d in (2, head_size - 2)]
    ring = lambda parts: [lax.ppermute(p, "head", r) for p, r in zip(parts, rings)]
    add = lambda parts, terms, step: [p + t[step] for p, t in zip(parts, terms)]

    own = attend(queries, near, stats, 0, half, first_row, arrays)
    other = lax.ppermute(own, "head", swap)
    first, terms = project(own, other, weights)
    q, *first = lax.optimization_barrier((queries, *first))
    moved = ring(first)
    own = attend(q, near, stats, half, half, first_row, arrays)
    own, *moved = lax.optimization_barrier((own, *moved))
    other = lax.ppermute(own, "head", swap)
    sums = add(moved, terms, 0)
    weights, *sums = lax.optimization_barrier((weights, *sums))
    moved = ring(sums)
    later, later_terms = project(own, other, weights)
    *moved, later_a, later_b = lax.optimization_barrier((*moved, *later))
    sums, later = add(moved, terms, 1), (later_a, later_b)
    sums, later = add(ring(sums), terms, 2), add(ring(later), later_terms, 0)
    later = add(ring(later), later_terms, 1)
    later = add(ring(later), later_terms, 2)
    return jnp.concatenate([*sums, *later], axis=0)


def solution(mesh):
    placed = (P("seq", "head"), P("seq", "head"), P("seq", "head"), P(), P(), P(), P("head", None))
    return jax.shard_map(
        body, mesh=mesh, in_specs=placed, out_specs=P("seq", "head"), check_vma=False
    )
```

```python
import functools
import math

import jax
import jax.numpy as jnp
from jax import lax
from jax.experimental import pallas as pl
from jax.experimental.pallas import tpu as pltpu
from jax.sharding import PartitionSpec as P

HEAD_SIZE = 128
BLOCK = 64
TILE = 256
FAR = 1 << 30
LOW = -1e30
LARGE = pl.CostEstimate(flops=4 << 30, bytes_accessed=4 << 20, transcendentals=0)
SMALL = pl.CostEstimate(flops=1024, bytes_accessed=1024, transcendentals=0)


def pick_kernel(place, held, *refs):
    *pieces, first, second, rows = refs
    size = pieces[0].shape[0]
    for at, piece in enumerate(pieces):
        rows[at * size : (at + 1) * size, :] = piece[...]
    slots = first.shape[0] // BLOCK
    for slot in range(2 * slots):
        out = first if slot < slots else second
        target = pl.ds(slot % slots * BLOCK, BLOCK)

        @pl.when(held[slot] == 1)
        def _():
            start = pl.multiple_of(place[slot] * BLOCK, BLOCK)
            out[target, :] = rows[pl.ds(start, BLOCK), :]

        @pl.when(held[slot] == 0)
        def _():
            out[target, :] = jnp.zeros((BLOCK, HEAD_SIZE), jnp.float32)


def pick_blocks(place, held, pieces):
    half = place.shape[0] // 2 * BLOCK
    smem = pl.BlockSpec(memory_space=pltpu.SMEM)
    vmem = pl.BlockSpec(memory_space=pltpu.VMEM)
    out = jax.ShapeDtypeStruct((half, HEAD_SIZE), jnp.float32)
    size = pieces[0].shape[0]
    return pl.pallas_call(
        pick_kernel,
        out_shape=[out, out],
        in_specs=[smem, smem] + [vmem] * len(pieces),
        out_specs=[vmem] * 2,
        scratch_shapes=[pltpu.VMEM((len(pieces) * size, HEAD_SIZE), jnp.float32)],
        compiler_params=pltpu.CompilerParams(vmem_limit_bytes=16 << 20),
        cost_estimate=SMALL,
    )(place, held, *pieces)


def split(x):
    high = x.astype(jnp.bfloat16)
    return high, (x - high.astype(jnp.float32)).astype(jnp.bfloat16)


def fold(x):
    half = x.shape[0] // 2
    return x[:half] + x[half:]


def put_parts(target, first, pieces):
    for piece in pieces:
        count = piece.shape[0]
        high, low = split(piece[...])
        target[first : first + count, 0:HEAD_SIZE] = high
        target[first : first + count, HEAD_SIZE:] = low
        first += count


dot = functools.partial(lax.dot_general, preferred_element_type=jnp.float32)
ACROSS = (((1,), (1,)), ((), ()))
DOWN = (((1,), (0,)), ((), ()))
SCALE = math.log2(math.e) / math.sqrt(HEAD_SIZE)


def query_parts(q):
    return (jnp.concatenate([x, x], axis=1) for x in split(q * SCALE))


def weights_of(scores, top):
    weights = jnp.exp2(scores - top)
    return weights, jnp.sum(weights, axis=1, keepdims=True)


def near_kernel(
    start, first_row, back, wraps, q, k_far, k_far_wrap, k_left, k_left_wrap, k_own,
    v_far_a, v_far_b, v_left, v_own, slash_pos, out, stats, near_k, near_v,
):
    turn = pl.program_id(0)

    @pl.when((turn == 0) & (pl.program_id(1) == 0))
    def _():
        rows = k_own.shape[0]
        for at, (plain, wrapped) in enumerate(((k_far, k_far_wrap), (k_left, k_left_wrap))):

            @pl.when(wraps[at] == 0)
            def _():
                put_parts(near_k, at * rows, (plain,))

            @pl.when(wraps[at] == 1)
            def _():
                put_parts(near_k, at * rows, (wrapped,))

        put_parts(near_k, 2 * rows, (k_own,))
        put_parts(near_v, 0, (v_far_a, v_far_b, v_left, v_own))

    q_pos = first_row[0] + start + turn * TILE + lax.broadcasted_iota(jnp.int32, (TILE, 1), 0)
    per_block = TILE // BLOCK
    pair = q.shape[1] // HEAD_SIZE
    lane = lax.broadcasted_iota(jnp.int32, (TILE, HEAD_SIZE), 1)
    known = jnp.zeros((TILE, HEAD_SIZE), jnp.float32)
    for part in range(pair):
        head = pl.program_id(1) * pair + part
        columns = slice(part * HEAD_SIZE, (part + 1) * HEAD_SIZE)
        high, low = query_parts(q[:, columns])
        scores, near = [], []
        for j in range(per_block):
            block = start // BLOCK + turn * per_block + j
            spots = [
                pl.ds(pl.multiple_of((block + back[head, n]) * BLOCK, BLOCK), BLOCK)
                for n in range(4)
            ]
            near.append(spots)
            keys = jnp.concatenate([near_k[s, :] for s in spots], axis=0)
            mine = slice(j * BLOCK, (j + 1) * BLOCK)
            score = fold(dot(jnp.concatenate([high[mine], low[mine]], axis=0), keys, ACROSS))
            scores.append(jnp.where(slash_pos[head, block] <= q_pos[mine], score, LOW))
        scores = jnp.concatenate(scores, axis=0)
        top = jnp.max(scores, axis=1, keepdims=True)
        weights, total = weights_of(scores, top)
        w_high, w_low = split(weights)
        parts = []
        for j in range(per_block):
            values = jnp.concatenate([near_v[s, :] for s in near[j]], axis=0)
            mine = slice(j * BLOCK, (j + 1) * BLOCK)
            stacked = jnp.concatenate([w_high[mine], w_low[mine]], axis=0)
            parts.append(fold(dot(stacked, values, DOWN)))
        mixed = jnp.concatenate(parts, axis=0)
        out[:, columns] = mixed[:, :HEAD_SIZE] + mixed[:, HEAD_SIZE:]
        known = jnp.where(lane == 2 * part, top, known)
        known = jnp.where(lane == 2 * part + 1, total, known)
    stats[...] = known


def attend_near(q, start, rows, first_row, back, wraps, arrays):
    width = q.shape[1]
    pair = 2
    count = width // (pair * HEAD_SIZE)
    base = start // TILE
    smem = pl.BlockSpec(memory_space=pltpu.SMEM)
    vmem = pl.BlockSpec(memory_space=pltpu.VMEM)
    wide = (TILE, pair * HEAD_SIZE)
    return pl.pallas_call(
        functools.partial(near_kernel, start),
        grid=(rows // TILE, count),
        out_shape=[
            jax.ShapeDtypeStruct((rows, width), jnp.float32),
            jax.ShapeDtypeStruct((rows, count * HEAD_SIZE), jnp.float32),
        ],
        in_specs=[smem, smem, smem, pl.BlockSpec(wide, lambda t, h: (base + t, h))]
        + [vmem] * len(arrays),
        out_specs=[
            pl.BlockSpec(wide, lambda t, h: (t, h)),
            pl.BlockSpec((TILE, HEAD_SIZE), lambda t, h: (t, h)),
        ],
        scratch_shapes=[pltpu.VMEM((3 * q.shape[0], 2 * HEAD_SIZE), jnp.bfloat16)] * 2,
        compiler_params=pltpu.CompilerParams(vmem_limit_bytes=40 << 20),
        cost_estimate=LARGE,
    )(first_row, back, wraps, q, *arrays)


def attend_kernel(
    start, first_row, q, near, stats, k_a, k_b, v_a, v_b, vert_pos, out_a, out_b, vert_k, vert_v
):
    turn = pl.program_id(0)

    @pl.when((turn == 0) & (pl.program_id(1) == 0))
    def _():
        put_parts(vert_k, 0, (k_a, k_b))
        put_parts(vert_v, 0, (v_a, v_b))

    q_pos = first_row[0] + start + turn * TILE + lax.broadcasted_iota(jnp.int32, (TILE, 1), 0)
    vert = vert_pos.shape[2]
    pair = q.shape[1] // HEAD_SIZE
    for part in range(pair):
        head = pl.program_id(1) * pair + part
        columns = slice(part * HEAD_SIZE, (part + 1) * HEAD_SIZE)
        rows = pl.ds(pl.multiple_of(head * vert, vert), vert)
        both = jnp.concatenate(list(query_parts(q[:, columns])), axis=0)
        scores = fold(dot(both, vert_k[rows, :], ACROSS))
        scores = jnp.where(vert_pos[head] <= q_pos, scores, LOW)
        near_top = stats[:, 2 * part : 2 * part + 1]
        top = jnp.maximum(jnp.max(scores, axis=1, keepdims=True), near_top)
        weights, total = weights_of(scores, top)
        keep = jnp.exp2(near_top - top)
        total = total + keep * stats[:, 2 * part + 1 : 2 * part + 2]
        mixed = fold(dot(jnp.concatenate(split(weights), axis=0), vert_v[rows, :], DOWN))
        mixed = mixed[:, :HEAD_SIZE] + mixed[:, HEAD_SIZE:] + keep * near[:, columns]
        mixed = mixed / total

        @pl.when(turn == 0)
        def _():
            out_a[:, columns] = mixed

        @pl.when(turn == 1)
        def _():
            out_b[:, columns] = mixed


def attend(q, near, stats, start, first_row, arrays):
    width = q.shape[1]
    heads = width // HEAD_SIZE
    pair = 2
    last = heads // pair - 1
    smem = pl.BlockSpec(memory_space=pltpu.SMEM)
    vmem = pl.BlockSpec(memory_space=pltpu.VMEM)
    base = start // TILE
    wide = (TILE, pair * HEAD_SIZE)
    out = jax.ShapeDtypeStruct((TILE, width), jnp.float32)
    return pl.pallas_call(
        functools.partial(attend_kernel, start),
        grid=(2, heads // pair),
        out_shape=[out, out],
        in_specs=[
            smem,
            pl.BlockSpec(wide, lambda t, h: (base + t, h)),
            pl.BlockSpec(wide, lambda t, h: (base + t, h)),
            pl.BlockSpec((TILE, HEAD_SIZE), lambda t, h: (base + t, h)),
        ]
        + [vmem] * len(arrays),
        out_specs=[
            pl.BlockSpec(wide, lambda t, h: (0, jnp.where(t == 0, h, last))),
            pl.BlockSpec(wide, lambda t, h: (0, jnp.where(t == 0, 0, h))),
        ],
        scratch_shapes=[pltpu.VMEM((heads * 8 * BLOCK, 2 * HEAD_SIZE), jnp.bfloat16)] * 2,
        compiler_params=pltpu.CompilerParams(vmem_limit_bytes=40 << 20),
        cost_estimate=LARGE,
    )(first_row, q, near, stats, *arrays)


def stack_split(x, at, ref):
    rows, depth = ref.shape
    high, low = split(ref[...])
    x[:rows, at : at + depth] = high
    x[rows:, at : at + depth] = low


def times_weight(x, w, refs):
    depth = refs[0].shape[0]
    for at, ref in enumerate(refs):
        rows = slice(at * depth, (at + 1) * depth)
        w[0, rows, :], w[1, rows, :] = split(ref[...])
    return fold(dot(x[...], w[0], DOWN)) + dot(x[: x.shape[0] // 2, :], w[1], DOWN)


def chip_kernel(order, *refs):
    own, mate = refs[0:2], refs[2:4]
    w_own, w_mate, out, x, w = refs[4:]
    for kind in range(2):

        @pl.when((pl.program_id(0) == kind) & (pl.program_id(1) == 0))
        def _():
            stack_split(x, 0, own[kind])
            stack_split(x, own[kind].shape[1], mate[kind])

    out[0] = times_weight(x, w, (w_own, w_mate))


def project_chip(own, mate, w_own, w_mate, order):
    rows, depth = own[0].shape
    width = depth
    vmem = pl.BlockSpec(memory_space=pltpu.VMEM)
    return pl.pallas_call(
        chip_kernel,
        out_shape=jax.ShapeDtypeStruct((2, rows, 2 * width), jnp.float32),
        grid_spec=pltpu.PrefetchScalarGridSpec(
            num_scalar_prefetch=1,
            grid=(2, 2),
            in_specs=[vmem] * 4
            + [
                pl.BlockSpec((depth, width), lambda k, d, o: (0, o[2 * k + d])),
                pl.BlockSpec((depth, width), lambda k, d, o: (0, d * (k + 1))),
            ],
            out_specs=pl.BlockSpec((1, rows, width), lambda k, d, o: (k, 0, d)),
            scratch_shapes=[
                pltpu.VMEM((2 * rows, 2 * depth), jnp.bfloat16),
                pltpu.VMEM((2, 2 * depth, width), jnp.bfloat16),
            ],
        ),
        compiler_params=pltpu.CompilerParams(vmem_limit_bytes=48 << 20),
        cost_estimate=LARGE,
    )(order, *own, *mate, w_own, w_mate)


def pair_kernel(core, *refs):
    got, mate = refs[0:2], refs[2:4]
    weights = (refs[4:6], refs[6:8])
    total, outs, x, w = refs[8], refs[9:13], refs[13], refs[14]
    for kind in range(2):

        @pl.when((pl.program_id(0) == kind) & (pl.program_id(1) == 0))
        def _():
            stack_split(x, 0, got[kind])
            stack_split(x, got[kind].shape[1], mate[kind])

        for chip in range(2):

            @pl.when((pl.program_id(0) == kind) & (pl.program_id(1) == chip))
            def _():
                outs[2 * kind + chip][...] = total[0] + times_weight(x, w, weights[kind])


def project_pair(got, mate, near, near_mate, far, far_mate, total, core):
    rows, depth = got[0].shape
    width = depth
    vmem = pl.BlockSpec(memory_space=pltpu.VMEM)
    out = jax.ShapeDtypeStruct((rows, width), jnp.float32)
    even = lambda k, d: jnp.where(k == 0, d, 1)
    odd = lambda k, d: jnp.where(k == 0, 0, d)
    w_spec = lambda place: pl.BlockSpec((depth, width), place)
    return pl.pallas_call(
        pair_kernel,
        out_shape=[out] * 4,
        grid_spec=pltpu.PrefetchScalarGridSpec(
            num_scalar_prefetch=1,
            grid=(2, 2),
            in_specs=[vmem] * 4
            + [
                w_spec(lambda k, d, c: (0, 2 * even(k, d) + c[0])),
                w_spec(lambda k, d, c: (0, even(k, d))),
                w_spec(lambda k, d, c: (0, 2 * odd(k, d) + c[0])),
                w_spec(lambda k, d, c: (0, odd(k, d))),
                pl.BlockSpec((1, rows, width), lambda k, d, c: (k, 0, d)),
            ],
            out_specs=[pl.BlockSpec((rows, width), lambda k, d, c: (0, 0))] * 4,
            scratch_shapes=[
                pltpu.VMEM((2 * rows, 2 * depth), jnp.bfloat16),
                pltpu.VMEM((2, 2 * depth, width), jnp.bfloat16),
            ],
        ),
        compiler_params=pltpu.CompilerParams(vmem_limit_bytes=48 << 20),
        cost_estimate=LARGE,
    )(core, *got, *mate, near, near_mate, far, far_mate, total)


def body(
    queries, key_rows, value_vectors, vertical_blocks, slash_offsets, prompt_length, out_weight
):
    rows = queries.shape[0]
    blocks = rows // BLOCK
    heads = queries.shape[1] // HEAD_SIZE
    seq_index = lax.axis_index("seq")
    head_index = lax.axis_index("head")
    head_size = lax.axis_size("head")
    core = head_index % 2
    chips = head_size // 2

    x, z = seq_index % 4, seq_index // 4
    ids = range(lax.axis_size("seq"))
    right = [(i, i // 4 * 4 + (i + 1) % 4) for i in ids]
    left = [(i, i // 4 * 4 + (i + 3) % 4) for i in ids]
    over = [(i, i // 4 * 4 + (i + 2) % 4) for i in ids]
    up = [(i, (i + 4) % 16) for i in ids]
    down = [(i, (i + 12) % 16) for i in ids]
    send = lambda a, pairs: lax.ppermute(a, "seq", pairs)
    swapped = lambda a, bits: send(a, [(i, i ^ bits) for i in ids])

    k_left = send(key_rows, right)
    k_right = send(key_rows, left)
    v_below = send(value_vectors, up)
    v_above = send(value_vectors, down)

    y = head_index // 2
    over_head = lambda a, bits: lax.ppermute(a, "head", [(i, i ^ bits) for i in range(head_size)])
    width = out_weight.shape[1] // head_size
    cut = lambda a, first, count: lax.dynamic_slice_in_dim(a, first * width, count * width, 1)
    beside = lambda *parts: jnp.concatenate(parts, axis=1)
    chip_columns = lambda chip: cut(out_weight, 2 * chip, 2)
    near_weight, far_weight = (
        over_head(beside(chip_columns(y ^ chip), chip_columns(y ^ 2)), 2 * chip) for chip in (1, 3)
    )
    mate_columns = (cut(out_weight, 2 * chip + 1 - core, 1) for chip in (y, y ^ 3, y ^ 1))
    mate_weight = over_head(beside(*mate_columns), 1)

    vert = lax.dynamic_slice_in_dim(vertical_blocks, head_index * heads, heads, 0)
    slash = lax.dynamic_slice_in_dim(slash_offsets, head_index * heads, heads, 0)
    prompt = prompt_length[0]
    named = vert.reshape(-1)
    inside = jnp.arange(BLOCK, dtype=jnp.int32)
    vert_pos = vert[:, :, None] * BLOCK + inside
    vert_pos = jnp.where(vert_pos < prompt, -1, vert_pos).reshape(heads, 1, -1)
    offsets = jnp.concatenate([jnp.zeros((heads, 1), jnp.int32), slash + 1], axis=1)
    block_ids = seq_index * blocks + jnp.arange(blocks, dtype=jnp.int32)
    slash_block = block_ids[None, :, None] - offsets[:, None, :]
    repeated = jnp.any(slash_block[:, :, :, None] == vert[:, None, None, :], axis=-1)
    usable = (slash_block >= 0) & jnp.logical_not(repeated)
    slash_pos = slash_block[..., None] * BLOCK + inside
    slash_pos = jnp.where(slash_pos < prompt, -1, slash_pos)
    slash_pos = jnp.where(usable[..., None], slash_pos, FAR).reshape(heads, blocks, 1, -1)
    first_row = (seq_index * rows).reshape(1)
    back = 2 * blocks - offsets
    wraps = jnp.stack([x < 2, x == 0]).astype(jnp.int32)
    order = jnp.stack([2 * chip + core for chip in (y, y ^ 3, y, y ^ 1)])
    my_core = core.reshape(1)
    owner = named // blocks
    at = named % blocks
    k_place, k_held = (owner % 4 - x) % 4 * blocks + at, (owner // 4 == z).astype(jnp.int32)
    v_place, v_held = (owner // 4 - z) % 4 * blocks + at, (owner % 4 == x).astype(jnp.int32)
    orders = (order, my_core)
    small = (vert_pos, slash_pos, first_row, back, wraps, orders, k_place, k_held, v_place, v_held)

    (k_left, k_right, v_below, v_above), small = lax.optimization_barrier(
        ((k_left, k_right, v_below, v_above), small)
    )
    vert_pos, slash_pos, first_row, back, wraps, orders, k_place, k_held, v_place, v_held = small
    half = rows // 2
    source = jnp.where(x >= 2, v_below, value_vectors)
    v_left = jnp.where(x == 3, v_below, value_vectors)
    moved_left = send(jnp.concatenate([k_right, source[half:]]), left)
    v_beyond = send(v_above, down)
    moved_right = send(jnp.concatenate([v_left, source[:half]]), right)
    k_left_wrap = send(k_left, [(i, i + 4) for i in ids if i % 4 == 0 and i + 4 in ids])
    moved_left, v_beyond, moved_right, k_left_wrap = lax.optimization_barrier(
        (moved_left, v_beyond, moved_right, k_left_wrap)
    )
    k_far, v_far_b = moved_left[:rows], moved_left[rows:]
    v_left, v_far_a = moved_right[:rows], moved_right[rows:]

    k_named = pick_blocks(k_place, k_held, (key_rows, k_right, k_far, k_left))
    v_named = pick_blocks(v_place, v_held, (value_vectors, v_above, v_beyond, v_below))
    v_far_a = send(v_far_a, right)
    v_far_b = send(v_far_b, left)
    k_far_wrap = send(k_far, [(i, i + 4) for i in ids if i % 4 < 2 and i + 4 in ids])
    named = [*k_named, *v_named]
    one, two = (4, 12, 1, 3), (12, 4, 3, 1)
    more = [swapped(a, bits) for a, bits in zip(named, one)]
    v_far_a, v_far_b, k_far_wrap, *more = lax.optimization_barrier(
        (v_far_a, v_far_b, k_far_wrap, *more)
    )
    named = [a + b for a, b in zip(named, more)]
    arrays = (k_far, k_far_wrap, k_left, k_left_wrap, key_rows, v_far_a, v_far_b, v_left)
    near_arrays = (*arrays, value_vectors, slash_pos)
    near = attend_near(queries, 0, rows, first_row, back, wraps, near_arrays)
    more = [swapped(a, bits) for a, bits in zip(named, two)]
    near, more = lax.optimization_barrier((near, more))
    arrays = (*(a + b for a, b in zip(named, more)), vert_pos)

    order, my_core = orders
    meet, end = (2, 6), (6, 2)
    across_chip = lambda parts: [over_head(a, 1) for a in parts]
    own = list(attend(queries, *near, 0, first_row, arrays))
    q, *own = lax.optimization_barrier((queries, *own))
    got_a = [over_head(a, bits) for a, bits in zip(own, meet)]
    mate, near_weight, far_weight = lax.optimization_barrier(
        (across_chip(own), near_weight, far_weight)
    )
    total = project_chip(own, mate, out_weight, mate_weight, order)
    q, total = lax.optimization_barrier((q, total))
    near_mate, far_mate = (
        over_head(beside(cut(a, 1 - core, 1), cut(a, 3 - core, 1)), 1)
        for a in (near_weight, far_weight)
    )
    own = attend(q, *near, half, first_row, arrays)
    own, got_a = lax.optimization_barrier((own, got_a))
    weights = (near_weight, near_mate, far_weight, far_mate)
    got_b = [over_head(a, bits) for a, bits in zip(own, meet)]
    mate = across_chip(own)
    keep_0, pass_0, keep_1, pass_1 = project_pair(
        got_a, across_chip(got_a), *weights, total, my_core
    )
    pass_0, pass_1, got_b, mate = lax.optimization_barrier((pass_0, pass_1, got_b, mate))
    sent_a = [over_head(a, bits) for a, bits in zip((pass_0, pass_1), end)]
    total = project_chip(own, mate, out_weight, mate_weight, order)
    keep_2, pass_2, keep_3, pass_3 = project_pair(
        got_b, across_chip(got_b), *weights, total, my_core
    )
    pass_2, pass_3, sent_a = lax.optimization_barrier((pass_2, pass_3, sent_a))
    sent = sent_a + [over_head(a, bits) for a, bits in zip((pass_2, pass_3), end)]
    return jnp.concatenate([a + b for a, b in zip((keep_0, keep_1, keep_2, keep_3), sent)], axis=0)


def solution(mesh):
    placed = (P("seq", "head"), P("seq", "head"), P("seq", "head"), P(), P(), P(), P("head", None))
    return jax.shard_map(
        body, mesh=mesh, in_specs=placed, out_specs=P("seq", "head"), check_vma=False
    )
```

```python
import functools
import math

import jax
import jax.numpy as jnp
from jax import lax
from jax.experimental import pallas as pl
from jax.experimental.pallas import tpu as pltpu
from jax.sharding import PartitionSpec as P

HEAD_SIZE = 128
BLOCK = 64
TILE = 256
FAR = 1 << 30
LOW = -1e30
LARGE = pl.CostEstimate(flops=1 << 30, bytes_accessed=1 << 20, transcendentals=0)
SMALL = pl.CostEstimate(flops=1024, bytes_accessed=1024, transcendentals=0)


def pick_kernel(place, held, *refs):
    *pieces, first, second, rows = refs
    size = pieces[0].shape[0]
    for at, piece in enumerate(pieces):
        rows[at * size : (at + 1) * size, :] = piece[...]
    slots = first.shape[0] // BLOCK
    for slot in range(2 * slots):
        out = first if slot < slots else second
        target = pl.ds(slot % slots * BLOCK, BLOCK)

        @pl.when(held[slot] == 1)
        def _():
            start = pl.multiple_of(place[slot] * BLOCK, BLOCK)
            out[target, :] = rows[pl.ds(start, BLOCK), :]

        @pl.when(held[slot] == 0)
        def _():
            out[target, :] = jnp.zeros((BLOCK, HEAD_SIZE), jnp.float32)


def pick_blocks(place, held, pieces):
    half = place.shape[0] // 2 * BLOCK
    smem = pl.BlockSpec(memory_space=pltpu.SMEM)
    vmem = pl.BlockSpec(memory_space=pltpu.VMEM)
    out = jax.ShapeDtypeStruct((half, HEAD_SIZE), jnp.float32)
    size = pieces[0].shape[0]
    return pl.pallas_call(
        pick_kernel,
        out_shape=[out, out],
        in_specs=[smem, smem] + [vmem] * len(pieces),
        out_specs=[vmem] * 2,
        scratch_shapes=[pltpu.VMEM((len(pieces) * size, HEAD_SIZE), jnp.float32)],
        compiler_params=pltpu.CompilerParams(vmem_limit_bytes=16 << 20),
        cost_estimate=SMALL,
    )(place, held, *pieces)


def split(x):
    high = x.astype(jnp.bfloat16)
    return high, (x - high.astype(jnp.float32)).astype(jnp.bfloat16)


def fold(x):
    half = x.shape[0] // 2
    return x[:half] + x[half:]


def put_parts(target, first, pieces):
    for piece in pieces:
        count = piece.shape[0]
        high, low = split(piece[...])
        target[first : first + count, 0:HEAD_SIZE] = high
        target[first : first + count, HEAD_SIZE:] = low
        first += count


dot = functools.partial(lax.dot_general, preferred_element_type=jnp.float32)
ACROSS = (((1,), (1,)), ((), ()))
DOWN = (((1,), (0,)), ((), ()))
SCALE = math.log2(math.e) / math.sqrt(HEAD_SIZE)


def query_parts(q):
    return (jnp.concatenate([x, x], axis=1) for x in split(q))


def scale_kernel(q, out):
    out[...] = q[...] * SCALE


def scaled(q):
    rows, width = q.shape
    spec = pl.BlockSpec((TILE, width), lambda i: (i, 0))
    return pl.pallas_call(
        scale_kernel,
        grid=(rows // TILE,),
        out_shape=jax.ShapeDtypeStruct(q.shape, jnp.float32),
        in_specs=[spec],
        out_specs=spec,
        compiler_params=pltpu.CompilerParams(vmem_limit_bytes=8 << 20),
        cost_estimate=LARGE,
    )(q)


def weights_of(scores, top):
    weights = jnp.exp2(scores - top)
    return weights, jnp.sum(weights, axis=1, keepdims=True)


def near_kernel(
    start, first_row, back, wraps, q, k_far, k_far_wrap, k_left, k_left_wrap, k_own,
    v_far_a, v_far_b, v_left, v_own, slash_pos, out, stats, near_k, near_v,
):
    turn = pl.program_id(0)

    @pl.when((turn == 0) & (pl.program_id(1) == 0))
    def _():
        rows = k_own.shape[0]
        for at, (plain, wrapped) in enumerate(((k_far, k_far_wrap), (k_left, k_left_wrap))):

            @pl.when(wraps[at] == 0)
            def _():
                put_parts(near_k, at * rows, (plain,))

            @pl.when(wraps[at] == 1)
            def _():
                put_parts(near_k, at * rows, (wrapped,))

        put_parts(near_k, 2 * rows, (k_own,))
        put_parts(near_v, 0, (v_far_a, v_far_b, v_left, v_own))

    q_pos = first_row[0] + start + turn * TILE + lax.broadcasted_iota(jnp.int32, (TILE, 1), 0)
    per_block = TILE // BLOCK
    pair = q.shape[1] // HEAD_SIZE
    lane = lax.broadcasted_iota(jnp.int32, (TILE, HEAD_SIZE), 1)
    known = jnp.zeros((TILE, HEAD_SIZE), jnp.float32)
    for part in range(pair):
        head = pl.program_id(1) * pair + part
        columns = slice(part * HEAD_SIZE, (part + 1) * HEAD_SIZE)
        high, low = query_parts(q[:, columns])
        scores, near = [], []
        for j in range(per_block):
            block = start // BLOCK + turn * per_block + j
            spots = [
                pl.ds(pl.multiple_of((block + back[head, n]) * BLOCK, BLOCK), BLOCK)
                for n in range(4)
            ]
            near.append(spots)
            keys = jnp.concatenate([near_k[s, :] for s in spots], axis=0)
            mine = slice(j * BLOCK, (j + 1) * BLOCK)
            score = fold(dot(jnp.concatenate([high[mine], low[mine]], axis=0), keys, ACROSS))
            scores.append(jnp.where(slash_pos[head, block] <= q_pos[mine], score, LOW))
        scores = jnp.concatenate(scores, axis=0)
        top = jnp.max(scores, axis=1, keepdims=True)
        weights, total = weights_of(scores, top)
        w_high, w_low = split(weights)
        parts = []
        for j in range(per_block):
            values = jnp.concatenate([near_v[s, :] for s in near[j]], axis=0)
            mine = slice(j * BLOCK, (j + 1) * BLOCK)
            stacked = jnp.concatenate([w_high[mine], w_low[mine]], axis=0)
            parts.append(fold(dot(stacked, values, DOWN)))
        mixed = jnp.concatenate(parts, axis=0)
        out[:, columns] = mixed[:, :HEAD_SIZE] + mixed[:, HEAD_SIZE:]
        known = jnp.where(lane == 2 * part, top, known)
        known = jnp.where(lane == 2 * part + 1, total, known)
    stats[...] = known


def attend_near(q, start, rows, first_row, back, wraps, arrays):
    width = q.shape[1]
    pair = 2
    count = width // (pair * HEAD_SIZE)
    base = start // TILE
    smem = pl.BlockSpec(memory_space=pltpu.SMEM)
    vmem = pl.BlockSpec(memory_space=pltpu.VMEM)
    wide = (TILE, pair * HEAD_SIZE)
    return pl.pallas_call(
        functools.partial(near_kernel, start),
        grid=(rows // TILE, count),
        out_shape=[
            jax.ShapeDtypeStruct((rows, width), jnp.float32),
            jax.ShapeDtypeStruct((rows, count * HEAD_SIZE), jnp.float32),
        ],
        in_specs=[smem, smem, smem, pl.BlockSpec(wide, lambda t, h: (base + t, h))]
        + [vmem] * len(arrays),
        out_specs=[
            pl.BlockSpec(wide, lambda t, h: (t, h)),
            pl.BlockSpec((TILE, HEAD_SIZE), lambda t, h: (t, h)),
        ],
        scratch_shapes=[pltpu.VMEM((3 * q.shape[0], 2 * HEAD_SIZE), jnp.bfloat16)] * 2,
        compiler_params=pltpu.CompilerParams(vmem_limit_bytes=24 << 20),
        cost_estimate=LARGE,
    )(first_row, back, wraps, q, *arrays)


def attend_kernel(
    start, first_row, q, near, stats, k_a, k_b, v_a, v_b, vert_pos, out, vert_k, vert_v
):
    turn = pl.program_id(0)

    @pl.when((turn == 0) & (pl.program_id(1) == 0))
    def _():
        put_parts(vert_k, 0, (k_a, k_b))
        put_parts(vert_v, 0, (v_a, v_b))

    q_pos = first_row[0] + start + turn * TILE + lax.broadcasted_iota(jnp.int32, (TILE, 1), 0)
    vert = vert_pos.shape[2]
    pair = q.shape[1] // HEAD_SIZE
    for part in range(pair):
        head = pl.program_id(1) * pair + part
        columns = slice(part * HEAD_SIZE, (part + 1) * HEAD_SIZE)
        rows = pl.ds(pl.multiple_of(head * vert, vert), vert)
        both = jnp.concatenate(list(query_parts(q[:, columns])), axis=0)
        scores = fold(dot(both, vert_k[rows, :], ACROSS))
        scores = jnp.where(vert_pos[head] <= q_pos, scores, LOW)
        near_top = stats[:, 2 * part : 2 * part + 1]
        top = jnp.maximum(jnp.max(scores, axis=1, keepdims=True), near_top)
        weights, total = weights_of(scores, top)
        keep = jnp.exp2(near_top - top)
        total = total + keep * stats[:, 2 * part + 1 : 2 * part + 2]
        mixed = fold(dot(jnp.concatenate(split(weights), axis=0), vert_v[rows, :], DOWN))
        mixed = mixed[:, :HEAD_SIZE] + mixed[:, HEAD_SIZE:] + keep * near[:, columns]
        out[0, :, columns] = mixed / total


def attend(q, near, stats, start, first_row, arrays):
    width = q.shape[1]
    heads = width // HEAD_SIZE
    pair = 2
    smem = pl.BlockSpec(memory_space=pltpu.SMEM)
    vmem = pl.BlockSpec(memory_space=pltpu.VMEM)
    base = start // TILE
    wide = (TILE, pair * HEAD_SIZE)
    return pl.pallas_call(
        functools.partial(attend_kernel, start),
        grid=(2, heads // pair),
        out_shape=jax.ShapeDtypeStruct((2, TILE, width), jnp.float32),
        in_specs=[
            smem,
            pl.BlockSpec(wide, lambda t, h: (base + t, h)),
            pl.BlockSpec(wide, lambda t, h: (base + t, h)),
            pl.BlockSpec((TILE, HEAD_SIZE), lambda t, h: (base + t, h)),
        ]
        + [vmem] * len(arrays),
        out_specs=pl.BlockSpec((1, TILE, pair * HEAD_SIZE), lambda t, h: (t, 0, h)),
        scratch_shapes=[pltpu.VMEM((heads * 8 * BLOCK, 2 * HEAD_SIZE), jnp.bfloat16)] * 2,
        compiler_params=pltpu.CompilerParams(vmem_limit_bytes=20 << 20),
        cost_estimate=LARGE,
    )(first_row, q, near, stats, *arrays)


def weight_term(x, block):
    high, low = split(block)
    return fold(dot(x, high, DOWN)) + dot(x[: x.shape[0] // 2], low, DOWN)


def stack(rows):
    return jnp.concatenate(split(rows), axis=0)


def chip_kernel(order, own_a, own_b, w, out, x):
    for kind in range(2):

        @pl.when((pl.program_id(0) == kind) & (pl.program_id(1) == 0))
        def _():
            x[...] = stack(jnp.concatenate([own_a[kind], own_b[kind]], axis=0))

    out[0] = weight_term(x[...], w[...])


def project_chip(own_a, own_b, weight, order):
    _, rows, depth = own_a.shape
    width = depth
    vmem = pl.BlockSpec(memory_space=pltpu.VMEM)
    return pl.pallas_call(
        chip_kernel,
        out_shape=jax.ShapeDtypeStruct((2, 2 * rows, 4 * width), jnp.float32),
        grid_spec=pltpu.PrefetchScalarGridSpec(
            num_scalar_prefetch=1,
            grid=(2, 4),
            in_specs=[vmem, vmem, pl.BlockSpec((depth, width), lambda k, j, o: (0, o[4 * k + j]))],
            out_specs=pl.BlockSpec((1, 2 * rows, width), lambda k, j, o: (k, 0, j)),
            scratch_shapes=[pltpu.VMEM((4 * rows, depth), jnp.bfloat16)],
        ),
        compiler_params=pltpu.CompilerParams(vmem_limit_bytes=20 << 20),
        cost_estimate=LARGE,
    )(order, own_a, own_b, weight)


def pair_kernel(cores, got_a, got_b, near, far, total, there, here, x):
    for kind, (got, weight) in enumerate(((got_a, near), (got_b, far))):

        @pl.when((pl.program_id(0) == kind) & (pl.program_id(1) == 0))
        def _():
            x[...] = stack(got[...])

        for side, out in enumerate((there, here)):

            @pl.when((pl.program_id(0) == kind) & (pl.program_id(1) == side))
            def _():
                out[0] = total[0] + weight_term(x[...], weight[...])


def project_pair(got, near, far, total, unit, keep, cores):
    rows, depth = got[0].shape
    width = depth
    base = 0 if keep else 2
    vmem = pl.BlockSpec(memory_space=pltpu.VMEM)
    out = jax.ShapeDtypeStruct((2, rows, width), jnp.float32)
    out_spec = pl.BlockSpec((1, rows, width), lambda k, s, c: (k, 0, 0))
    w_spec = lambda side: pl.BlockSpec(
        (depth, width), lambda k, s, c: (0, base + c[side(k, s)])
    )
    return pl.pallas_call(
        pair_kernel,
        out_shape=[out, out],
        grid_spec=pltpu.PrefetchScalarGridSpec(
            num_scalar_prefetch=1,
            grid=(2, 2),
            in_specs=[
                vmem,
                vmem,
                w_spec(lambda k, s: jnp.where(k == 0, s, 1)),
                w_spec(lambda k, s: jnp.where(k == 0, 0, s)),
                pl.BlockSpec((1, rows, width), lambda k, s, c: (k, unit, 2 - base + s)),
            ],
            out_specs=[out_spec, out_spec],
            scratch_shapes=[pltpu.VMEM((2 * rows, depth), jnp.bfloat16)],
        ),
        compiler_params=pltpu.CompilerParams(vmem_limit_bytes=16 << 20),
        cost_estimate=LARGE,
    )(cores, *got, near, far, total)


def body(
    queries, key_rows, value_vectors, vertical_blocks, slash_offsets, prompt_length, out_weight
):
    rows = queries.shape[0]
    blocks = rows // BLOCK
    heads = queries.shape[1] // HEAD_SIZE
    seq_index = lax.axis_index("seq")
    head_index = lax.axis_index("head")
    head_size = lax.axis_size("head")
    core = head_index % 2
    chips = head_size // 2

    x, z = seq_index % 4, seq_index // 4
    ids = range(lax.axis_size("seq"))
    right = [(i, i // 4 * 4 + (i + 1) % 4) for i in ids]
    left = [(i, i // 4 * 4 + (i + 3) % 4) for i in ids]
    over = [(i, i // 4 * 4 + (i + 2) % 4) for i in ids]
    up = [(i, (i + 4) % 16) for i in ids]
    down = [(i, (i + 12) % 16) for i in ids]
    send = lambda a, pairs: lax.ppermute(a, "seq", pairs)
    swapped = lambda a, bits: send(a, [(i, i ^ bits) for i in ids])

    k_left = send(key_rows, right)
    k_right = send(key_rows, left)
    v_below = send(value_vectors, up)
    v_above = send(value_vectors, down)

    y = head_index // 2
    over_head = lambda a, bits: lax.ppermute(a, "head", [(i, i ^ bits) for i in range(head_size)])
    width = out_weight.shape[1] // head_size
    cut = lambda a, first, count: lax.dynamic_slice_in_dim(a, first * width, count * width, 1)
    beside = lambda *parts: jnp.concatenate(parts, axis=1)
    chip_columns = lambda chip: cut(out_weight, 2 * chip, 2)
    near_weight, far_weight = (
        over_head(beside(chip_columns(y ^ chip), chip_columns(y ^ 2)), 2 * chip) for chip in (1, 3)
    )

    vert = lax.dynamic_slice_in_dim(vertical_blocks, head_index * heads, heads, 0)
    slash = lax.dynamic_slice_in_dim(slash_offsets, head_index * heads, heads, 0)
    prompt = prompt_length[0]
    named = vert.reshape(-1)
    inside = jnp.arange(BLOCK, dtype=jnp.int32)
    vert_pos = vert[:, :, None] * BLOCK + inside
    vert_pos = jnp.where(vert_pos < prompt, -1, vert_pos).reshape(heads, 1, -1)
    offsets = jnp.concatenate([jnp.zeros((heads, 1), jnp.int32), slash + 1], axis=1)
    block_ids = seq_index * blocks + jnp.arange(blocks, dtype=jnp.int32)
    slash_block = block_ids[None, :, None] - offsets[:, None, :]
    repeated = jnp.any(slash_block[:, :, :, None] == vert[:, None, None, :], axis=-1)
    usable = (slash_block >= 0) & jnp.logical_not(repeated)
    slash_pos = slash_block[..., None] * BLOCK + inside
    slash_pos = jnp.where(slash_pos < prompt, -1, slash_pos)
    slash_pos = jnp.where(usable[..., None], slash_pos, FAR).reshape(heads, blocks, 1, -1)
    first_row = (seq_index * rows).reshape(1)
    back = 2 * blocks - offsets
    wraps = jnp.stack([x < 2, x == 0]).astype(jnp.int32)
    cores = jnp.stack([1 - core, core])
    order = jnp.concatenate([2 * chip + cores for chip in (y ^ 3, y, y ^ 1, y)])
    owner = named // blocks
    at = named % blocks
    k_place, k_held = (owner % 4 - x) % 4 * blocks + at, (owner // 4 == z).astype(jnp.int32)
    v_place, v_held = (owner // 4 - z) % 4 * blocks + at, (owner % 4 == x).astype(jnp.int32)
    orders = (order, cores)
    small = (vert_pos, slash_pos, first_row, back, wraps, orders, k_place, k_held, v_place, v_held)

    (k_left, k_right, v_below, v_above), small = lax.optimization_barrier(
        ((k_left, k_right, v_below, v_above), small)
    )
    vert_pos, slash_pos, first_row, back, wraps, orders, k_place, k_held, v_place, v_held = small
    half = rows // 2
    source = jnp.where(x >= 2, v_below, value_vectors)
    v_left = jnp.where(x == 3, v_below, value_vectors)
    moved_left = send(jnp.concatenate([k_right, source[half:]]), left)
    v_beyond = send(v_above, down)
    moved_right = send(jnp.concatenate([v_left, source[:half]]), right)
    k_left_wrap = send(k_left, [(i, i + 4) for i in ids if i % 4 == 0 and i + 4 in ids])
    moved_left, v_beyond, moved_right, k_left_wrap = lax.optimization_barrier(
        (moved_left, v_beyond, moved_right, k_left_wrap)
    )
    k_far, v_far_b = moved_left[:rows], moved_left[rows:]
    v_left, v_far_a = moved_right[:rows], moved_right[rows:]

    k_named = pick_blocks(k_place, k_held, (key_rows, k_right, k_far, k_left))
    v_named = pick_blocks(v_place, v_held, (value_vectors, v_above, v_beyond, v_below))
    v_far_a = send(v_far_a, right)
    v_far_b = send(v_far_b, left)
    k_far_wrap = send(k_far, [(i, i + 4) for i in ids if i % 4 < 2 and i + 4 in ids])
    named = [*k_named, *v_named]
    one, two = (4, 12, 1, 3), (12, 4, 3, 1)
    more = [swapped(a, bits) for a, bits in zip(named, one)]
    q = scaled(queries)
    q, v_far_a, v_far_b, k_far_wrap, *more = lax.optimization_barrier(
        (q, v_far_a, v_far_b, k_far_wrap, *more)
    )
    named = [a + b for a, b in zip(named, more)]
    arrays = (k_far, k_far_wrap, k_left, k_left_wrap, key_rows, v_far_a, v_far_b, v_left)
    near_arrays = (*arrays, value_vectors, slash_pos)
    near = attend_near(q, 0, rows, first_row, back, wraps, near_arrays)
    more = [swapped(a, bits) for a, bits in zip(named, two)]
    near, more = lax.optimization_barrier((near, more))
    arrays = (*(a + b for a, b in zip(named, more)), vert_pos)

    order, cores = orders
    meet, end = (2, 6), (6, 2)
    own_a = attend(q, *near, 0, first_row, arrays)
    q, own_a = lax.optimization_barrier((q, own_a))
    meeting = lambda parts: [over_head(parts[i], bits) for i, bits in enumerate(meet)]
    ending = lambda parts: [over_head(parts[i], bits) for i, bits in enumerate(end)]
    got_a = meeting(own_a)
    own_b = attend(q, *near, half, first_row, arrays)
    total = project_chip(own_a, own_b, out_weight, order)
    total, near_weight, far_weight, got_a = lax.optimization_barrier(
        (total, near_weight, far_weight, got_a)
    )
    got_b = meeting(own_b)
    product = lambda got, unit, keep: project_pair(
        got, near_weight, far_weight, total, unit, keep, cores
    )
    there_a, here_a = product(got_a, 0, False)
    there_a, here_a, got_a = lax.optimization_barrier((there_a, here_a, got_a))
    pass_a = here_a + over_head(there_a, 1)
    keep_there_a, keep_here_a = product(got_a, 0, True)
    pass_a, got_b, keep_there_a = lax.optimization_barrier((pass_a, got_b, keep_there_a))
    sent_a = ending(pass_a)
    there_b, here_b = product(got_b, 1, False)
    there_b, here_b, got_b = lax.optimization_barrier((there_b, here_b, got_b))
    pass_b = here_b + over_head(there_b, 1)
    keep_there_b, keep_here_b = product(got_b, 1, True)
    kept_a = keep_here_a + over_head(keep_there_a, 1)
    pass_b, sent_a, keep_there_b = lax.optimization_barrier((pass_b, sent_a, keep_there_b))
    sent_b = ending(pass_b)
    kept_b = keep_here_b + over_head(keep_there_b, 1)
    kept = (kept_a[0], kept_a[1], kept_b[0], kept_b[1])
    return jnp.concatenate([a + b for a, b in zip(kept, (*sent_a, *sent_b))], axis=0)


def solution(mesh):
    placed = (P("seq", "head"), P("seq", "head"), P("seq", "head"), P(), P(), P(), P("head", None))
    return jax.shard_map(
        body, mesh=mesh, in_specs=placed, out_specs=P("seq", "head"), check_vma=False
    )
```

```python
import functools
import math

import jax
import jax.numpy as jnp
from jax import lax
from jax.experimental import pallas as pl
from jax.experimental.pallas import tpu as pltpu
from jax.sharding import PartitionSpec as P

HEAD_SIZE = 128
BLOCK = 64
TILE = 256
FAR = 1 << 30
LOW = -1e30
LARGE = pl.CostEstimate(flops=1 << 30, bytes_accessed=1 << 20, transcendentals=0)
SMALL = pl.CostEstimate(flops=1024, bytes_accessed=1024, transcendentals=0)


def pick_kernel(place, held, *refs):
    *pieces, first, second, rows = refs
    size = pieces[0].shape[0]
    for at, piece in enumerate(pieces):
        rows[at * size : (at + 1) * size, :] = piece[...]
    slots = first.shape[0] // BLOCK
    for slot in range(2 * slots):
        out = first if slot < slots else second
        target = pl.ds(slot % slots * BLOCK, BLOCK)

        @pl.when(held[slot] == 1)
        def _():
            start = pl.multiple_of(place[slot] * BLOCK, BLOCK)
            out[target, :] = rows[pl.ds(start, BLOCK), :]

        @pl.when(held[slot] == 0)
        def _():
            out[target, :] = jnp.zeros((BLOCK, HEAD_SIZE), jnp.float32)


def pick_blocks(place, held, pieces):
    half = place.shape[0] // 2 * BLOCK
    smem = pl.BlockSpec(memory_space=pltpu.SMEM)
    vmem = pl.BlockSpec(memory_space=pltpu.VMEM)
    out = jax.ShapeDtypeStruct((half, HEAD_SIZE), jnp.float32)
    size = pieces[0].shape[0]
    return pl.pallas_call(
        pick_kernel,
        out_shape=[out, out],
        in_specs=[smem, smem] + [vmem] * len(pieces),
        out_specs=[vmem] * 2,
        scratch_shapes=[pltpu.VMEM((len(pieces) * size, HEAD_SIZE), jnp.float32)],
        compiler_params=pltpu.CompilerParams(vmem_limit_bytes=16 << 20),
        cost_estimate=SMALL,
    )(place, held, *pieces)


def split(x):
    high = x.astype(jnp.bfloat16)
    return high, (x - high.astype(jnp.float32)).astype(jnp.bfloat16)


def fold(x):
    half = x.shape[0] // 2
    return x[:half] + x[half:]


def put_parts(target, first, pieces):
    for piece in pieces:
        count = piece.shape[0]
        high, low = split(piece[...])
        target[first : first + count, 0:HEAD_SIZE] = high
        target[first : first + count, HEAD_SIZE:] = low
        first += count


dot = functools.partial(lax.dot_general, preferred_element_type=jnp.float32)
ACROSS = (((1,), (1,)), ((), ()))
DOWN = (((1,), (0,)), ((), ()))
SCALE = math.log2(math.e) / math.sqrt(HEAD_SIZE)


def query_parts(q):
    return (jnp.concatenate([x, x], axis=1) for x in split(q))


def scale_kernel(q, out):
    out[...] = q[...] * SCALE


def scaled(q):
    rows, width = q.shape
    spec = pl.BlockSpec((TILE, width), lambda i: (i, 0))
    return pl.pallas_call(
        scale_kernel,
        grid=(rows // TILE,),
        out_shape=jax.ShapeDtypeStruct(q.shape, jnp.float32),
        in_specs=[spec],
        out_specs=spec,
        compiler_params=pltpu.CompilerParams(vmem_limit_bytes=8 << 20),
        cost_estimate=LARGE,
    )(q)


def weights_of(scores, top):
    weights = jnp.exp2(scores - top)
    return weights, jnp.sum(weights, axis=1, keepdims=True)


def near_kernel(
    start, first_row, back, wraps, q, k_far, k_far_wrap, k_left, k_left_wrap, k_own,
    v_far_a, v_far_b, v_left, v_own, slash_pos, out, stats, near_k, near_v,
):
    turn = pl.program_id(0)

    @pl.when((turn == 0) & (pl.program_id(1) == 0))
    def _():
        rows = k_own.shape[0]
        for at, (plain, wrapped) in enumerate(((k_far, k_far_wrap), (k_left, k_left_wrap))):

            @pl.when(wraps[at] == 0)
            def _():
                put_parts(near_k, at * rows, (plain,))

            @pl.when(wraps[at] == 1)
            def _():
                put_parts(near_k, at * rows, (wrapped,))

        put_parts(near_k, 2 * rows, (k_own,))
        put_parts(near_v, 0, (v_far_a, v_far_b, v_left, v_own))

    q_pos = first_row[0] + start + turn * TILE + lax.broadcasted_iota(jnp.int32, (TILE, 1), 0)
    per_block = TILE // BLOCK
    pair = q.shape[1] // HEAD_SIZE
    lane = lax.broadcasted_iota(jnp.int32, (TILE, HEAD_SIZE), 1)
    known = jnp.zeros((TILE, HEAD_SIZE), jnp.float32)
    for part in range(pair):
        head = pl.program_id(1) * pair + part
        columns = slice(part * HEAD_SIZE, (part + 1) * HEAD_SIZE)
        high, low = query_parts(q[:, columns])
        scores, near = [], []
        for j in range(per_block):
            block = start // BLOCK + turn * per_block + j
            spots = [
                pl.ds(pl.multiple_of((block + back[head, n]) * BLOCK, BLOCK), BLOCK)
                for n in range(4)
            ]
            near.append(spots)
            keys = jnp.concatenate([near_k[s, :] for s in spots], axis=0)
            mine = slice(j * BLOCK, (j + 1) * BLOCK)
            score = fold(dot(jnp.concatenate([high[mine], low[mine]], axis=0), keys, ACROSS))
            scores.append(jnp.where(slash_pos[head, block] <= q_pos[mine], score, LOW))
        scores = jnp.concatenate(scores, axis=0)
        top = jnp.max(scores, axis=1, keepdims=True)
        weights, total = weights_of(scores, top)
        w_high, w_low = split(weights)
        parts = []
        for j in range(per_block):
            values = jnp.concatenate([near_v[s, :] for s in near[j]], axis=0)
            mine = slice(j * BLOCK, (j + 1) * BLOCK)
            stacked = jnp.concatenate([w_high[mine], w_low[mine]], axis=0)
            parts.append(fold(dot(stacked, values, DOWN)))
        mixed = jnp.concatenate(parts, axis=0)
        out[:, columns] = mixed[:, :HEAD_SIZE] + mixed[:, HEAD_SIZE:]
        known = jnp.where(lane == 2 * part, top, known)
        known = jnp.where(lane == 2 * part + 1, total, known)
    stats[...] = known


def attend_near(q, start, rows, first_row, back, wraps, arrays):
    width = q.shape[1]
    pair = 2
    count = width // (pair * HEAD_SIZE)
    base = start // TILE
    smem = pl.BlockSpec(memory_space=pltpu.SMEM)
    vmem = pl.BlockSpec(memory_space=pltpu.VMEM)
    wide = (TILE, pair * HEAD_SIZE)
    return pl.pallas_call(
        functools.partial(near_kernel, start),
        grid=(rows // TILE, count),
        out_shape=[
            jax.ShapeDtypeStruct((rows, width), jnp.float32),
            jax.ShapeDtypeStruct((rows, count * HEAD_SIZE), jnp.float32),
        ],
        in_specs=[smem, smem, smem, pl.BlockSpec(wide, lambda t, h: (base + t, h))]
        + [vmem] * len(arrays),
        out_specs=[
            pl.BlockSpec(wide, lambda t, h: (t, h)),
            pl.BlockSpec((TILE, HEAD_SIZE), lambda t, h: (t, h)),
        ],
        scratch_shapes=[pltpu.VMEM((3 * q.shape[0], 2 * HEAD_SIZE), jnp.bfloat16)] * 2,
        compiler_params=pltpu.CompilerParams(vmem_limit_bytes=24 << 20),
        cost_estimate=LARGE,
    )(first_row, back, wraps, q, *arrays)


def attend_kernel(
    start, first_row, q, near, stats, k_a, k_b, v_a, v_b, vert_pos, out, vert_k, vert_v
):
    turn = pl.program_id(0)

    @pl.when((turn == 0) & (pl.program_id(1) == 0))
    def _():
        put_parts(vert_k, 0, (k_a, k_b))
        put_parts(vert_v, 0, (v_a, v_b))

    q_pos = first_row[0] + start + turn * TILE + lax.broadcasted_iota(jnp.int32, (TILE, 1), 0)
    vert = vert_pos.shape[2]
    pair = q.shape[1] // HEAD_SIZE
    for part in range(pair):
        head = pl.program_id(1) * pair + part
        columns = slice(part * HEAD_SIZE, (part + 1) * HEAD_SIZE)
        rows = pl.ds(pl.multiple_of(head * vert, vert), vert)
        both = jnp.concatenate(list(query_parts(q[:, columns])), axis=0)
        scores = fold(dot(both, vert_k[rows, :], ACROSS))
        scores = jnp.where(vert_pos[head] <= q_pos, scores, LOW)
        near_top = stats[:, 2 * part : 2 * part + 1]
        top = jnp.maximum(jnp.max(scores, axis=1, keepdims=True), near_top)
        weights, total = weights_of(scores, top)
        keep = jnp.exp2(near_top - top)
        total = total + keep * stats[:, 2 * part + 1 : 2 * part + 2]
        mixed = fold(dot(jnp.concatenate(split(weights), axis=0), vert_v[rows, :], DOWN))
        mixed = mixed[:, :HEAD_SIZE] + mixed[:, HEAD_SIZE:] + keep * near[:, columns]
        out[0, :, columns] = mixed / total


def attend(q, near, stats, start, first_row, arrays):
    width = q.shape[1]
    heads = width // HEAD_SIZE
    pair = 2
    smem = pl.BlockSpec(memory_space=pltpu.SMEM)
    vmem = pl.BlockSpec(memory_space=pltpu.VMEM)
    base = start // TILE
    wide = (TILE, pair * HEAD_SIZE)
    return pl.pallas_call(
        functools.partial(attend_kernel, start),
        grid=(2, heads // pair),
        out_shape=jax.ShapeDtypeStruct((2, TILE, width), jnp.float32),
        in_specs=[
            smem,
            pl.BlockSpec(wide, lambda t, h: (base + t, h)),
            pl.BlockSpec(wide, lambda t, h: (base + t, h)),
            pl.BlockSpec((TILE, HEAD_SIZE), lambda t, h: (base + t, h)),
        ]
        + [vmem] * len(arrays),
        out_specs=pl.BlockSpec((1, TILE, pair * HEAD_SIZE), lambda t, h: (t, 0, h)),
        scratch_shapes=[pltpu.VMEM((heads * 8 * BLOCK, 2 * HEAD_SIZE), jnp.bfloat16)] * 2,
        compiler_params=pltpu.CompilerParams(vmem_limit_bytes=20 << 20),
        cost_estimate=LARGE,
    )(first_row, q, near, stats, *arrays)


def take_kernel(order, source, out):
    out[...] = source[...]


def take_columns(weight, order, width):
    rows = weight.shape[0]
    count = order.shape[0]
    return pl.pallas_call(
        take_kernel,
        out_shape=jax.ShapeDtypeStruct((rows, count * width), jnp.float32),
        grid_spec=pltpu.PrefetchScalarGridSpec(
            num_scalar_prefetch=1,
            grid=(count,),
            in_specs=[pl.BlockSpec((rows, width), lambda i, o: (0, o[i]))],
            out_specs=pl.BlockSpec((rows, width), lambda i, o: (0, i)),
        ),
        compiler_params=pltpu.CompilerParams(vmem_limit_bytes=58 << 20),
        cost_estimate=SMALL,
    )(order, weight)


def weight_term(x, block):
    high, low = split(block)
    return fold(dot(x, high, DOWN)) + dot(x[: x.shape[0] // 2], low, DOWN)


def stack(rows):
    return jnp.concatenate(split(rows), axis=0)


def chip_kernel(order, own_a, own_b, w, out, x):
    for kind in range(2):

        @pl.when((pl.program_id(0) == kind) & (pl.program_id(1) == 0))
        def _():
            x[...] = stack(jnp.concatenate([own_a[kind], own_b[kind]], axis=0))

    out[0] = weight_term(x[...], w[...])


def project_chip(own_a, own_b, weight, order):
    _, rows, depth = own_a.shape
    width = depth
    vmem = pl.BlockSpec(memory_space=pltpu.VMEM)
    return pl.pallas_call(
        chip_kernel,
        out_shape=jax.ShapeDtypeStruct((2, 2 * rows, 4 * width), jnp.float32),
        grid_spec=pltpu.PrefetchScalarGridSpec(
            num_scalar_prefetch=1,
            grid=(2, 4),
            in_specs=[vmem, vmem, pl.BlockSpec((depth, width), lambda k, j, o: (0, o[4 * k + j]))],
            out_specs=pl.BlockSpec((1, 2 * rows, width), lambda k, j, o: (k, 0, j)),
            scratch_shapes=[pltpu.VMEM((4 * rows, depth), jnp.bfloat16)],
        ),
        compiler_params=pltpu.CompilerParams(vmem_limit_bytes=20 << 20),
        cost_estimate=LARGE,
    )(order, own_a, own_b, weight)


def pair_kernel(cores, got_a, got_b, near, far, total, there, here, x):
    for kind, (got, weight) in enumerate(((got_a, near), (got_b, far))):

        @pl.when((pl.program_id(0) == kind) & (pl.program_id(1) == 0))
        def _():
            x[...] = stack(got[...])

        for side, out in enumerate((there, here)):

            @pl.when((pl.program_id(0) == kind) & (pl.program_id(1) == side))
            def _():
                out[0] = total[0] + weight_term(x[...], weight[...])


def project_pair(got, near, far, total, unit, keep, cores):
    rows, depth = got[0].shape
    width = depth
    base = 0 if keep else 2
    vmem = pl.BlockSpec(memory_space=pltpu.VMEM)
    out = jax.ShapeDtypeStruct((2, rows, width), jnp.float32)
    out_spec = pl.BlockSpec((1, rows, width), lambda k, s, c: (k, 0, 0))
    w_spec = lambda side: pl.BlockSpec(
        (depth, width), lambda k, s, c: (0, base + c[side(k, s)])
    )
    return pl.pallas_call(
        pair_kernel,
        out_shape=[out, out],
        grid_spec=pltpu.PrefetchScalarGridSpec(
            num_scalar_prefetch=1,
            grid=(2, 2),
            in_specs=[
                vmem,
                vmem,
                w_spec(lambda k, s: jnp.where(k == 0, s, 1)),
                w_spec(lambda k, s: jnp.where(k == 0, 0, s)),
                pl.BlockSpec((1, rows, width), lambda k, s, c: (k, unit, 2 - base + s)),
            ],
            out_specs=[out_spec, out_spec],
            scratch_shapes=[pltpu.VMEM((2 * rows, depth), jnp.bfloat16)],
        ),
        compiler_params=pltpu.CompilerParams(vmem_limit_bytes=16 << 20),
        cost_estimate=LARGE,
    )(cores, *got, near, far, total)


def body(
    queries, key_rows, value_vectors, vertical_blocks, slash_offsets, prompt_length, out_weight
):
    rows = queries.shape[0]
    blocks = rows // BLOCK
    heads = queries.shape[1] // HEAD_SIZE
    seq_index = lax.axis_index("seq")
    head_index = lax.axis_index("head")
    head_size = lax.axis_size("head")
    core = head_index % 2
    chips = head_size // 2

    x, z = seq_index % 4, seq_index // 4
    ids = range(lax.axis_size("seq"))
    right = [(i, i // 4 * 4 + (i + 1) % 4) for i in ids]
    left = [(i, i // 4 * 4 + (i + 3) % 4) for i in ids]
    over = [(i, i // 4 * 4 + (i + 2) % 4) for i in ids]
    up = [(i, (i + 4) % 16) for i in ids]
    down = [(i, (i + 12) % 16) for i in ids]
    send = lambda a, pairs: lax.ppermute(a, "seq", pairs)
    swapped = lambda a, bits: send(a, [(i, i ^ bits) for i in ids])

    k_left = send(key_rows, right)
    k_right = send(key_rows, left)
    v_below = send(value_vectors, up)
    v_above = send(value_vectors, down)

    y = head_index // 2
    over_head = lambda a, bits: lax.ppermute(a, "head", [(i, i ^ bits) for i in range(head_size)])
    width = out_weight.shape[1] // head_size
    near_weight, far_weight = (
        over_head(take_columns(out_weight, jnp.stack([y ^ chip, y ^ 2]), 2 * width), 2 * chip)
        for chip in (1, 3)
    )

    vert = lax.dynamic_slice_in_dim(vertical_blocks, head_index * heads, heads, 0)
    slash = lax.dynamic_slice_in_dim(slash_offsets, head_index * heads, heads, 0)
    prompt = prompt_length[0]
    named = vert.reshape(-1)
    inside = jnp.arange(BLOCK, dtype=jnp.int32)
    vert_pos = vert[:, :, None] * BLOCK + inside
    vert_pos = jnp.where(vert_pos < prompt, -1, vert_pos).reshape(heads, 1, -1)
    offsets = jnp.concatenate([jnp.zeros((heads, 1), jnp.int32), slash + 1], axis=1)
    block_ids = seq_index * blocks + jnp.arange(blocks, dtype=jnp.int32)
    slash_block = block_ids[None, :, None] - offsets[:, None, :]
    repeated = jnp.any(slash_block[:, :, :, None] == vert[:, None, None, :], axis=-1)
    usable = (slash_block >= 0) & jnp.logical_not(repeated)
    slash_pos = slash_block[..., None] * BLOCK + inside
    slash_pos = jnp.where(slash_pos < prompt, -1, slash_pos)
    slash_pos = jnp.where(usable[..., None], slash_pos, FAR).reshape(heads, blocks, 1, -1)
    first_row = (seq_index * rows).reshape(1)
    back = 2 * blocks - offsets
    wraps = jnp.stack([x < 2, x == 0]).astype(jnp.int32)
    cores = jnp.stack([1 - core, core])
    order = jnp.concatenate([2 * chip + cores for chip in (y ^ 3, y, y ^ 1, y)])
    owner = named // blocks
    at = named % blocks
    k_place, k_held = (owner % 4 - x) % 4 * blocks + at, (owner // 4 == z).astype(jnp.int32)
    v_place, v_held = (owner // 4 - z) % 4 * blocks + at, (owner % 4 == x).astype(jnp.int32)
    orders = (order, cores)
    small = (vert_pos, slash_pos, first_row, back, wraps, orders, k_place, k_held, v_place, v_held)

    (k_left, k_right, v_below, v_above), small = lax.optimization_barrier(
        ((k_left, k_right, v_below, v_above), small)
    )
    vert_pos, slash_pos, first_row, back, wraps, orders, k_place, k_held, v_place, v_held = small
    half = rows // 2
    source = jnp.where(x >= 2, v_below, value_vectors)
    v_left = jnp.where(x == 3, v_below, value_vectors)
    moved_left = send(jnp.concatenate([k_right, source[half:]]), left)
    v_beyond = send(v_above, down)
    moved_right = send(jnp.concatenate([v_left, source[:half]]), right)
    k_left_wrap = send(k_left, [(i, i + 4) for i in ids if i % 4 == 0 and i + 4 in ids])
    moved_left, v_beyond, moved_right, k_left_wrap = lax.optimization_barrier(
        (moved_left, v_beyond, moved_right, k_left_wrap)
    )
    k_far, v_far_b = moved_left[:rows], moved_left[rows:]
    v_left, v_far_a = moved_right[:rows], moved_right[rows:]

    k_named = pick_blocks(k_place, k_held, (key_rows, k_right, k_far, k_left))
    v_named = pick_blocks(v_place, v_held, (value_vectors, v_above, v_beyond, v_below))
    v_far_a = send(v_far_a, right)
    v_far_b = send(v_far_b, left)
    k_far_wrap = send(k_far, [(i, i + 4) for i in ids if i % 4 < 2 and i + 4 in ids])
    named = [*k_named, *v_named]
    one, two = (4, 12, 1, 3), (12, 4, 3, 1)
    more = [swapped(a, bits) for a, bits in zip(named, one)]
    q = scaled(queries)
    q, v_far_a, v_far_b, k_far_wrap, *more = lax.optimization_barrier(
        (q, v_far_a, v_far_b, k_far_wrap, *more)
    )
    named = [a + b for a, b in zip(named, more)]
    arrays = (k_far, k_far_wrap, k_left, k_left_wrap, key_rows, v_far_a, v_far_b, v_left)
    near_arrays = (*arrays, value_vectors, slash_pos)
    near = attend_near(q, 0, rows, first_row, back, wraps, near_arrays)
    more = [swapped(a, bits) for a, bits in zip(named, two)]
    near, more = lax.optimization_barrier((near, more))
    arrays = (*(a + b for a, b in zip(named, more)), vert_pos)

    order, cores = orders
    meet, end = (2, 6), (6, 2)
    own_a = attend(q, *near, 0, first_row, arrays)
    q, own_a = lax.optimization_barrier((q, own_a))
    meeting = lambda parts: [over_head(parts[i], bits) for i, bits in enumerate(meet)]
    ending = lambda parts: [over_head(parts[i], bits) for i, bits in enumerate(end)]
    got_a = meeting(own_a)
    own_b = attend(q, *near, half, first_row, arrays)
    got_b = meeting(own_b)
    own_b, near_weight, far_weight = lax.optimization_barrier((own_b, near_weight, far_weight))
    total = project_chip(own_a, own_b, out_weight, order)
    total, got_a = lax.optimization_barrier((total, got_a))
    product = lambda got, unit, keep: project_pair(
        got, near_weight, far_weight, total, unit, keep, cores
    )
    there_a, here_a = product(got_a, 0, False)
    there_a, here_a, got_a = lax.optimization_barrier((there_a, here_a, got_a))
    keep_a = product(got_a, 0, True)
    there_a, keep_a, got_b = lax.optimization_barrier((there_a, keep_a, got_b))
    moved_a, keep_moved_a = over_head(there_a, 1), over_head(keep_a[0], 1)
    there_b, here_b = product(got_b, 1, False)
    there_b, here_b, moved_a, keep_moved_a, got_b = lax.optimization_barrier(
        (there_b, here_b, moved_a, keep_moved_a, got_b)
    )
    pass_a, pass_b = here_a + moved_a, here_b + over_head(there_b, 1)
    pass_a, pass_b, got_b = lax.optimization_barrier((pass_a, pass_b, got_b))
    sent = ending(pass_a) + ending(pass_b)
    keep_b = product(got_b, 1, True)
    keep_b, sent = lax.optimization_barrier((keep_b, sent))
    keep_moved_b = over_head(keep_b[0], 1)
    kept_a, kept_b = keep_a[1] + keep_moved_a, keep_b[1] + keep_moved_b
    kept = (kept_a[0], kept_a[1], kept_b[0], kept_b[1])
    return jnp.concatenate([a + b for a, b in zip(kept, sent)], axis=0)


def solution(mesh):
    placed = (P("seq", "head"), P("seq", "head"), P("seq", "head"), P(), P(), P(), P("head", None))
    return jax.shard_map(
        body, mesh=mesh, in_specs=placed, out_specs=P("seq", "head"), check_vma=False
    )
```

```python
import functools
import math

import jax
import jax.numpy as jnp
from jax import lax
from jax.experimental import pallas as pl
from jax.experimental.pallas import tpu as pltpu
from jax.sharding import PartitionSpec as P

HEAD_SIZE = 128
BLOCK = 64
TILE = 256
FAR = 1 << 30
LOW = -1e30
LARGE = pl.CostEstimate(flops=100000, bytes_accessed=1024, transcendentals=0)
HUGE = pl.CostEstimate(flops=6 << 30, bytes_accessed=1024, transcendentals=0)
SMALL = pl.CostEstimate(flops=1024, bytes_accessed=1024, transcendentals=0)


def pick_kernel(k_place, k_held, v_place, v_held, *refs):
    pieces, outs, rows = refs[:8], refs[8:12], refs[12:]
    size = pieces[0].shape[0]
    slots = outs[0].shape[0] // BLOCK
    for which, (place, held) in enumerate(((k_place, k_held), (v_place, v_held))):
        for at in range(4):
            rows[which][at * size : (at + 1) * size, :] = pieces[4 * which + at][...]
        for slot in range(2 * slots):
            out = outs[2 * which + slot // slots]
            target = pl.ds(slot % slots * BLOCK, BLOCK)

            @pl.when(held[slot] == 1)
            def _():
                start = pl.multiple_of(place[slot] * BLOCK, BLOCK)
                out[target, :] = rows[which][pl.ds(start, BLOCK), :]

            @pl.when(held[slot] == 0)
            def _():
                out[target, :] = jnp.zeros((BLOCK, HEAD_SIZE), jnp.float32)


def pick_blocks(k_place, k_held, v_place, v_held, k_pieces, v_pieces):
    half = k_place.shape[0] // 2 * BLOCK
    smem = pl.BlockSpec(memory_space=pltpu.SMEM)
    vmem = pl.BlockSpec(memory_space=pltpu.VMEM)
    out = jax.ShapeDtypeStruct((half, HEAD_SIZE), jnp.float32)
    size = k_pieces[0].shape[0]
    return pl.pallas_call(
        pick_kernel,
        out_shape=[out] * 4,
        in_specs=[smem] * 4 + [vmem] * 8,
        out_specs=[vmem] * 4,
        scratch_shapes=[pltpu.VMEM((4 * size, HEAD_SIZE), jnp.float32)] * 2,
        compiler_params=pltpu.CompilerParams(vmem_limit_bytes=16 << 20),
        cost_estimate=SMALL,
    )(k_place, k_held, v_place, v_held, *k_pieces, *v_pieces)


def split(x):
    high = x.astype(jnp.bfloat16)
    return high, (x - high.astype(jnp.float32)).astype(jnp.bfloat16)


def fold(x):
    half = x.shape[0] // 2
    return x[:half] + x[half:]


def put_parts(target, first, pieces):
    for piece in pieces:
        count = piece.shape[0]
        high, low = split(piece[...])
        target[first : first + count, 0:HEAD_SIZE] = high
        target[first : first + count, HEAD_SIZE:] = low
        first += count


dot = functools.partial(lax.dot_general, preferred_element_type=jnp.float32)
ACROSS = (((1,), (1,)), ((), ()))
DOWN = (((1,), (0,)), ((), ()))
SCALE = math.log2(math.e) / math.sqrt(HEAD_SIZE)


def query_parts(q):
    return (jnp.concatenate([x, x], axis=1) for x in split(q))


def scale_kernel(q, out):
    out[...] = q[...] * SCALE


def scaled(q):
    rows, width = q.shape
    spec = pl.BlockSpec((TILE, width), lambda i: (i, 0))
    return pl.pallas_call(
        scale_kernel,
        grid=(rows // TILE,),
        out_shape=jax.ShapeDtypeStruct(q.shape, jnp.float32),
        in_specs=[spec],
        out_specs=spec,
        compiler_params=pltpu.CompilerParams(vmem_limit_bytes=8 << 20),
        cost_estimate=HUGE,
    )(q)


def weights_of(scores, top):
    weights = jnp.exp2(scores - top)
    return weights, jnp.sum(weights, axis=1, keepdims=True)


def near_kernel(
    start, first_row, back, wraps, q, k_far, k_far_wrap, k_left, k_left_wrap, k_own,
    v_far_a, v_far_b, v_left, v_own, slash_pos, out, stats, near_k, near_v,
):
    turn = pl.program_id(0)

    @pl.when((turn == 0) & (pl.program_id(1) == 0))
    def _():
        rows = k_own.shape[0]
        for at, (plain, wrapped) in enumerate(((k_far, k_far_wrap), (k_left, k_left_wrap))):

            @pl.when(wraps[at] == 0)
            def _():
                put_parts(near_k, at * rows, (plain,))

            @pl.when(wraps[at] == 1)
            def _():
                put_parts(near_k, at * rows, (wrapped,))

        put_parts(near_k, 2 * rows, (k_own,))
        put_parts(near_v, 0, (v_far_a, v_far_b, v_left, v_own))

    q_pos = first_row[0] + start + turn * TILE + lax.broadcasted_iota(jnp.int32, (TILE, 1), 0)
    per_block = TILE // BLOCK
    pair = q.shape[1] // HEAD_SIZE
    lane = lax.broadcasted_iota(jnp.int32, (TILE, HEAD_SIZE), 1)
    known = jnp.zeros((TILE, HEAD_SIZE), jnp.float32)
    for part in range(pair):
        head = pl.program_id(1) * pair + part
        columns = slice(part * HEAD_SIZE, (part + 1) * HEAD_SIZE)
        high, low = query_parts(q[:, columns])
        scores, near = [], []
        for j in range(per_block):
            block = start // BLOCK + turn * per_block + j
            spots = [
                pl.ds(pl.multiple_of((block + back[head, n]) * BLOCK, BLOCK), BLOCK)
                for n in range(4)
            ]
            near.append(spots)
            keys = jnp.concatenate([near_k[s, :] for s in spots], axis=0)
            mine = slice(j * BLOCK, (j + 1) * BLOCK)
            score = fold(dot(jnp.concatenate([high[mine], low[mine]], axis=0), keys, ACROSS))
            scores.append(jnp.where(slash_pos[head, block] <= q_pos[mine], score, LOW))
        scores = jnp.concatenate(scores, axis=0)
        top = jnp.max(scores, axis=1, keepdims=True)
        weights, total = weights_of(scores, top)
        w_high, w_low = split(weights)
        parts = []
        for j in range(per_block):
            values = jnp.concatenate([near_v[s, :] for s in near[j]], axis=0)
            mine = slice(j * BLOCK, (j + 1) * BLOCK)
            stacked = jnp.concatenate([w_high[mine], w_low[mine]], axis=0)
            parts.append(fold(dot(stacked, values, DOWN)))
        mixed = jnp.concatenate(parts, axis=0)
        out[:, columns] = mixed[:, :HEAD_SIZE] + mixed[:, HEAD_SIZE:]
        known = jnp.where(lane == 2 * part, top, known)
        known = jnp.where(lane == 2 * part + 1, total, known)
    stats[...] = known


def attend_near(q, start, rows, first_row, back, wraps, arrays):
    width = q.shape[1]
    pair = 2
    count = width // (pair * HEAD_SIZE)
    base = start // TILE
    smem = pl.BlockSpec(memory_space=pltpu.SMEM)
    vmem = pl.BlockSpec(memory_space=pltpu.VMEM)
    wide = (TILE, pair * HEAD_SIZE)
    return pl.pallas_call(
        functools.partial(near_kernel, start),
        grid=(rows // TILE, count),
        out_shape=[
            jax.ShapeDtypeStruct((rows, width), jnp.float32),
            jax.ShapeDtypeStruct((rows, count * HEAD_SIZE), jnp.float32),
        ],
        in_specs=[smem, smem, smem, pl.BlockSpec(wide, lambda t, h: (base + t, h))]
        + [vmem] * len(arrays),
        out_specs=[
            pl.BlockSpec(wide, lambda t, h: (t, h)),
            pl.BlockSpec((TILE, HEAD_SIZE), lambda t, h: (t, h)),
        ],
        scratch_shapes=[pltpu.VMEM((3 * q.shape[0], 2 * HEAD_SIZE), jnp.bfloat16)] * 2,
        compiler_params=pltpu.CompilerParams(vmem_limit_bytes=24 << 20),
        cost_estimate=LARGE,
    )(first_row, back, wraps, q, *arrays)


def attend_kernel(
    start, first_row, q, near, stats, k_a, k_b, v_a, v_b, vert_pos, out, vert_k, vert_v
):
    turn = pl.program_id(0)

    @pl.when((turn == 0) & (pl.program_id(1) == 0))
    def _():
        put_parts(vert_k, 0, (k_a, k_b))
        put_parts(vert_v, 0, (v_a, v_b))

    q_pos = first_row[0] + start + turn * TILE + lax.broadcasted_iota(jnp.int32, (TILE, 1), 0)
    vert = vert_pos.shape[2]
    pair = q.shape[1] // HEAD_SIZE
    for part in range(pair):
        head = pl.program_id(1) * pair + part
        columns = slice(part * HEAD_SIZE, (part + 1) * HEAD_SIZE)
        rows = pl.ds(pl.multiple_of(head * vert, vert), vert)
        both = jnp.concatenate(list(query_parts(q[:, columns])), axis=0)
        scores = fold(dot(both, vert_k[rows, :], ACROSS))
        scores = jnp.where(vert_pos[head] <= q_pos, scores, LOW)
        near_top = stats[:, 2 * part : 2 * part + 1]
        top = jnp.maximum(jnp.max(scores, axis=1, keepdims=True), near_top)
        weights, total = weights_of(scores, top)
        keep = jnp.exp2(near_top - top)
        total = total + keep * stats[:, 2 * part + 1 : 2 * part + 2]
        mixed = fold(dot(jnp.concatenate(split(weights), axis=0), vert_v[rows, :], DOWN))
        mixed = mixed[:, :HEAD_SIZE] + mixed[:, HEAD_SIZE:] + keep * near[:, columns]
        out[0, :, columns] = mixed / total


def attend(q, near, stats, start, first_row, arrays):
    width = q.shape[1]
    heads = width // HEAD_SIZE
    pair = 2
    smem = pl.BlockSpec(memory_space=pltpu.SMEM)
    vmem = pl.BlockSpec(memory_space=pltpu.VMEM)
    base = start // TILE
    wide = (TILE, pair * HEAD_SIZE)
    return pl.pallas_call(
        functools.partial(attend_kernel, start),
        grid=(2, heads // pair),
        out_shape=jax.ShapeDtypeStruct((2, TILE, width), jnp.float32),
        in_specs=[
            smem,
            pl.BlockSpec(wide, lambda t, h: (base + t, h)),
            pl.BlockSpec(wide, lambda t, h: (t, h)),
            pl.BlockSpec((TILE, HEAD_SIZE), lambda t, h: (t, h)),
        ]
        + [vmem] * len(arrays),
        out_specs=pl.BlockSpec((1, TILE, pair * HEAD_SIZE), lambda t, h: (t, 0, h)),
        scratch_shapes=[pltpu.VMEM((heads * 8 * BLOCK, 2 * HEAD_SIZE), jnp.bfloat16)] * 2,
        compiler_params=pltpu.CompilerParams(vmem_limit_bytes=20 << 20),
        cost_estimate=LARGE,
    )(first_row, q, near, stats, *arrays)


def take_kernel(chips, one, two, three, near, far):
    width = one.shape[1]
    near[:, :width], near[:, width:] = one[...], two[...]
    far[:, :width], far[:, width:] = three[...], two[...]


def take_columns(weight, chips, width):
    rows = weight.shape[0]
    step = rows // 8
    out = jax.ShapeDtypeStruct((rows, 2 * width), jnp.float32)
    out_spec = pl.BlockSpec((step, 2 * width), lambda i, o: (i, 0))
    w_spec = lambda at: pl.BlockSpec((step, width), lambda i, o: (i, o[at]))
    return pl.pallas_call(
        take_kernel,
        out_shape=[out, out],
        grid_spec=pltpu.PrefetchScalarGridSpec(
            num_scalar_prefetch=1,
            grid=(rows // step,),
            in_specs=[w_spec(0), w_spec(1), w_spec(2)],
            out_specs=[out_spec, out_spec],
        ),
        compiler_params=pltpu.CompilerParams(vmem_limit_bytes=58 << 20),
        cost_estimate=SMALL,
    )(chips, weight, weight, weight)


def weight_term(x, block):
    high, low = split(block)
    return fold(dot(x, high, DOWN)) + dot(x[: x.shape[0] // 2], low, DOWN)


def stack(rows):
    return jnp.concatenate(split(rows), axis=0)


def chip_kernel(order, own_a, own_b, w, out, x):
    for kind in range(2):

        @pl.when((pl.program_id(0) == kind) & (pl.program_id(1) == 0))
        def _():
            x[...] = stack(jnp.concatenate([own_a[kind], own_b[kind]], axis=0))

    out[0] = weight_term(x[...], w[...])


def project_chip(own_a, own_b, weight, order):
    _, rows, depth = own_a.shape
    width = depth
    vmem = pl.BlockSpec(memory_space=pltpu.VMEM)
    return pl.pallas_call(
        chip_kernel,
        out_shape=jax.ShapeDtypeStruct((2, 2 * rows, 2 * width), jnp.float32),
        grid_spec=pltpu.PrefetchScalarGridSpec(
            num_scalar_prefetch=1,
            grid=(2, 2),
            in_specs=[vmem, vmem, pl.BlockSpec((depth, width), lambda k, j, o: (0, o[2 * k + j]))],
            out_specs=pl.BlockSpec((1, 2 * rows, width), lambda k, j, o: (k, 0, j)),
            scratch_shapes=[pltpu.VMEM((4 * rows, depth), jnp.bfloat16)],
        ),
        compiler_params=pltpu.CompilerParams(vmem_limit_bytes=20 << 20),
        cost_estimate=LARGE,
    )(order, own_a, own_b, weight)


def pair_kernel(cores, got_a, got_b, near, far, total, there, here, x):
    for kind, (got, weight) in enumerate(((got_a, near), (got_b, far))):

        @pl.when((pl.program_id(0) == kind) & (pl.program_id(1) == 0))
        def _():
            x[...] = stack(got[...])

        for side, out in enumerate((there, here)):

            @pl.when((pl.program_id(0) == kind) & (pl.program_id(1) == side))
            def _():
                out[0] = total[0] + weight_term(x[...], weight[...])


def project_pair(got, near, far, total, unit, keep, cores):
    rows, depth = got[0].shape
    width = depth
    base = 0 if keep else 2
    vmem = pl.BlockSpec(memory_space=pltpu.VMEM)
    out = jax.ShapeDtypeStruct((2, rows, width), jnp.float32)
    out_spec = pl.BlockSpec((1, rows, width), lambda k, s, c: (k, 0, 0))
    w_spec = lambda side: pl.BlockSpec(
        (depth, width), lambda k, s, c: (0, base + c[side(k, s)])
    )
    return pl.pallas_call(
        pair_kernel,
        out_shape=[out, out],
        grid_spec=pltpu.PrefetchScalarGridSpec(
            num_scalar_prefetch=1,
            grid=(2, 2),
            in_specs=[
                vmem,
                vmem,
                w_spec(lambda k, s: jnp.where(k == 0, s, 1)),
                w_spec(lambda k, s: jnp.where(k == 0, 0, s)),
                pl.BlockSpec((1, rows, width), lambda k, s, c: (k, unit, s)),
            ],
            out_specs=[out_spec, out_spec],
            scratch_shapes=[pltpu.VMEM((2 * rows, depth), jnp.bfloat16)],
        ),
        compiler_params=pltpu.CompilerParams(vmem_limit_bytes=16 << 20),
        cost_estimate=LARGE,
    )(cores, *got, near, far, total)


def body(
    queries, key_rows, value_vectors, vertical_blocks, slash_offsets, prompt_length, out_weight
):
    rows = queries.shape[0]
    blocks = rows // BLOCK
    heads = queries.shape[1] // HEAD_SIZE
    seq_index = lax.axis_index("seq")
    head_index = lax.axis_index("head")
    head_size = lax.axis_size("head")
    core = head_index % 2
    chips = head_size // 2

    x, z = seq_index % 4, seq_index // 4
    ids = range(lax.axis_size("seq"))
    right = [(i, i // 4 * 4 + (i + 1) % 4) for i in ids]
    left = [(i, i // 4 * 4 + (i + 3) % 4) for i in ids]
    over = [(i, i // 4 * 4 + (i + 2) % 4) for i in ids]
    up = [(i, (i + 4) % 16) for i in ids]
    down = [(i, (i + 12) % 16) for i in ids]
    send = lambda a, pairs: lax.ppermute(a, "seq", pairs)
    swapped = lambda a, bits: send(a, [(i, i ^ bits) for i in ids])

    k_left = send(key_rows, right)
    k_right = send(key_rows, left)
    v_below = send(value_vectors, up)
    v_above = send(value_vectors, down)

    y = head_index // 2
    over_head = lambda a, bits: lax.ppermute(a, "head", [(i, i ^ bits) for i in range(head_size)])
    width = out_weight.shape[1] // head_size
    near_weight, far_weight = take_columns(out_weight, y ^ jnp.arange(1, 4), 2 * width)
    near_weight, far_weight = over_head(near_weight, 2), over_head(far_weight, 6)

    vert = lax.dynamic_slice_in_dim(vertical_blocks, head_index * heads, heads, 0)
    slash = lax.dynamic_slice_in_dim(slash_offsets, head_index * heads, heads, 0)
    prompt = prompt_length[0]
    named = vert.reshape(-1)
    inside = jnp.arange(BLOCK, dtype=jnp.int32)
    vert_pos = vert[:, :, None] * BLOCK + inside
    vert_pos = jnp.where(vert_pos < prompt, -1, vert_pos).reshape(heads, 1, -1)
    offsets = jnp.concatenate([jnp.zeros((heads, 1), jnp.int32), slash + 1], axis=1)
    block_ids = seq_index * blocks + jnp.arange(blocks, dtype=jnp.int32)
    slash_block = block_ids[None, :, None] - offsets[:, None, :]
    repeated = jnp.any(slash_block[:, :, :, None] == vert[:, None, None, :], axis=-1)
    usable = (slash_block >= 0) & jnp.logical_not(repeated)
    slash_pos = slash_block[..., None] * BLOCK + inside
    slash_pos = jnp.where(slash_pos < prompt, -1, slash_pos)
    slash_pos = jnp.where(usable[..., None], slash_pos, FAR).reshape(heads, blocks, 1, -1)
    first_row = (seq_index * rows).reshape(1)
    back = 2 * blocks - offsets
    wraps = jnp.stack([x < 2, x == 0]).astype(jnp.int32)
    cores = jnp.stack([1 - core, core])
    pass_order = jnp.concatenate([2 * chip + cores for chip in (y ^ 3, y ^ 1)])
    keep_order = jnp.concatenate([2 * y + cores] * 2)
    owner = named // blocks
    at = named % blocks
    k_place, k_held = (owner % 4 - x) % 4 * blocks + at, (owner // 4 == z).astype(jnp.int32)
    v_place, v_held = (owner // 4 - z) % 4 * blocks + at, (owner % 4 == x).astype(jnp.int32)
    orders = (pass_order, keep_order, cores)
    small = (vert_pos, slash_pos, first_row, back, wraps, orders, k_place, k_held, v_place, v_held)

    (k_left, k_right, v_below, v_above), small = lax.optimization_barrier(
        ((k_left, k_right, v_below, v_above), small)
    )
    vert_pos, slash_pos, first_row, back, wraps, orders, k_place, k_held, v_place, v_held = small
    half = rows // 2
    source = jnp.where(x >= 2, v_below, value_vectors)
    v_left = jnp.where(x == 3, v_below, value_vectors)
    moved_left = send(jnp.concatenate([k_right, source[half:]]), left)
    v_beyond = send(v_above, down)
    moved_right = send(jnp.concatenate([v_left, source[:half]]), right)
    k_left_wrap = send(k_left, [(i, i + 4) for i in ids if i % 4 == 0 and i + 4 in ids])
    moved_left, v_beyond, moved_right, k_left_wrap = lax.optimization_barrier(
        (moved_left, v_beyond, moved_right, k_left_wrap)
    )
    k_far, v_far_b = moved_left[:rows], moved_left[rows:]
    v_left, v_far_a = moved_right[:rows], moved_right[rows:]

    k_pieces = (key_rows, k_right, k_far, k_left)
    v_pieces = (value_vectors, v_above, v_beyond, v_below)
    named = pick_blocks(k_place, k_held, v_place, v_held, k_pieces, v_pieces)
    v_far_a = send(v_far_a, right)
    v_far_b = send(v_far_b, left)
    k_far_wrap = send(k_far, [(i, i + 4) for i in ids if i % 4 < 2 and i + 4 in ids])
    one, two = (4, 12, 1, 3), (12, 4, 3, 1)
    more = [swapped(a, bits) for a, bits in zip(named, one)]
    q = scaled(queries)
    q, v_far_a, v_far_b, k_far_wrap, *more = lax.optimization_barrier(
        (q, v_far_a, v_far_b, k_far_wrap, *more)
    )
    named = [a + b for a, b in zip(named, more)]
    arrays = (k_far, k_far_wrap, k_left, k_left_wrap, key_rows, v_far_a, v_far_b, v_left)
    near_arrays = (*arrays, value_vectors, slash_pos)
    near = attend_near(q, 0, half, first_row, back, wraps, near_arrays)
    more = [swapped(a, bits) for a, bits in zip(named, two)]
    near, more = lax.optimization_barrier((near, more))
    arrays = (*(a + b for a, b in zip(named, more)), vert_pos)

    pass_order, keep_order, cores = orders
    meet, end = (2, 6), (6, 2)
    own_a = attend(q, *near, 0, first_row, arrays)
    q, own_a = lax.optimization_barrier((q, own_a))
    meeting = lambda parts: [over_head(parts[i], bits) for i, bits in enumerate(meet)]
    ending = lambda parts: [over_head(parts[i], bits) for i, bits in enumerate(end)]
    got_a = meeting(own_a)
    near = attend_near(q, half, half, first_row, back, wraps, near_arrays)
    own_b = attend(q, *near, half, first_row, arrays)
    got_b = meeting(own_b)
    own_b, near_weight, far_weight = lax.optimization_barrier((own_b, near_weight, far_weight))
    total = project_chip(own_a, own_b, out_weight, pass_order)
    total, got_a = lax.optimization_barrier((total, got_a))
    product = lambda got, total, unit, keep: project_pair(
        got, near_weight, far_weight, total, unit, keep, cores
    )
    there_a, here_a = product(got_a, total, 0, False)
    own_b, there_a, here_a, got_a = lax.optimization_barrier((own_b, there_a, here_a, got_a))
    kept_total = project_chip(own_a, own_b, out_weight, keep_order)
    kept_total, there_a, got_b = lax.optimization_barrier((kept_total, there_a, got_b))
    moved_a = over_head(there_a, 1)
    there_b, here_b = product(got_b, total, 1, False)
    there_b, here_b, moved_a, got_b = lax.optimization_barrier((there_b, here_b, moved_a, got_b))
    pass_a, pass_b = here_a + moved_a, here_b + over_head(there_b, 1)
    pass_a, pass_b, got_a, got_b = lax.optimization_barrier((pass_a, pass_b, got_a, got_b))
    sent = ending(pass_a) + ending(pass_b)
    keep_a = product(got_a, kept_total, 0, True)
    keep_b = product(got_b, kept_total, 1, True)
    keep_a, keep_b, sent = lax.optimization_barrier((keep_a, keep_b, sent))
    kept_a, kept_b = (here + over_head(there, 1) for there, here in (keep_a, keep_b))
    kept = (kept_a[0], kept_a[1], kept_b[0], kept_b[1])
    return jnp.concatenate([a + b for a, b in zip(kept, sent)], axis=0)


def solution(mesh):
    placed = (P("seq", "head"), P("seq", "head"), P("seq", "head"), P(), P(), P(), P("head", None))
    return jax.shard_map(
        body, mesh=mesh, in_specs=placed, out_specs=P("seq", "head"), check_vma=False
    )
```

```python
import functools
import math

import jax
import jax.numpy as jnp
from jax import lax
from jax.experimental import pallas as pl
from jax.experimental.pallas import tpu as pltpu
from jax.sharding import PartitionSpec as P

HEAD_SIZE = 128
BLOCK = 64
TILE = 256
FAR = 1 << 30
LOW = -1e30
LARGE = pl.CostEstimate(flops=100000, bytes_accessed=1024, transcendentals=0)
HUGE = pl.CostEstimate(flops=6 << 30, bytes_accessed=1024, transcendentals=0)
SMALL = pl.CostEstimate(flops=1024, bytes_accessed=1024, transcendentals=0)


def pick_kernel(k_place, k_held, v_place, v_held, *refs):
    pieces, outs, rows = refs[:8], refs[8:12], refs[12:]
    size = pieces[0].shape[0]
    slots = outs[0].shape[0] // BLOCK
    for which, (place, held) in enumerate(((k_place, k_held), (v_place, v_held))):
        for at in range(4):
            rows[which][at * size : (at + 1) * size, :] = pieces[4 * which + at][...]
        for slot in range(2 * slots):
            out = outs[2 * which + slot // slots]
            target = pl.ds(slot % slots * BLOCK, BLOCK)

            @pl.when(held[slot] == 1)
            def _():
                start = pl.multiple_of(place[slot] * BLOCK, BLOCK)
                out[target, :] = rows[which][pl.ds(start, BLOCK), :]

            @pl.when(held[slot] == 0)
            def _():
                out[target, :] = jnp.zeros((BLOCK, HEAD_SIZE), jnp.float32)


def pick_blocks(k_place, k_held, v_place, v_held, k_pieces, v_pieces):
    half = k_place.shape[0] // 2 * BLOCK
    smem = pl.BlockSpec(memory_space=pltpu.SMEM)
    vmem = pl.BlockSpec(memory_space=pltpu.VMEM)
    out = jax.ShapeDtypeStruct((half, HEAD_SIZE), jnp.float32)
    size = k_pieces[0].shape[0]
    return pl.pallas_call(
        pick_kernel,
        out_shape=[out] * 4,
        in_specs=[smem] * 4 + [vmem] * 8,
        out_specs=[vmem] * 4,
        scratch_shapes=[pltpu.VMEM((4 * size, HEAD_SIZE), jnp.float32)] * 2,
        compiler_params=pltpu.CompilerParams(vmem_limit_bytes=16 << 20),
        cost_estimate=SMALL,
    )(k_place, k_held, v_place, v_held, *k_pieces, *v_pieces)


def split(x):
    high = x.astype(jnp.bfloat16)
    return high, (x - high.astype(jnp.float32)).astype(jnp.bfloat16)


def fold(x):
    half = x.shape[0] // 2
    return x[:half] + x[half:]


def put_parts(target, first, pieces):
    for piece in pieces:
        count = piece.shape[0]
        high, low = split(piece[...])
        target[first : first + count, 0:HEAD_SIZE] = high
        target[first : first + count, HEAD_SIZE:] = low
        first += count


dot = functools.partial(lax.dot_general, preferred_element_type=jnp.float32)
ACROSS = (((1,), (1,)), ((), ()))
DOWN = (((1,), (0,)), ((), ()))
SCALE = math.log2(math.e) / math.sqrt(HEAD_SIZE)


def query_parts(q):
    return (jnp.concatenate([x, x], axis=1) for x in split(q))


def scale_kernel(q, out):
    out[...] = q[...] * SCALE


def scaled(q):
    rows, width = q.shape
    spec = pl.BlockSpec((TILE, width), lambda i: (i, 0))
    return pl.pallas_call(
        scale_kernel,
        grid=(rows // TILE,),
        out_shape=jax.ShapeDtypeStruct(q.shape, jnp.float32),
        in_specs=[spec],
        out_specs=spec,
        compiler_params=pltpu.CompilerParams(vmem_limit_bytes=8 << 20),
        cost_estimate=HUGE,
    )(q)


def weights_of(scores, top):
    weights = jnp.exp2(scores - top)
    return weights, jnp.sum(weights, axis=1, keepdims=True)


def near_kernel(
    start, first_row, back, wraps, q, k_far, k_far_wrap, k_left, k_left_wrap, k_own,
    v_far_a, v_far_b, v_left, v_own, slash_pos, out, stats, near_k, near_v,
):
    turn = pl.program_id(0)

    @pl.when((turn == 0) & (pl.program_id(1) == 0))
    def _():
        rows = k_own.shape[0]
        for at, (plain, wrapped) in enumerate(((k_far, k_far_wrap), (k_left, k_left_wrap))):

            @pl.when(wraps[at] == 0)
            def _():
                put_parts(near_k, at * rows, (plain,))

            @pl.when(wraps[at] == 1)
            def _():
                put_parts(near_k, at * rows, (wrapped,))

        put_parts(near_k, 2 * rows, (k_own,))
        put_parts(near_v, 0, (v_far_a, v_far_b, v_left, v_own))

    q_pos = first_row[0] + start + turn * TILE + lax.broadcasted_iota(jnp.int32, (TILE, 1), 0)
    per_block = TILE // BLOCK
    pair = q.shape[1] // HEAD_SIZE
    lane = lax.broadcasted_iota(jnp.int32, (TILE, HEAD_SIZE), 1)
    known = jnp.zeros((TILE, HEAD_SIZE), jnp.float32)
    for part in range(pair):
        head = pl.program_id(1) * pair + part
        columns = slice(part * HEAD_SIZE, (part + 1) * HEAD_SIZE)
        high, low = query_parts(q[:, columns])
        scores, near = [], []
        for j in range(per_block):
            block = start // BLOCK + turn * per_block + j
            spots = [
                pl.ds(pl.multiple_of((block + back[head, n]) * BLOCK, BLOCK), BLOCK)
                for n in range(4)
            ]
            near.append(spots)
            keys = jnp.concatenate([near_k[s, :] for s in spots], axis=0)
            mine = slice(j * BLOCK, (j + 1) * BLOCK)
            score = fold(dot(jnp.concatenate([high[mine], low[mine]], axis=0), keys, ACROSS))
            scores.append(jnp.where(slash_pos[head, block] <= q_pos[mine], score, LOW))
        scores = jnp.concatenate(scores, axis=0)
        top = jnp.max(scores, axis=1, keepdims=True)
        weights, total = weights_of(scores, top)
        w_high, w_low = split(weights)
        parts = []
        for j in range(per_block):
            values = jnp.concatenate([near_v[s, :] for s in near[j]], axis=0)
            mine = slice(j * BLOCK, (j + 1) * BLOCK)
            stacked = jnp.concatenate([w_high[mine], w_low[mine]], axis=0)
            parts.append(fold(dot(stacked, values, DOWN)))
        mixed = jnp.concatenate(parts, axis=0)
        out[:, columns] = mixed[:, :HEAD_SIZE] + mixed[:, HEAD_SIZE:]
        known = jnp.where(lane == 2 * part, top, known)
        known = jnp.where(lane == 2 * part + 1, total, known)
    stats[...] = known


def attend_near(q, start, rows, first_row, back, wraps, arrays):
    width = q.shape[1]
    pair = 2
    count = width // (pair * HEAD_SIZE)
    base = start // TILE
    smem = pl.BlockSpec(memory_space=pltpu.SMEM)
    vmem = pl.BlockSpec(memory_space=pltpu.VMEM)
    wide = (TILE, pair * HEAD_SIZE)
    return pl.pallas_call(
        functools.partial(near_kernel, start),
        grid=(rows // TILE, count),
        out_shape=[
            jax.ShapeDtypeStruct((rows, width), jnp.float32),
            jax.ShapeDtypeStruct((rows, count * HEAD_SIZE), jnp.float32),
        ],
        in_specs=[smem, smem, smem, pl.BlockSpec(wide, lambda t, h: (base + t, h))]
        + [vmem] * len(arrays),
        out_specs=[
            pl.BlockSpec(wide, lambda t, h: (t, h)),
            pl.BlockSpec((TILE, HEAD_SIZE), lambda t, h: (t, h)),
        ],
        scratch_shapes=[pltpu.VMEM((3 * q.shape[0], 2 * HEAD_SIZE), jnp.bfloat16)] * 2,
        compiler_params=pltpu.CompilerParams(vmem_limit_bytes=24 << 20),
        cost_estimate=LARGE,
    )(first_row, back, wraps, q, *arrays)


def attend_kernel(
    start, first_row, q, near, stats, k_a, k_b, v_a, v_b, vert_pos, out, vert_k, vert_v
):
    turn = pl.program_id(0)

    @pl.when((turn == 0) & (pl.program_id(1) == 0))
    def _():
        put_parts(vert_k, 0, (k_a, k_b))
        put_parts(vert_v, 0, (v_a, v_b))

    q_pos = first_row[0] + start + turn * TILE + lax.broadcasted_iota(jnp.int32, (TILE, 1), 0)
    vert = vert_pos.shape[2]
    pair = q.shape[1] // HEAD_SIZE
    for part in range(pair):
        head = pl.program_id(1) * pair + part
        columns = slice(part * HEAD_SIZE, (part + 1) * HEAD_SIZE)
        rows = pl.ds(pl.multiple_of(head * vert, vert), vert)
        both = jnp.concatenate(list(query_parts(q[:, columns])), axis=0)
        scores = fold(dot(both, vert_k[rows, :], ACROSS))
        scores = jnp.where(vert_pos[head] <= q_pos, scores, LOW)
        near_top = stats[:, 2 * part : 2 * part + 1]
        top = jnp.maximum(jnp.max(scores, axis=1, keepdims=True), near_top)
        weights, total = weights_of(scores, top)
        keep = jnp.exp2(near_top - top)
        total = total + keep * stats[:, 2 * part + 1 : 2 * part + 2]
        mixed = fold(dot(jnp.concatenate(split(weights), axis=0), vert_v[rows, :], DOWN))
        mixed = mixed[:, :HEAD_SIZE] + mixed[:, HEAD_SIZE:] + keep * near[:, columns]
        out[0, :, columns] = mixed / total


def attend(q, near, stats, start, first_row, arrays):
    width = q.shape[1]
    heads = width // HEAD_SIZE
    pair = 2
    smem = pl.BlockSpec(memory_space=pltpu.SMEM)
    vmem = pl.BlockSpec(memory_space=pltpu.VMEM)
    base = start // TILE
    wide = (TILE, pair * HEAD_SIZE)
    return pl.pallas_call(
        functools.partial(attend_kernel, start),
        grid=(2, heads // pair),
        out_shape=jax.ShapeDtypeStruct((2, TILE, width), jnp.float32),
        in_specs=[
            smem,
            pl.BlockSpec(wide, lambda t, h: (base + t, h)),
            pl.BlockSpec(wide, lambda t, h: (base + t, h)),
            pl.BlockSpec((TILE, HEAD_SIZE), lambda t, h: (base + t, h)),
        ]
        + [vmem] * len(arrays),
        out_specs=pl.BlockSpec((1, TILE, pair * HEAD_SIZE), lambda t, h: (t, 0, h)),
        scratch_shapes=[pltpu.VMEM((heads * 8 * BLOCK, 2 * HEAD_SIZE), jnp.bfloat16)] * 2,
        compiler_params=pltpu.CompilerParams(vmem_limit_bytes=20 << 20),
        cost_estimate=LARGE,
    )(first_row, q, near, stats, *arrays)


def take_kernel(chips, one, two, three, near, far, near_late, far_late):
    rows = one.shape[0]
    early = near.shape[0] - rows
    near[:rows, :] = two[...]
    far[:rows, :] = two[...]
    near[rows:, :] = one[:early, :]
    far[rows:, :] = three[:early, :]
    near_late[...] = one[early:, :]
    far_late[...] = three[early:, :]


def take_columns(weight, chips, width, late):
    rows = weight.shape[0]
    part = width // 4
    shape = lambda n: jax.ShapeDtypeStruct((n, width), jnp.float32)
    out_spec = lambda n: pl.BlockSpec((n, part), lambda i, o: (0, i))
    w_spec = lambda at: pl.BlockSpec((rows, part), lambda i, o: (0, 4 * o[at] + i))
    sizes = (2 * rows - late, 2 * rows - late, late, late)
    return pl.pallas_call(
        take_kernel,
        out_shape=[shape(n) for n in sizes],
        grid_spec=pltpu.PrefetchScalarGridSpec(
            num_scalar_prefetch=1,
            grid=(4,),
            in_specs=[w_spec(0), w_spec(1), w_spec(2)],
            out_specs=[out_spec(n) for n in sizes],
        ),
        compiler_params=pltpu.CompilerParams(vmem_limit_bytes=58 << 20),
        cost_estimate=SMALL,
    )(chips, weight, weight, weight)


def weight_term(x, block):
    high, low = split(block)
    return fold(dot(x, high, DOWN)) + dot(x[: x.shape[0] // 2], low, DOWN)


def stack(rows):
    return jnp.concatenate(split(rows), axis=0)


def chip_kernel(order, own_a, own_b, w, out, x):
    for kind in range(2):

        @pl.when((pl.program_id(0) == kind) & (pl.program_id(1) == 0))
        def _():
            x[...] = stack(jnp.concatenate([own_a[kind], own_b[kind]], axis=0))

    out[0] = weight_term(x[...], w[...])


def project_chip(own_a, own_b, weight, order):
    _, rows, depth = own_a.shape
    width = depth
    vmem = pl.BlockSpec(memory_space=pltpu.VMEM)
    return pl.pallas_call(
        chip_kernel,
        out_shape=jax.ShapeDtypeStruct((2, 2 * rows, 2 * width), jnp.float32),
        grid_spec=pltpu.PrefetchScalarGridSpec(
            num_scalar_prefetch=1,
            grid=(2, 2),
            in_specs=[vmem, vmem, pl.BlockSpec((depth, width), lambda k, j, o: (0, o[2 * k + j]))],
            out_specs=pl.BlockSpec((1, 2 * rows, width), lambda k, j, o: (k, 0, j)),
            scratch_shapes=[pltpu.VMEM((4 * rows, depth), jnp.bfloat16)],
        ),
        compiler_params=pltpu.CompilerParams(vmem_limit_bytes=20 << 20),
        cost_estimate=LARGE,
    )(order, own_a, own_b, weight)


def pair_kernel(cores, got_a, got_b, near, far, total, there, here, x):
    for kind, (got, weight) in enumerate(((got_a, near), (got_b, far))):

        @pl.when((pl.program_id(0) == kind) & (pl.program_id(1) == 0))
        def _():
            x[...] = stack(got[...])

        for side, out in enumerate((there, here)):

            @pl.when((pl.program_id(0) == kind) & (pl.program_id(1) == side))
            def _():
                out[0] = total[0] + weight_term(x[...], weight[...])


def project_pair(got, near, far, total, unit, cores):
    rows, depth = got[0].shape
    width = depth
    vmem = pl.BlockSpec(memory_space=pltpu.VMEM)
    out = jax.ShapeDtypeStruct((2, rows, width), jnp.float32)
    out_spec = pl.BlockSpec((1, rows, width), lambda k, s, c: (k, 0, 0))
    w_spec = lambda side: pl.BlockSpec(
        (depth, width), lambda k, s, c: (0, c[side(k, s)])
    )
    return pl.pallas_call(
        pair_kernel,
        out_shape=[out, out],
        grid_spec=pltpu.PrefetchScalarGridSpec(
            num_scalar_prefetch=1,
            grid=(2, 2),
            in_specs=[
                vmem,
                vmem,
                w_spec(lambda k, s: jnp.where(k == 0, s, 1)),
                w_spec(lambda k, s: jnp.where(k == 0, 0, s)),
                pl.BlockSpec((1, rows, width), lambda k, s, c: (k, unit, s)),
            ],
            out_specs=[out_spec, out_spec],
            scratch_shapes=[pltpu.VMEM((2 * rows, depth), jnp.bfloat16)],
        ),
        compiler_params=pltpu.CompilerParams(vmem_limit_bytes=16 << 20),
        cost_estimate=LARGE,
    )(cores, *got, near, far, total)


def body(
    queries, key_rows, value_vectors, vertical_blocks, slash_offsets, prompt_length, out_weight
):
    rows = queries.shape[0]
    blocks = rows // BLOCK
    heads = queries.shape[1] // HEAD_SIZE
    seq_index = lax.axis_index("seq")
    head_index = lax.axis_index("head")
    head_size = lax.axis_size("head")
    core = head_index % 2
    chips = head_size // 2

    x, z = seq_index % 4, seq_index // 4
    ids = range(lax.axis_size("seq"))
    right = [(i, i // 4 * 4 + (i + 1) % 4) for i in ids]
    left = [(i, i // 4 * 4 + (i + 3) % 4) for i in ids]
    over = [(i, i // 4 * 4 + (i + 2) % 4) for i in ids]
    up = [(i, (i + 4) % 16) for i in ids]
    down = [(i, (i + 12) % 16) for i in ids]
    send = lambda a, pairs: lax.ppermute(a, "seq", pairs)
    swapped = lambda a, bits: send(a, [(i, i ^ bits) for i in ids])

    k_left = send(key_rows, right)
    k_right = send(key_rows, left)
    v_below = send(value_vectors, up)
    v_above = send(value_vectors, down)

    y = head_index // 2
    over_head = lambda a, bits: lax.ppermute(a, "head", [(i, i ^ bits) for i in range(head_size)])
    width = out_weight.shape[1] // head_size
    late = out_weight.shape[0] // 8
    near_weight, far_weight, *late_weights = take_columns(
        out_weight, y ^ jnp.arange(1, 4), 2 * width, late
    )
    near_weight, far_weight = over_head(near_weight, 2), over_head(far_weight, 6)

    vert = lax.dynamic_slice_in_dim(vertical_blocks, head_index * heads, heads, 0)
    slash = lax.dynamic_slice_in_dim(slash_offsets, head_index * heads, heads, 0)
    prompt = prompt_length[0]
    named = vert.reshape(-1)
    inside = jnp.arange(BLOCK, dtype=jnp.int32)
    vert_pos = vert[:, :, None] * BLOCK + inside
    vert_pos = jnp.where(vert_pos < prompt, -1, vert_pos).reshape(heads, 1, -1)
    offsets = jnp.concatenate([jnp.zeros((heads, 1), jnp.int32), slash + 1], axis=1)
    block_ids = seq_index * blocks + jnp.arange(blocks, dtype=jnp.int32)
    slash_block = block_ids[None, :, None] - offsets[:, None, :]
    repeated = jnp.any(slash_block[:, :, :, None] == vert[:, None, None, :], axis=-1)
    usable = (slash_block >= 0) & jnp.logical_not(repeated)
    slash_pos = slash_block[..., None] * BLOCK + inside
    slash_pos = jnp.where(slash_pos < prompt, -1, slash_pos)
    slash_pos = jnp.where(usable[..., None], slash_pos, FAR).reshape(heads, blocks, 1, -1)
    first_row = (seq_index * rows).reshape(1)
    back = 2 * blocks - offsets
    wraps = jnp.stack([x < 2, x == 0]).astype(jnp.int32)
    cores = jnp.stack([1 - core, core])
    pass_order = jnp.concatenate([2 * chip + cores for chip in (y ^ 3, y ^ 1)])
    keep_order = jnp.concatenate([2 * y + cores] * 2)
    owner = named // blocks
    at = named % blocks
    k_place, k_held = (owner % 4 - x) % 4 * blocks + at, (owner // 4 == z).astype(jnp.int32)
    v_place, v_held = (owner // 4 - z) % 4 * blocks + at, (owner % 4 == x).astype(jnp.int32)
    orders = (pass_order, keep_order, cores)
    small = (vert_pos, slash_pos, first_row, back, wraps, orders, k_place, k_held, v_place, v_held)

    (k_left, k_right, v_below, v_above), small = lax.optimization_barrier(
        ((k_left, k_right, v_below, v_above), small)
    )
    vert_pos, slash_pos, first_row, back, wraps, orders, k_place, k_held, v_place, v_held = small
    half = rows // 2
    source = jnp.where(x >= 2, v_below, value_vectors)
    v_left = jnp.where(x == 3, v_below, value_vectors)
    moved_left = send(jnp.concatenate([k_right, source[half:]]), left)
    v_beyond = send(v_above, down)
    moved_right = send(jnp.concatenate([v_left, source[:half]]), right)
    k_left_wrap = send(k_left, [(i, i + 4) for i in ids if i % 4 == 0 and i + 4 in ids])
    moved_left, v_beyond, moved_right, k_left_wrap = lax.optimization_barrier(
        (moved_left, v_beyond, moved_right, k_left_wrap)
    )
    k_far, v_far_b = moved_left[:rows], moved_left[rows:]
    v_left, v_far_a = moved_right[:rows], moved_right[rows:]

    k_pieces = (key_rows, k_right, k_far, k_left)
    v_pieces = (value_vectors, v_above, v_beyond, v_below)
    named = pick_blocks(k_place, k_held, v_place, v_held, k_pieces, v_pieces)
    v_far_a = send(v_far_a, right)
    v_far_b = send(v_far_b, left)
    k_far_wrap = send(k_far, [(i, i + 4) for i in ids if i % 4 < 2 and i + 4 in ids])
    one, two = (4, 12, 1, 3), (12, 4, 3, 1)
    more = [swapped(a, bits) for a, bits in zip(named, one)]
    q = scaled(queries)
    q, v_far_a, v_far_b, k_far_wrap, *more = lax.optimization_barrier(
        (q, v_far_a, v_far_b, k_far_wrap, *more)
    )
    named = [a + b for a, b in zip(named, more)]
    arrays = (k_far, k_far_wrap, k_left, k_left_wrap, key_rows, v_far_a, v_far_b, v_left)
    near_arrays = (*arrays, value_vectors, slash_pos)
    near = attend_near(q, 0, rows, first_row, back, wraps, near_arrays)
    more = [swapped(a, bits) for a, bits in zip(named, two)]
    near, more = lax.optimization_barrier((near, more))
    arrays = (*(a + b for a, b in zip(named, more)), vert_pos)

    pass_order, keep_order, cores = orders
    meet, end = (2, 6), (6, 2)
    own_a = attend(q, *near, 0, first_row, arrays)
    q, own_a, near_weight, far_weight = lax.optimization_barrier(
        (q, own_a, near_weight, far_weight)
    )
    meeting = lambda parts: [over_head(parts[i], bits) for i, bits in enumerate(meet)]
    ending = lambda parts: [over_head(parts[i], bits) for i, bits in enumerate(end)]
    got_a = meeting(own_a)
    own_b = attend(q, *near, half, first_row, arrays)
    got_b = meeting(own_b)
    own_b, got_a = lax.optimization_barrier((own_b, got_a))
    total = project_chip(own_a, own_b, out_weight, pass_order)
    product = lambda got, weights, total, unit: project_pair(got, *weights, total, unit, cores)
    weights = (near_weight, far_weight)
    there_a, here_a = product(got_a, weights, total, 0)
    there_a, here_a, got_a, got_b = lax.optimization_barrier((there_a, here_a, got_a, got_b))
    moved_a = over_head(there_a, 1)
    there_b, here_b = product(got_b, weights, total, 1)
    late_weights = [over_head(a, bits) for a, bits in zip(late_weights, meet)]
    there_b, here_b, moved_a, late_weights = lax.optimization_barrier(
        (there_b, here_b, moved_a, late_weights)
    )
    pass_a, pass_b = here_a + moved_a, here_b + over_head(there_b, 1)
    pass_a, pass_b, got_a, got_b, own_b = lax.optimization_barrier(
        (pass_a, pass_b, got_a, got_b, own_b)
    )
    sent = ending(pass_a) + ending(pass_b)
    rows = out_weight.shape[0]
    weights = [jnp.concatenate([a[rows:], b]) for a, b in zip(weights, late_weights)]
    total = project_chip(own_a, own_b, out_weight, keep_order)
    keep_a = product(got_a, weights, total, 0)
    keep_b = product(got_b, weights, total, 1)
    keep_a, keep_b, sent = lax.optimization_barrier((keep_a, keep_b, sent))
    kept_a, kept_b = (here + over_head(there, 1) for there, here in (keep_a, keep_b))
    kept = (kept_a[0], kept_a[1], kept_b[0], kept_b[1])
    return jnp.concatenate([a + b for a, b in zip(kept, sent)], axis=0)


def solution(mesh):
    placed = (P("seq", "head"), P("seq", "head"), P("seq", "head"), P(), P(), P(), P("head", None))
    return jax.shard_map(
        body, mesh=mesh, in_specs=placed, out_specs=P("seq", "head"), check_vma=False
    )
```

```python
import functools
import math

import jax
import jax.numpy as jnp
from jax import lax
from jax.experimental import pallas as pl
from jax.experimental.pallas import tpu as pltpu
from jax.sharding import PartitionSpec as P

HEAD_SIZE = 128
BLOCK = 64
TILE = 256
FAR = 1 << 30
LOW = -1e30
LARGE = pl.CostEstimate(flops=100000, bytes_accessed=1024, transcendentals=0)
HUGE = pl.CostEstimate(flops=6 << 30, bytes_accessed=1024, transcendentals=0)
SMALL = pl.CostEstimate(flops=1024, bytes_accessed=1024, transcendentals=0)


def pick_kernel(k_place, k_held, v_place, v_held, *refs):
    pieces, outs, rows = refs[:8], refs[8:12], refs[12:]
    size = pieces[0].shape[0]
    slots = outs[0].shape[0] // BLOCK
    for which, (place, held) in enumerate(((k_place, k_held), (v_place, v_held))):
        for at in range(4):
            rows[which][at * size : (at + 1) * size, :] = pieces[4 * which + at][...]
        for slot in range(2 * slots):
            out = outs[2 * which + slot // slots]
            target = pl.ds(slot % slots * BLOCK, BLOCK)

            @pl.when(held[slot] == 1)
            def _():
                start = pl.multiple_of(place[slot] * BLOCK, BLOCK)
                out[target, :] = rows[which][pl.ds(start, BLOCK), :]

            @pl.when(held[slot] == 0)
            def _():
                out[target, :] = jnp.zeros((BLOCK, HEAD_SIZE), jnp.float32)


def pick_blocks(k_place, k_held, v_place, v_held, k_pieces, v_pieces):
    half = k_place.shape[0] // 2 * BLOCK
    smem = pl.BlockSpec(memory_space=pltpu.SMEM)
    vmem = pl.BlockSpec(memory_space=pltpu.VMEM)
    out = jax.ShapeDtypeStruct((half, HEAD_SIZE), jnp.float32)
    size = k_pieces[0].shape[0]
    return pl.pallas_call(
        pick_kernel,
        out_shape=[out] * 4,
        in_specs=[smem] * 4 + [vmem] * 8,
        out_specs=[vmem] * 4,
        scratch_shapes=[pltpu.VMEM((4 * size, HEAD_SIZE), jnp.float32)] * 2,
        compiler_params=pltpu.CompilerParams(vmem_limit_bytes=16 << 20),
        cost_estimate=SMALL,
    )(k_place, k_held, v_place, v_held, *k_pieces, *v_pieces)


def split(x):
    high = x.astype(jnp.bfloat16)
    return high, (x - high.astype(jnp.float32)).astype(jnp.bfloat16)


def fold(x):
    half = x.shape[0] // 2
    return x[:half] + x[half:]


def put_parts(target, first, pieces):
    for piece in pieces:
        count = piece.shape[0]
        high, low = split(piece[...])
        target[first : first + count, 0:HEAD_SIZE] = high
        target[first : first + count, HEAD_SIZE:] = low
        first += count


dot = functools.partial(lax.dot_general, preferred_element_type=jnp.float32)
ACROSS = (((1,), (1,)), ((), ()))
DOWN = (((1,), (0,)), ((), ()))
SCALE = math.log2(math.e) / math.sqrt(HEAD_SIZE)


def query_parts(q):
    return (jnp.concatenate([x, x], axis=1) for x in split(q))


def scale_kernel(q, out):
    out[...] = q[...] * SCALE


def scaled(q):
    rows, width = q.shape
    spec = pl.BlockSpec((TILE, width), lambda i: (i, 0))
    return pl.pallas_call(
        scale_kernel,
        grid=(rows // TILE,),
        out_shape=jax.ShapeDtypeStruct(q.shape, jnp.float32),
        in_specs=[spec],
        out_specs=spec,
        compiler_params=pltpu.CompilerParams(vmem_limit_bytes=8 << 20),
        cost_estimate=HUGE,
    )(q)


def weights_of(scores, top):
    weights = jnp.exp2(scores - top)
    return weights, jnp.sum(weights, axis=1, keepdims=True)


def near_kernel(
    start, first_row, back, wraps, q, k_far, k_far_wrap, k_left, k_left_wrap, k_own,
    v_far_a, v_far_b, v_left, v_own, slash_pos, out, stats, near_k, near_v,
):
    turn = pl.program_id(0)

    @pl.when((turn == 0) & (pl.program_id(1) == 0))
    def _():
        rows = k_own.shape[0]
        for at, (plain, wrapped) in enumerate(((k_far, k_far_wrap), (k_left, k_left_wrap))):

            @pl.when(wraps[at] == 0)
            def _():
                put_parts(near_k, at * rows, (plain,))

            @pl.when(wraps[at] == 1)
            def _():
                put_parts(near_k, at * rows, (wrapped,))

        put_parts(near_k, 2 * rows, (k_own,))
        put_parts(near_v, 0, (v_far_a, v_far_b, v_left, v_own))

    q_pos = first_row[0] + start + turn * TILE + lax.broadcasted_iota(jnp.int32, (TILE, 1), 0)
    per_block = TILE // BLOCK
    pair = q.shape[1] // HEAD_SIZE
    lane = lax.broadcasted_iota(jnp.int32, (TILE, HEAD_SIZE), 1)
    known = jnp.zeros((TILE, HEAD_SIZE), jnp.float32)
    for part in range(pair):
        head = pl.program_id(1) * pair + part
        columns = slice(part * HEAD_SIZE, (part + 1) * HEAD_SIZE)
        high, low = query_parts(q[:, columns])
        scores, near = [], []
        for j in range(per_block):
            block = start // BLOCK + turn * per_block + j
            spots = [
                pl.ds(pl.multiple_of((block + back[head, n]) * BLOCK, BLOCK), BLOCK)
                for n in range(4)
            ]
            near.append(spots)
            keys = jnp.concatenate([near_k[s, :] for s in spots], axis=0)
            mine = slice(j * BLOCK, (j + 1) * BLOCK)
            score = fold(dot(jnp.concatenate([high[mine], low[mine]], axis=0), keys, ACROSS))
            scores.append(jnp.where(slash_pos[head, block] <= q_pos[mine], score, LOW))
        scores = jnp.concatenate(scores, axis=0)
        top = jnp.max(scores, axis=1, keepdims=True)
        weights, total = weights_of(scores, top)
        w_high, w_low = split(weights)
        parts = []
        for j in range(per_block):
            values = jnp.concatenate([near_v[s, :] for s in near[j]], axis=0)
            mine = slice(j * BLOCK, (j + 1) * BLOCK)
            stacked = jnp.concatenate([w_high[mine], w_low[mine]], axis=0)
            parts.append(fold(dot(stacked, values, DOWN)))
        mixed = jnp.concatenate(parts, axis=0)
        out[:, columns] = mixed[:, :HEAD_SIZE] + mixed[:, HEAD_SIZE:]
        known = jnp.where(lane == 2 * part, top, known)
        known = jnp.where(lane == 2 * part + 1, total, known)
    stats[...] = known


def attend_near(q, start, rows, first_row, back, wraps, arrays):
    width = q.shape[1]
    pair = 2
    count = width // (pair * HEAD_SIZE)
    base = start // TILE
    smem = pl.BlockSpec(memory_space=pltpu.SMEM)
    vmem = pl.BlockSpec(memory_space=pltpu.VMEM)
    wide = (TILE, pair * HEAD_SIZE)
    return pl.pallas_call(
        functools.partial(near_kernel, start),
        grid=(rows // TILE, count),
        out_shape=[
            jax.ShapeDtypeStruct((rows, width), jnp.float32),
            jax.ShapeDtypeStruct((rows, count * HEAD_SIZE), jnp.float32),
        ],
        in_specs=[smem, smem, smem, pl.BlockSpec(wide, lambda t, h: (base + t, h))]
        + [vmem] * len(arrays),
        out_specs=[
            pl.BlockSpec(wide, lambda t, h: (t, h)),
            pl.BlockSpec((TILE, HEAD_SIZE), lambda t, h: (t, h)),
        ],
        scratch_shapes=[pltpu.VMEM((3 * q.shape[0], 2 * HEAD_SIZE), jnp.bfloat16)] * 2,
        compiler_params=pltpu.CompilerParams(vmem_limit_bytes=24 << 20),
        cost_estimate=LARGE,
    )(first_row, back, wraps, q, *arrays)


def attend_kernel(
    start, first_row, q, near, stats, k_a, k_b, v_a, v_b, vert_pos, out, vert_k, vert_v
):
    turn = pl.program_id(0)

    @pl.when((turn == 0) & (pl.program_id(1) == 0))
    def _():
        put_parts(vert_k, 0, (k_a, k_b))
        put_parts(vert_v, 0, (v_a, v_b))

    q_pos = first_row[0] + start + turn * TILE + lax.broadcasted_iota(jnp.int32, (TILE, 1), 0)
    vert = vert_pos.shape[2]
    pair = q.shape[1] // HEAD_SIZE
    for part in range(pair):
        head = pl.program_id(1) * pair + part
        columns = slice(part * HEAD_SIZE, (part + 1) * HEAD_SIZE)
        rows = pl.ds(pl.multiple_of(head * vert, vert), vert)
        both = jnp.concatenate(list(query_parts(q[:, columns])), axis=0)
        scores = fold(dot(both, vert_k[rows, :], ACROSS))
        scores = jnp.where(vert_pos[head] <= q_pos, scores, LOW)
        near_top = stats[:, 2 * part : 2 * part + 1]
        top = jnp.maximum(jnp.max(scores, axis=1, keepdims=True), near_top)
        weights, total = weights_of(scores, top)
        keep = jnp.exp2(near_top - top)
        total = total + keep * stats[:, 2 * part + 1 : 2 * part + 2]
        mixed = fold(dot(jnp.concatenate(split(weights), axis=0), vert_v[rows, :], DOWN))
        mixed = mixed[:, :HEAD_SIZE] + mixed[:, HEAD_SIZE:] + keep * near[:, columns]
        out[0, :, columns] = mixed / total


def attend(q, near, stats, start, first_row, arrays):
    width = q.shape[1]
    heads = width // HEAD_SIZE
    pair = 2
    smem = pl.BlockSpec(memory_space=pltpu.SMEM)
    vmem = pl.BlockSpec(memory_space=pltpu.VMEM)
    base = start // TILE
    wide = (TILE, pair * HEAD_SIZE)
    return pl.pallas_call(
        functools.partial(attend_kernel, start),
        grid=(2, heads // pair),
        out_shape=jax.ShapeDtypeStruct((2, TILE, width), jnp.float32),
        in_specs=[
            smem,
            pl.BlockSpec(wide, lambda t, h: (base + t, h)),
            pl.BlockSpec(wide, lambda t, h: (base + t, h)),
            pl.BlockSpec((TILE, HEAD_SIZE), lambda t, h: (base + t, h)),
        ]
        + [vmem] * len(arrays),
        out_specs=pl.BlockSpec((1, TILE, pair * HEAD_SIZE), lambda t, h: (t, 0, h)),
        scratch_shapes=[pltpu.VMEM((heads * 8 * BLOCK, 2 * HEAD_SIZE), jnp.bfloat16)] * 2,
        compiler_params=pltpu.CompilerParams(vmem_limit_bytes=20 << 20),
        cost_estimate=LARGE,
    )(first_row, q, near, stats, *arrays)


def take_kernel(chips, one, two, three, near, far):
    width = one.shape[1]
    near[:, :width], near[:, width:] = one[...], two[...]
    far[:, :width], far[:, width:] = three[...], two[...]


def take_columns(weight, chips, width):
    rows = weight.shape[0]
    step = rows // 8
    out = jax.ShapeDtypeStruct((rows, 2 * width), jnp.float32)
    out_spec = pl.BlockSpec((step, 2 * width), lambda i, o: (i, 0))
    w_spec = lambda at: pl.BlockSpec((step, width), lambda i, o: (i, o[at]))
    return pl.pallas_call(
        take_kernel,
        out_shape=[out, out],
        grid_spec=pltpu.PrefetchScalarGridSpec(
            num_scalar_prefetch=1,
            grid=(rows // step,),
            in_specs=[w_spec(0), w_spec(1), w_spec(2)],
            out_specs=[out_spec, out_spec],
        ),
        compiler_params=pltpu.CompilerParams(vmem_limit_bytes=58 << 20),
        cost_estimate=SMALL,
    )(chips, weight, weight, weight)


def weight_term(x, block):
    high, low = split(block)
    return fold(dot(x, high, DOWN)) + dot(x[: x.shape[0] // 2], low, DOWN)


def stack(rows):
    return jnp.concatenate(split(rows), axis=0)


def chip_kernel(order, own_a, own_b, w, out, x):
    for kind in range(2):

        @pl.when((pl.program_id(0) == kind) & (pl.program_id(1) == 0))
        def _():
            x[...] = stack(jnp.concatenate([own_a[kind], own_b[kind]], axis=0))

    out[0] = weight_term(x[...], w[...])


def project_chip(own_a, own_b, weight, order):
    _, rows, depth = own_a.shape
    width = depth
    vmem = pl.BlockSpec(memory_space=pltpu.VMEM)
    return pl.pallas_call(
        chip_kernel,
        out_shape=jax.ShapeDtypeStruct((2, 2 * rows, 2 * width), jnp.float32),
        grid_spec=pltpu.PrefetchScalarGridSpec(
            num_scalar_prefetch=1,
            grid=(2, 2),
            in_specs=[vmem, vmem, pl.BlockSpec((depth, width), lambda k, j, o: (0, o[2 * k + j]))],
            out_specs=pl.BlockSpec((1, 2 * rows, width), lambda k, j, o: (k, 0, j)),
            scratch_shapes=[pltpu.VMEM((4 * rows, depth), jnp.bfloat16)],
        ),
        compiler_params=pltpu.CompilerParams(vmem_limit_bytes=20 << 20),
        cost_estimate=LARGE,
    )(order, own_a, own_b, weight)


def pair_kernel(cores, got_a, got_b, near, far, total, there, here, x):
    for kind, (got, weight) in enumerate(((got_a, near), (got_b, far))):

        @pl.when((pl.program_id(0) == kind) & (pl.program_id(1) == 0))
        def _():
            x[...] = stack(got[...])

        for side, out in enumerate((there, here)):

            @pl.when((pl.program_id(0) == kind) & (pl.program_id(1) == side))
            def _():
                out[0] = total[0] + weight_term(x[...], weight[...])


def project_pair(got, near, far, total, unit, keep, cores):
    rows, depth = got[0].shape
    width = depth
    base = 0 if keep else 2
    vmem = pl.BlockSpec(memory_space=pltpu.VMEM)
    out = jax.ShapeDtypeStruct((2, rows, width), jnp.float32)
    out_spec = pl.BlockSpec((1, rows, width), lambda k, s, c: (k, 0, 0))
    w_spec = lambda side: pl.BlockSpec(
        (depth, width), lambda k, s, c: (0, base + c[side(k, s)])
    )
    return pl.pallas_call(
        pair_kernel,
        out_shape=[out, out],
        grid_spec=pltpu.PrefetchScalarGridSpec(
            num_scalar_prefetch=1,
            grid=(2, 2),
            in_specs=[
                vmem,
                vmem,
                w_spec(lambda k, s: jnp.where(k == 0, s, 1)),
                w_spec(lambda k, s: jnp.where(k == 0, 0, s)),
                pl.BlockSpec((1, rows, width), lambda k, s, c: (k, unit, s)),
            ],
            out_specs=[out_spec, out_spec],
            scratch_shapes=[pltpu.VMEM((2 * rows, depth), jnp.bfloat16)],
        ),
        compiler_params=pltpu.CompilerParams(vmem_limit_bytes=16 << 20),
        cost_estimate=LARGE,
    )(cores, *got, near, far, total)


def body(
    queries, key_rows, value_vectors, vertical_blocks, slash_offsets, prompt_length, out_weight
):
    rows = queries.shape[0]
    blocks = rows // BLOCK
    heads = queries.shape[1] // HEAD_SIZE
    seq_index = lax.axis_index("seq")
    head_index = lax.axis_index("head")
    head_size = lax.axis_size("head")
    core = head_index % 2
    chips = head_size // 2

    x, z = seq_index % 4, seq_index // 4
    ids = range(lax.axis_size("seq"))
    right = [(i, i // 4 * 4 + (i + 1) % 4) for i in ids]
    left = [(i, i // 4 * 4 + (i + 3) % 4) for i in ids]
    over = [(i, i // 4 * 4 + (i + 2) % 4) for i in ids]
    up = [(i, (i + 4) % 16) for i in ids]
    down = [(i, (i + 12) % 16) for i in ids]
    send = lambda a, pairs: lax.ppermute(a, "seq", pairs)
    swapped = lambda a, bits: send(a, [(i, i ^ bits) for i in ids])

    k_left = send(key_rows, right)
    k_right = send(key_rows, left)
    v_below = send(value_vectors, up)

    y = head_index // 2
    over_head = lambda a, bits: lax.ppermute(a, "head", [(i, i ^ bits) for i in range(head_size)])
    width = out_weight.shape[1] // head_size
    near_weight, far_weight = take_columns(out_weight, y ^ jnp.arange(1, 4), 2 * width)
    near_weight, far_weight = over_head(near_weight, 2), over_head(far_weight, 6)

    vert = lax.dynamic_slice_in_dim(vertical_blocks, head_index * heads, heads, 0)
    slash = lax.dynamic_slice_in_dim(slash_offsets, head_index * heads, heads, 0)
    prompt = prompt_length[0]
    named = vert.reshape(-1)
    inside = jnp.arange(BLOCK, dtype=jnp.int32)
    vert_pos = vert[:, :, None] * BLOCK + inside
    vert_pos = jnp.where(vert_pos < prompt, -1, vert_pos).reshape(heads, 1, -1)
    offsets = jnp.concatenate([jnp.zeros((heads, 1), jnp.int32), slash + 1], axis=1)
    block_ids = seq_index * blocks + jnp.arange(blocks, dtype=jnp.int32)
    slash_block = block_ids[None, :, None] - offsets[:, None, :]
    repeated = jnp.any(slash_block[:, :, :, None] == vert[:, None, None, :], axis=-1)
    usable = (slash_block >= 0) & jnp.logical_not(repeated)
    slash_pos = slash_block[..., None] * BLOCK + inside
    slash_pos = jnp.where(slash_pos < prompt, -1, slash_pos)
    slash_pos = jnp.where(usable[..., None], slash_pos, FAR).reshape(heads, blocks, 1, -1)
    first_row = (seq_index * rows).reshape(1)
    back = 2 * blocks - offsets
    wraps = jnp.stack([x < 2, x == 0]).astype(jnp.int32)
    cores = jnp.stack([1 - core, core])
    pass_order = jnp.concatenate([2 * chip + cores for chip in (y ^ 3, y ^ 1)])
    keep_order = jnp.concatenate([2 * y + cores] * 2)
    owner = named // blocks
    at = named % blocks
    k_place, k_held = (owner % 4 - x) % 4 * blocks + at, (owner // 4 == z).astype(jnp.int32)
    v_place, v_held = (owner // 4 - z) % 4 * blocks + at, (owner % 4 == x).astype(jnp.int32)
    orders = (pass_order, keep_order, cores)
    small = (vert_pos, slash_pos, first_row, back, wraps, orders, k_place, k_held, v_place, v_held)

    k_left, late_values = lax.optimization_barrier((k_left, value_vectors))
    v_above = send(late_values, down)
    (k_left, k_right, v_below), small = lax.optimization_barrier(
        ((k_left, k_right, v_below), small)
    )
    vert_pos, slash_pos, first_row, back, wraps, orders, k_place, k_held, v_place, v_held = small
    half = rows // 2
    source = jnp.where(x >= 2, v_below, value_vectors)
    v_left = jnp.where(x == 3, v_below, value_vectors)
    moved_left = send(jnp.concatenate([k_right, source[half:]]), left)
    v_beyond = send(v_above, down)
    moved_right = send(jnp.concatenate([v_left, source[:half]]), right)
    k_left_wrap = send(k_left, [(i, i + 4) for i in ids if i % 4 == 0 and i + 4 in ids])
    moved_left, v_beyond, moved_right, k_left_wrap = lax.optimization_barrier(
        (moved_left, v_beyond, moved_right, k_left_wrap)
    )
    k_far, v_far_b = moved_left[:rows], moved_left[rows:]
    v_left, v_far_a = moved_right[:rows], moved_right[rows:]

    k_pieces = (key_rows, k_right, k_far, k_left)
    v_pieces = (value_vectors, v_above, v_beyond, v_below)
    named = pick_blocks(k_place, k_held, v_place, v_held, k_pieces, v_pieces)
    v_far_a = send(v_far_a, right)
    v_far_b = send(v_far_b, left)
    k_far_wrap = send(k_far, [(i, i + 4) for i in ids if i % 4 < 2 and i + 4 in ids])
    one, two = (4, 12, 1, 3), (12, 4, 3, 1)
    more = [swapped(a, bits) for a, bits in zip(named, one)]
    q = scaled(queries)
    q, v_far_a, v_far_b, k_far_wrap, *more = lax.optimization_barrier(
        (q, v_far_a, v_far_b, k_far_wrap, *more)
    )
    named = [a + b for a, b in zip(named, more)]
    arrays = (k_far, k_far_wrap, k_left, k_left_wrap, key_rows, v_far_a, v_far_b, v_left)
    near_arrays = (*arrays, value_vectors, slash_pos)
    near = attend_near(q, 0, rows, first_row, back, wraps, near_arrays)
    more = [swapped(a, bits) for a, bits in zip(named, two)]
    near, more = lax.optimization_barrier((near, more))
    arrays = (*(a + b for a, b in zip(named, more)), vert_pos)

    pass_order, keep_order, cores = orders
    meet, end = (2, 6), (6, 2)
    own_a = attend(q, *near, 0, first_row, arrays)
    q, own_a = lax.optimization_barrier((q, own_a))
    meeting = lambda parts: [over_head(parts[i], bits) for i, bits in enumerate(meet)]
    ending = lambda parts: [over_head(parts[i], bits) for i, bits in enumerate(end)]
    got_a = meeting(own_a)
    own_b = attend(q, *near, half, first_row, arrays)
    got_b = meeting(own_b)
    own_b, near_weight, far_weight = lax.optimization_barrier((own_b, near_weight, far_weight))
    total = project_chip(own_a, own_b, out_weight, pass_order)
    total, got_a = lax.optimization_barrier((total, got_a))
    product = lambda got, total, unit, keep: project_pair(
        got, near_weight, far_weight, total, unit, keep, cores
    )
    there_a, here_a = product(got_a, total, 0, False)
    there_a, here_a, got_a, got_b = lax.optimization_barrier((there_a, here_a, got_a, got_b))
    moved_a = over_head(there_a, 1)
    there_b, here_b = product(got_b, total, 1, False)
    there_b, here_b, moved_a = lax.optimization_barrier((there_b, here_b, moved_a))
    here = jnp.concatenate([here_a, here_b], axis=1)
    passed = here + jnp.concatenate([moved_a, over_head(there_b, 1)], axis=1)
    passed = [passed[0], passed[1]]
    passed, got_a, got_b, own_b = lax.optimization_barrier((passed, got_a, got_b, own_b))
    sent = ending(passed)
    kept_total = project_chip(own_a, own_b, out_weight, keep_order)
    keep_a = product(got_a, kept_total, 0, True)
    keep_b = product(got_b, kept_total, 1, True)
    keep_a, keep_b, sent = lax.optimization_barrier((keep_a, keep_b, sent))
    kept_a, kept_b = (here + over_head(there, 1) for there, here in (keep_a, keep_b))
    kept = (kept_a[0], kept_a[1], kept_b[0], kept_b[1])
    rows = kept_a.shape[1]
    sent = (sent[0][:rows], sent[1][:rows], sent[0][rows:], sent[1][rows:])
    return jnp.concatenate([a + b for a, b in zip(kept, sent)], axis=0)


def solution(mesh):
    placed = (P("seq", "head"), P("seq", "head"), P("seq", "head"), P(), P(), P(), P("head", None))
    return jax.shard_map(
        body, mesh=mesh, in_specs=placed, out_specs=P("seq", "head"), check_vma=False
    )
```

```python
import functools
import math

import jax
import jax.numpy as jnp
from jax import lax
from jax.experimental import pallas as pl
from jax.experimental.pallas import tpu as pltpu
from jax.sharding import PartitionSpec as P

HEAD_SIZE = 128
BLOCK = 64
TILE = 256
FAR = 1 << 30
LOW = -1e30
LARGE = pl.CostEstimate(flops=100000, bytes_accessed=1024, transcendentals=0)
HUGE = pl.CostEstimate(flops=6 << 30, bytes_accessed=1024, transcendentals=0)
SMALL = pl.CostEstimate(flops=1024, bytes_accessed=1024, transcendentals=0)


def pick_kernel(k_place, k_held, v_place, v_held, *refs):
    pieces, outs, rows = refs[:8], refs[8:12], refs[12:]
    size = pieces[0].shape[0]
    slots = outs[0].shape[0] // BLOCK
    for which, (place, held) in enumerate(((k_place, k_held), (v_place, v_held))):
        for at in range(4):
            rows[which][at * size : (at + 1) * size, :] = pieces[4 * which + at][...]
        for slot in range(2 * slots):
            out = outs[2 * which + slot // slots]
            target = pl.ds(slot % slots * BLOCK, BLOCK)

            @pl.when(held[slot] == 1)
            def _():
                start = pl.multiple_of(place[slot] * BLOCK, BLOCK)
                out[target, :] = rows[which][pl.ds(start, BLOCK), :]

            @pl.when(held[slot] == 0)
            def _():
                out[target, :] = jnp.zeros((BLOCK, HEAD_SIZE), jnp.float32)


def pick_blocks(k_place, k_held, v_place, v_held, k_pieces, v_pieces):
    half = k_place.shape[0] // 2 * BLOCK
    smem = pl.BlockSpec(memory_space=pltpu.SMEM)
    vmem = pl.BlockSpec(memory_space=pltpu.VMEM)
    out = jax.ShapeDtypeStruct((half, HEAD_SIZE), jnp.float32)
    size = k_pieces[0].shape[0]
    return pl.pallas_call(
        pick_kernel,
        out_shape=[out] * 4,
        in_specs=[smem] * 4 + [vmem] * 8,
        out_specs=[vmem] * 4,
        scratch_shapes=[pltpu.VMEM((4 * size, HEAD_SIZE), jnp.float32)] * 2,
        compiler_params=pltpu.CompilerParams(vmem_limit_bytes=16 << 20),
        cost_estimate=SMALL,
    )(k_place, k_held, v_place, v_held, *k_pieces, *v_pieces)


def split(x):
    high = x.astype(jnp.bfloat16)
    return high, (x - high.astype(jnp.float32)).astype(jnp.bfloat16)


def fold(x):
    half = x.shape[0] // 2
    return x[:half] + x[half:]


def put_parts(target, first, pieces):
    for piece in pieces:
        count = piece.shape[0]
        high, low = split(piece[...])
        target[first : first + count, 0:HEAD_SIZE] = high
        target[first : first + count, HEAD_SIZE:] = low
        first += count


dot = functools.partial(lax.dot_general, preferred_element_type=jnp.float32)
ACROSS = (((1,), (1,)), ((), ()))
DOWN = (((1,), (0,)), ((), ()))
SCALE = math.log2(math.e) / math.sqrt(HEAD_SIZE)


def query_parts(q):
    return (jnp.concatenate([x, x], axis=1) for x in split(q))


def scale_kernel(q, out):
    out[...] = q[...] * SCALE


def scaled(q):
    rows, width = q.shape
    spec = pl.BlockSpec((TILE, width), lambda i: (i, 0))
    return pl.pallas_call(
        scale_kernel,
        grid=(rows // TILE,),
        out_shape=jax.ShapeDtypeStruct(q.shape, jnp.float32),
        in_specs=[spec],
        out_specs=spec,
        compiler_params=pltpu.CompilerParams(vmem_limit_bytes=8 << 20),
        cost_estimate=HUGE,
    )(q)


def weights_of(scores, top):
    weights = jnp.exp2(scores - top)
    return weights, jnp.sum(weights, axis=1, keepdims=True)


def near_kernel(
    start, first_row, back, wraps, q, k_far, k_far_wrap, k_left, k_left_wrap, k_own,
    v_far_a, v_far_b, v_left, v_own, slash_pos, out, stats, near_k, near_v,
):
    turn = pl.program_id(0)

    @pl.when((turn == 0) & (pl.program_id(1) == 0))
    def _():
        rows = k_own.shape[0]
        for at, (plain, wrapped) in enumerate(((k_far, k_far_wrap), (k_left, k_left_wrap))):

            @pl.when(wraps[at] == 0)
            def _():
                put_parts(near_k, at * rows, (plain,))

            @pl.when(wraps[at] == 1)
            def _():
                put_parts(near_k, at * rows, (wrapped,))

        put_parts(near_k, 2 * rows, (k_own,))
        put_parts(near_v, 0, (v_far_a, v_far_b, v_left, v_own))

    q_pos = first_row[0] + start + turn * TILE + lax.broadcasted_iota(jnp.int32, (TILE, 1), 0)
    per_block = TILE // BLOCK
    pair = q.shape[1] // HEAD_SIZE
    lane = lax.broadcasted_iota(jnp.int32, (TILE, HEAD_SIZE), 1)
    known = jnp.zeros((TILE, HEAD_SIZE), jnp.float32)
    for part in range(pair):
        head = pl.program_id(1) * pair + part
        columns = slice(part * HEAD_SIZE, (part + 1) * HEAD_SIZE)
        high, low = query_parts(q[:, columns])
        scores, near = [], []
        for j in range(per_block):
            block = start // BLOCK + turn * per_block + j
            spots = [
                pl.ds(pl.multiple_of((block + back[head, n]) * BLOCK, BLOCK), BLOCK)
                for n in range(4)
            ]
            near.append(spots)
            keys = jnp.concatenate([near_k[s, :] for s in spots], axis=0)
            mine = slice(j * BLOCK, (j + 1) * BLOCK)
            score = fold(dot(jnp.concatenate([high[mine], low[mine]], axis=0), keys, ACROSS))
            scores.append(jnp.where(slash_pos[head, block] <= q_pos[mine], score, LOW))
        scores = jnp.concatenate(scores, axis=0)
        top = jnp.max(scores, axis=1, keepdims=True)
        weights, total = weights_of(scores, top)
        w_high, w_low = split(weights)
        parts = []
        for j in range(per_block):
            values = jnp.concatenate([near_v[s, :] for s in near[j]], axis=0)
            mine = slice(j * BLOCK, (j + 1) * BLOCK)
            stacked = jnp.concatenate([w_high[mine], w_low[mine]], axis=0)
            parts.append(fold(dot(stacked, values, DOWN)))
        mixed = jnp.concatenate(parts, axis=0)
        out[:, columns] = mixed[:, :HEAD_SIZE] + mixed[:, HEAD_SIZE:]
        known = jnp.where(lane == 2 * part, top, known)
        known = jnp.where(lane == 2 * part + 1, total, known)
    stats[...] = known


def attend_near(q, start, rows, first_row, back, wraps, arrays):
    width = q.shape[1]
    pair = 2
    count = width // (pair * HEAD_SIZE)
    base = start // TILE
    smem = pl.BlockSpec(memory_space=pltpu.SMEM)
    vmem = pl.BlockSpec(memory_space=pltpu.VMEM)
    wide = (TILE, pair * HEAD_SIZE)
    return pl.pallas_call(
        functools.partial(near_kernel, start),
        grid=(rows // TILE, count),
        out_shape=[
            jax.ShapeDtypeStruct((rows, width), jnp.float32),
            jax.ShapeDtypeStruct((rows, count * HEAD_SIZE), jnp.float32),
        ],
        in_specs=[smem, smem, smem, pl.BlockSpec(wide, lambda t, h: (base + t, h))]
        + [vmem] * len(arrays),
        out_specs=[
            pl.BlockSpec(wide, lambda t, h: (t, h)),
            pl.BlockSpec((TILE, HEAD_SIZE), lambda t, h: (t, h)),
        ],
        scratch_shapes=[pltpu.VMEM((3 * q.shape[0], 2 * HEAD_SIZE), jnp.bfloat16)] * 2,
        compiler_params=pltpu.CompilerParams(vmem_limit_bytes=24 << 20),
        cost_estimate=LARGE,
    )(first_row, back, wraps, q, *arrays)


def attend_kernel(
    start, first_row, q, near, stats, k_a, k_b, v_a, v_b, vert_pos, out, vert_k, vert_v
):
    turn = pl.program_id(0)

    @pl.when((turn == 0) & (pl.program_id(1) == 0))
    def _():
        put_parts(vert_k, 0, (k_a, k_b))
        put_parts(vert_v, 0, (v_a, v_b))

    q_pos = first_row[0] + start + turn * TILE + lax.broadcasted_iota(jnp.int32, (TILE, 1), 0)
    vert = vert_pos.shape[2]
    pair = q.shape[1] // HEAD_SIZE
    for part in range(pair):
        head = pl.program_id(1) * pair + part
        columns = slice(part * HEAD_SIZE, (part + 1) * HEAD_SIZE)
        rows = pl.ds(pl.multiple_of(head * vert, vert), vert)
        both = jnp.concatenate(list(query_parts(q[:, columns])), axis=0)
        scores = fold(dot(both, vert_k[rows, :], ACROSS))
        scores = jnp.where(vert_pos[head] <= q_pos, scores, LOW)
        near_top = stats[:, 2 * part : 2 * part + 1]
        top = jnp.maximum(jnp.max(scores, axis=1, keepdims=True), near_top)
        weights, total = weights_of(scores, top)
        keep = jnp.exp2(near_top - top)
        total = total + keep * stats[:, 2 * part + 1 : 2 * part + 2]
        mixed = fold(dot(jnp.concatenate(split(weights), axis=0), vert_v[rows, :], DOWN))
        mixed = mixed[:, :HEAD_SIZE] + mixed[:, HEAD_SIZE:] + keep * near[:, columns]
        out[0, :, columns] = mixed / total


def attend(q, near, stats, start, first_row, arrays):
    width = q.shape[1]
    heads = width // HEAD_SIZE
    pair = 2
    smem = pl.BlockSpec(memory_space=pltpu.SMEM)
    vmem = pl.BlockSpec(memory_space=pltpu.VMEM)
    base = start // TILE
    wide = (TILE, pair * HEAD_SIZE)
    return pl.pallas_call(
        functools.partial(attend_kernel, start),
        grid=(2, heads // pair),
        out_shape=jax.ShapeDtypeStruct((2, TILE, width), jnp.float32),
        in_specs=[
            smem,
            pl.BlockSpec(wide, lambda t, h: (base + t, h)),
            pl.BlockSpec(wide, lambda t, h: (base + t, h)),
            pl.BlockSpec((TILE, HEAD_SIZE), lambda t, h: (base + t, h)),
        ]
        + [vmem] * len(arrays),
        out_specs=pl.BlockSpec((1, TILE, pair * HEAD_SIZE), lambda t, h: (t, 0, h)),
        scratch_shapes=[pltpu.VMEM((heads * 8 * BLOCK, 2 * HEAD_SIZE), jnp.bfloat16)] * 2,
        compiler_params=pltpu.CompilerParams(vmem_limit_bytes=20 << 20),
        cost_estimate=LARGE,
    )(first_row, q, near, stats, *arrays)


def take_kernel(chips, one, two, three, near, far):
    width = one.shape[1]
    near[:, :width], near[:, width:] = one[...], two[...]
    far[:, :width], far[:, width:] = three[...], two[...]


def take_columns(weight, chips, width):
    rows = weight.shape[0]
    step = rows // 8
    out = jax.ShapeDtypeStruct((rows, 2 * width), jnp.float32)
    out_spec = pl.BlockSpec((step, 2 * width), lambda i, o: (i, 0))
    w_spec = lambda at: pl.BlockSpec((step, width), lambda i, o: (i, o[at]))
    return pl.pallas_call(
        take_kernel,
        out_shape=[out, out],
        grid_spec=pltpu.PrefetchScalarGridSpec(
            num_scalar_prefetch=1,
            grid=(rows // step,),
            in_specs=[w_spec(0), w_spec(1), w_spec(2)],
            out_specs=[out_spec, out_spec],
        ),
        compiler_params=pltpu.CompilerParams(vmem_limit_bytes=58 << 20),
        cost_estimate=SMALL,
    )(chips, weight, weight, weight)


def weight_term(x, block):
    high, low = split(block)
    return fold(dot(x, high, DOWN)) + dot(x[: x.shape[0] // 2], low, DOWN)


def stack(rows):
    return jnp.concatenate(split(rows), axis=0)


def chip_kernel(order, own_a, own_b, w, out, x):
    for kind in range(2):

        @pl.when((pl.program_id(0) == kind) & (pl.program_id(1) == 0))
        def _():
            x[...] = stack(jnp.concatenate([own_a[kind], own_b[kind]], axis=0))

    out[0] = weight_term(x[...], w[...])


def project_chip(own_a, own_b, weight, order):
    _, rows, depth = own_a.shape
    width = depth
    vmem = pl.BlockSpec(memory_space=pltpu.VMEM)
    return pl.pallas_call(
        chip_kernel,
        out_shape=jax.ShapeDtypeStruct((2, 2 * rows, 2 * width), jnp.float32),
        grid_spec=pltpu.PrefetchScalarGridSpec(
            num_scalar_prefetch=1,
            grid=(2, 2),
            in_specs=[vmem, vmem, pl.BlockSpec((depth, width), lambda k, j, o: (0, o[2 * k + j]))],
            out_specs=pl.BlockSpec((1, 2 * rows, width), lambda k, j, o: (k, 0, j)),
            scratch_shapes=[pltpu.VMEM((4 * rows, depth), jnp.bfloat16)],
        ),
        compiler_params=pltpu.CompilerParams(vmem_limit_bytes=20 << 20),
        cost_estimate=LARGE,
    )(order, own_a, own_b, weight)


def pair_kernel(cores, got_a, got_b, near, far, total, *refs):
    *there, here, x = refs
    width = here.shape[2] * 2 // len(there)
    for kind, (got, weight) in enumerate(((got_a, near), (got_b, far))):

        @pl.when((pl.program_id(0) == kind) & (pl.program_id(1) == 0))
        def _():
            x[...] = stack(got[...])

        @pl.when((pl.program_id(0) == kind) & (pl.program_id(1) == 0))
        def _():
            term = total[0] + weight_term(x[...], weight[...])
            mine = there[kind * len(there) // 2 : (kind + 1) * len(there) // 2]
            for at, out in enumerate(mine):
                out[...] = term[:, at * width : (at + 1) * width]

        @pl.when((pl.program_id(0) == kind) & (pl.program_id(1) == 1))
        def _():
            here[0] = total[0] + weight_term(x[...], weight[...])


def project_pair(got, near, far, total, unit, keep, cores):
    rows, depth = got[0].shape
    width = depth
    base = 0 if keep else 2
    vmem = pl.BlockSpec(memory_space=pltpu.VMEM)
    pieces = 4 if keep else 2
    here = jax.ShapeDtypeStruct((2, rows, width), jnp.float32)
    there = jax.ShapeDtypeStruct((rows, 2 * width // pieces), jnp.float32)
    w_spec = lambda side: pl.BlockSpec(
        (depth, width), lambda k, s, c: (0, base + c[side(k, s)])
    )
    *there, here = pl.pallas_call(
        pair_kernel,
        out_shape=[there] * pieces + [here],
        grid_spec=pltpu.PrefetchScalarGridSpec(
            num_scalar_prefetch=1,
            grid=(2, 2),
            in_specs=[
                vmem,
                vmem,
                w_spec(lambda k, s: jnp.where(k == 0, s, 1)),
                w_spec(lambda k, s: jnp.where(k == 0, 0, s)),
                pl.BlockSpec((1, rows, width), lambda k, s, c: (k, unit, s)),
            ],
            out_specs=[pl.BlockSpec(there.shape, lambda k, s, c: (0, 0))] * pieces
            + [pl.BlockSpec((1, rows, width), lambda k, s, c: (k, 0, 0))],
            scratch_shapes=[pltpu.VMEM((2 * rows, depth), jnp.bfloat16)],
        ),
        compiler_params=pltpu.CompilerParams(vmem_limit_bytes=16 << 20),
        cost_estimate=LARGE,
    )(cores, *got, near, far, total)
    return there, here


def body(
    queries, key_rows, value_vectors, vertical_blocks, slash_offsets, prompt_length, out_weight
):
    rows = queries.shape[0]
    blocks = rows // BLOCK
    heads = queries.shape[1] // HEAD_SIZE
    seq_index = lax.axis_index("seq")
    head_index = lax.axis_index("head")
    head_size = lax.axis_size("head")
    core = head_index % 2
    chips = head_size // 2

    x, z = seq_index % 4, seq_index // 4
    ids = range(lax.axis_size("seq"))
    right = [(i, i // 4 * 4 + (i + 1) % 4) for i in ids]
    left = [(i, i // 4 * 4 + (i + 3) % 4) for i in ids]
    over = [(i, i // 4 * 4 + (i + 2) % 4) for i in ids]
    up = [(i, (i + 4) % 16) for i in ids]
    down = [(i, (i + 12) % 16) for i in ids]
    send = lambda a, pairs: lax.ppermute(a, "seq", pairs)
    swapped = lambda a, bits: send(a, [(i, i ^ bits) for i in ids])

    k_left = send(key_rows, right)
    k_right = send(key_rows, left)
    v_below = send(value_vectors, up)

    y = head_index // 2
    over_head = lambda a, bits: lax.ppermute(a, "head", [(i, i ^ bits) for i in range(head_size)])
    width = out_weight.shape[1] // head_size
    near_weight, far_weight = take_columns(out_weight, y ^ jnp.arange(1, 4), 2 * width)
    near_weight, far_weight = over_head(near_weight, 2), over_head(far_weight, 6)

    vert = lax.dynamic_slice_in_dim(vertical_blocks, head_index * heads, heads, 0)
    slash = lax.dynamic_slice_in_dim(slash_offsets, head_index * heads, heads, 0)
    prompt = prompt_length[0]
    named = vert.reshape(-1)
    inside = jnp.arange(BLOCK, dtype=jnp.int32)
    vert_pos = vert[:, :, None] * BLOCK + inside
    vert_pos = jnp.where(vert_pos < prompt, -1, vert_pos).reshape(heads, 1, -1)
    offsets = jnp.concatenate([jnp.zeros((heads, 1), jnp.int32), slash + 1], axis=1)
    block_ids = seq_index * blocks + jnp.arange(blocks, dtype=jnp.int32)
    slash_block = block_ids[None, :, None] - offsets[:, None, :]
    repeated = jnp.any(slash_block[:, :, :, None] == vert[:, None, None, :], axis=-1)
    usable = (slash_block >= 0) & jnp.logical_not(repeated)
    slash_pos = slash_block[..., None] * BLOCK + inside
    slash_pos = jnp.where(slash_pos < prompt, -1, slash_pos)
    slash_pos = jnp.where(usable[..., None], slash_pos, FAR).reshape(heads, blocks, 1, -1)
    first_row = (seq_index * rows).reshape(1)
    back = 2 * blocks - offsets
    wraps = jnp.stack([x < 2, x == 0]).astype(jnp.int32)
    cores = jnp.stack([1 - core, core])
    pass_order = jnp.concatenate([2 * chip + cores for chip in (y ^ 3, y ^ 1)])
    keep_order = jnp.concatenate([2 * y + cores] * 2)
    owner = named // blocks
    at = named % blocks
    k_place, k_held = (owner % 4 - x) % 4 * blocks + at, (owner // 4 == z).astype(jnp.int32)
    v_place, v_held = (owner // 4 - z) % 4 * blocks + at, (owner % 4 == x).astype(jnp.int32)
    orders = (pass_order, keep_order, cores)
    small = (vert_pos, slash_pos, first_row, back, wraps, orders, k_place, k_held, v_place, v_held)

    k_left, late_values = lax.optimization_barrier((k_left, value_vectors))
    v_above = send(late_values, down)
    (k_left, k_right, v_below), small = lax.optimization_barrier(
        ((k_left, k_right, v_below), small)
    )
    vert_pos, slash_pos, first_row, back, wraps, orders, k_place, k_held, v_place, v_held = small
    half = rows // 2
    source = jnp.where(x >= 2, v_below, value_vectors)
    v_left = jnp.where(x == 3, v_below, value_vectors)
    moved_left = send(jnp.concatenate([k_right, source[half:]]), left)
    v_beyond = send(v_above, down)
    moved_right = send(jnp.concatenate([v_left, source[:half]]), right)
    k_left_wrap = send(k_left, [(i, i + 4) for i in ids if i % 4 == 0 and i + 4 in ids])
    moved_left, v_beyond, moved_right, k_left_wrap = lax.optimization_barrier(
        (moved_left, v_beyond, moved_right, k_left_wrap)
    )
    k_far, v_far_b = moved_left[:rows], moved_left[rows:]
    v_left, v_far_a = moved_right[:rows], moved_right[rows:]

    k_pieces = (key_rows, k_right, k_far, k_left)
    v_pieces = (value_vectors, v_above, v_beyond, v_below)
    named = pick_blocks(k_place, k_held, v_place, v_held, k_pieces, v_pieces)
    v_far_a = send(v_far_a, right)
    v_far_b = send(v_far_b, left)
    k_far_wrap = send(k_far, [(i, i + 4) for i in ids if i % 4 < 2 and i + 4 in ids])
    one, two = (4, 12, 1, 3), (12, 4, 3, 1)
    more = [swapped(a, bits) for a, bits in zip(named, one)]
    q = scaled(queries)
    q, v_far_a, v_far_b, k_far_wrap, *more = lax.optimization_barrier(
        (q, v_far_a, v_far_b, k_far_wrap, *more)
    )
    named = [a + b for a, b in zip(named, more)]
    arrays = (k_far, k_far_wrap, k_left, k_left_wrap, key_rows, v_far_a, v_far_b, v_left)
    near_arrays = (*arrays, value_vectors, slash_pos)
    near = attend_near(q, 0, rows, first_row, back, wraps, near_arrays)
    more = [swapped(a, bits) for a, bits in zip(named, two)]
    near, more = lax.optimization_barrier((near, more))
    arrays = (*(a + b for a, b in zip(named, more)), vert_pos)

    pass_order, keep_order, cores = orders
    meet, end = (2, 6), (6, 2)
    own_a = attend(q, *near, 0, first_row, arrays)
    q, own_a = lax.optimization_barrier((q, own_a))
    meeting = lambda parts: [over_head(parts[i], bits) for i, bits in enumerate(meet)]
    ending = lambda parts: [over_head(parts[i], bits) for i, bits in enumerate(end)]
    got_a = meeting(own_a)
    own_b = attend(q, *near, half, first_row, arrays)
    got_b = meeting(own_b)
    own_b, near_weight, far_weight = lax.optimization_barrier((own_b, near_weight, far_weight))
    total = project_chip(own_a, own_b, out_weight, pass_order)
    total, got_a = lax.optimization_barrier((total, got_a))
    product = lambda got, total, unit, keep: project_pair(
        got, near_weight, far_weight, total, unit, keep, cores
    )
    there_a, here_a = product(got_a, total, 0, False)
    there_a, here_a, got_a, got_b = lax.optimization_barrier((there_a, here_a, got_a, got_b))
    across = lambda parts: [over_head(a, 1) for a in parts]
    moved_a = across(there_a)
    there_b, here_b = product(got_b, total, 1, False)
    there_b, here_b, moved_a = lax.optimization_barrier((there_b, here_b, moved_a))
    moved = zip(moved_a, across(there_b))
    passed = [
        jnp.concatenate([here_a[i] + a, here_b[i] + b]) for i, (a, b) in enumerate(moved)
    ]
    passed, got_a, got_b, own_b = lax.optimization_barrier((passed, got_a, got_b, own_b))
    sent = ending(passed)
    kept_total = project_chip(own_a, own_b, out_weight, keep_order)
    keep_a = product(got_a, kept_total, 0, True)
    keep_b = product(got_b, kept_total, 1, True)
    kept = []
    for there, here in (keep_a, keep_b):
        moved = across(there)
        kept += [here[i] + jnp.concatenate(moved[2 * i : 2 * i + 2], axis=1) for i in range(2)]
    rows = kept[0].shape[0]
    sent = (sent[0][:rows], sent[1][:rows], sent[0][rows:], sent[1][rows:])
    return jnp.concatenate([a + b for a, b in zip(kept, sent)], axis=0)


def solution(mesh):
    placed = (P("seq", "head"), P("seq", "head"), P("seq", "head"), P(), P(), P(), P("head", None))
    return jax.shard_map(
        body, mesh=mesh, in_specs=placed, out_specs=P("seq", "head"), check_vma=False
    )
```

```python
import functools
import math

import jax
import jax.numpy as jnp
from jax import lax
from jax.experimental import pallas as pl
from jax.experimental.pallas import tpu as pltpu
from jax.sharding import PartitionSpec as P

HEAD_SIZE = 128
BLOCK = 64
TILE = 256
FAR = 1 << 30
LOW = -1e30
LARGE = pl.CostEstimate(flops=100000, bytes_accessed=1024, transcendentals=0)
HUGE = pl.CostEstimate(flops=6 << 30, bytes_accessed=1024, transcendentals=0)
SMALL = pl.CostEstimate(flops=1024, bytes_accessed=1024, transcendentals=0)


def pick_kernel(k_place, k_held, v_place, v_held, *refs):
    pieces, outs, rows = refs[:8], refs[8:12], refs[12:]
    size = pieces[0].shape[0]
    slots = outs[0].shape[0] // BLOCK
    for which, (place, held) in enumerate(((k_place, k_held), (v_place, v_held))):
        for at in range(4):
            rows[which][at * size : (at + 1) * size, :] = pieces[4 * which + at][...]
        for slot in range(2 * slots):
            out = outs[2 * which + slot // slots]
            target = pl.ds(slot % slots * BLOCK, BLOCK)

            @pl.when(held[slot] == 1)
            def _():
                start = pl.multiple_of(place[slot] * BLOCK, BLOCK)
                out[target, :] = rows[which][pl.ds(start, BLOCK), :]

            @pl.when(held[slot] == 0)
            def _():
                out[target, :] = jnp.zeros((BLOCK, HEAD_SIZE), jnp.float32)


def pick_blocks(k_place, k_held, v_place, v_held, k_pieces, v_pieces):
    half = k_place.shape[0] // 2 * BLOCK
    smem = pl.BlockSpec(memory_space=pltpu.SMEM)
    vmem = pl.BlockSpec(memory_space=pltpu.VMEM)
    out = jax.ShapeDtypeStruct((half, HEAD_SIZE), jnp.float32)
    size = k_pieces[0].shape[0]
    return pl.pallas_call(
        pick_kernel,
        out_shape=[out] * 4,
        in_specs=[smem] * 4 + [vmem] * 8,
        out_specs=[vmem] * 4,
        scratch_shapes=[pltpu.VMEM((4 * size, HEAD_SIZE), jnp.float32)] * 2,
        compiler_params=pltpu.CompilerParams(vmem_limit_bytes=16 << 20),
        cost_estimate=SMALL,
    )(k_place, k_held, v_place, v_held, *k_pieces, *v_pieces)


def split(x):
    high = x.astype(jnp.bfloat16)
    return high, (x - high.astype(jnp.float32)).astype(jnp.bfloat16)


def fold(x):
    half = x.shape[0] // 2
    return x[:half] + x[half:]


def put_parts(target, first, pieces):
    for piece in pieces:
        count = piece.shape[0]
        high, low = split(piece[...])
        target[first : first + count, 0:HEAD_SIZE] = high
        target[first : first + count, HEAD_SIZE:] = low
        first += count


dot = functools.partial(lax.dot_general, preferred_element_type=jnp.float32)
ACROSS = (((1,), (1,)), ((), ()))
DOWN = (((1,), (0,)), ((), ()))
SCALE = math.log2(math.e) / math.sqrt(HEAD_SIZE)


def query_parts(q):
    return (jnp.concatenate([x, x], axis=1) for x in split(q))


def scale_kernel(q, out):
    out[...] = q[...] * SCALE


def scaled(q):
    rows, width = q.shape
    spec = pl.BlockSpec((TILE, width), lambda i: (i, 0))
    return pl.pallas_call(
        scale_kernel,
        grid=(rows // TILE,),
        out_shape=jax.ShapeDtypeStruct(q.shape, jnp.float32),
        in_specs=[spec],
        out_specs=spec,
        compiler_params=pltpu.CompilerParams(vmem_limit_bytes=8 << 20),
        cost_estimate=HUGE,
    )(q)


def weights_of(scores, top):
    weights = jnp.exp2(scores - top)
    return weights, jnp.sum(weights, axis=1, keepdims=True)


def near_kernel(
    start, first_row, back, wraps, q, k_far, k_far_wrap, k_left, k_left_wrap, k_own,
    v_far_a, v_far_b, v_left, v_own, slash_pos, out, stats, near_k, near_v,
):
    turn = pl.program_id(0)

    @pl.when((turn == 0) & (pl.program_id(1) == 0))
    def _():
        rows = k_own.shape[0]
        for at, (plain, wrapped) in enumerate(((k_far, k_far_wrap), (k_left, k_left_wrap))):

            @pl.when(wraps[at] == 0)
            def _():
                put_parts(near_k, at * rows, (plain,))

            @pl.when(wraps[at] == 1)
            def _():
                put_parts(near_k, at * rows, (wrapped,))

        put_parts(near_k, 2 * rows, (k_own,))
        put_parts(near_v, 0, (v_far_a, v_far_b, v_left, v_own))

    q_pos = first_row[0] + start + turn * TILE + lax.broadcasted_iota(jnp.int32, (TILE, 1), 0)
    per_block = TILE // BLOCK
    pair = q.shape[1] // HEAD_SIZE
    lane = lax.broadcasted_iota(jnp.int32, (TILE, HEAD_SIZE), 1)
    known = jnp.zeros((TILE, HEAD_SIZE), jnp.float32)
    for part in range(pair):
        head = pl.program_id(1) * pair + part
        columns = slice(part * HEAD_SIZE, (part + 1) * HEAD_SIZE)
        high, low = query_parts(q[:, columns])
        scores, near = [], []
        for j in range(per_block):
            block = start // BLOCK + turn * per_block + j
            spots = [
                pl.ds(pl.multiple_of((block + back[head, n]) * BLOCK, BLOCK), BLOCK)
                for n in range(4)
            ]
            near.append(spots)
            keys = jnp.concatenate([near_k[s, :] for s in spots], axis=0)
            mine = slice(j * BLOCK, (j + 1) * BLOCK)
            score = fold(dot(jnp.concatenate([high[mine], low[mine]], axis=0), keys, ACROSS))
            scores.append(jnp.where(slash_pos[head, block] <= q_pos[mine], score, LOW))
        scores = jnp.concatenate(scores, axis=0)
        top = jnp.max(scores, axis=1, keepdims=True)
        weights, total = weights_of(scores, top)
        w_high, w_low = split(weights)
        parts = []
        for j in range(per_block):
            values = jnp.concatenate([near_v[s, :] for s in near[j]], axis=0)
            mine = slice(j * BLOCK, (j + 1) * BLOCK)
            stacked = jnp.concatenate([w_high[mine], w_low[mine]], axis=0)
            parts.append(fold(dot(stacked, values, DOWN)))
        mixed = jnp.concatenate(parts, axis=0)
        out[:, columns] = mixed[:, :HEAD_SIZE] + mixed[:, HEAD_SIZE:]
        known = jnp.where(lane == 2 * part, top, known)
        known = jnp.where(lane == 2 * part + 1, total, known)
    stats[...] = known


def attend_near(q, start, rows, first_row, back, wraps, arrays):
    width = q.shape[1]
    pair = 2
    count = width // (pair * HEAD_SIZE)
    base = start // TILE
    smem = pl.BlockSpec(memory_space=pltpu.SMEM)
    vmem = pl.BlockSpec(memory_space=pltpu.VMEM)
    wide = (TILE, pair * HEAD_SIZE)
    return pl.pallas_call(
        functools.partial(near_kernel, start),
        grid=(rows // TILE, count),
        out_shape=[
            jax.ShapeDtypeStruct((rows, width), jnp.float32),
            jax.ShapeDtypeStruct((rows, count * HEAD_SIZE), jnp.float32),
        ],
        in_specs=[smem, smem, smem, pl.BlockSpec(wide, lambda t, h: (base + t, h))]
        + [vmem] * len(arrays),
        out_specs=[
            pl.BlockSpec(wide, lambda t, h: (t, h)),
            pl.BlockSpec((TILE, HEAD_SIZE), lambda t, h: (t, h)),
        ],
        scratch_shapes=[pltpu.VMEM((3 * q.shape[0], 2 * HEAD_SIZE), jnp.bfloat16)] * 2,
        compiler_params=pltpu.CompilerParams(vmem_limit_bytes=24 << 20),
        cost_estimate=LARGE,
    )(first_row, back, wraps, q, *arrays)


def attend_kernel(
    start, first_row, q, near, stats, k_a, k_b, v_a, v_b, vert_pos, out, vert_k, vert_v
):
    turn = pl.program_id(0)

    @pl.when((turn == 0) & (pl.program_id(1) == 0))
    def _():
        put_parts(vert_k, 0, (k_a, k_b))
        put_parts(vert_v, 0, (v_a, v_b))

    q_pos = first_row[0] + start + turn * TILE + lax.broadcasted_iota(jnp.int32, (TILE, 1), 0)
    vert = vert_pos.shape[2]
    pair = q.shape[1] // HEAD_SIZE
    for part in range(pair):
        head = pl.program_id(1) * pair + part
        columns = slice(part * HEAD_SIZE, (part + 1) * HEAD_SIZE)
        rows = pl.ds(pl.multiple_of(head * vert, vert), vert)
        both = jnp.concatenate(list(query_parts(q[:, columns])), axis=0)
        scores = fold(dot(both, vert_k[rows, :], ACROSS))
        scores = jnp.where(vert_pos[head] <= q_pos, scores, LOW)
        near_top = stats[:, 2 * part : 2 * part + 1]
        top = jnp.maximum(jnp.max(scores, axis=1, keepdims=True), near_top)
        weights, total = weights_of(scores, top)
        keep = jnp.exp2(near_top - top)
        total = total + keep * stats[:, 2 * part + 1 : 2 * part + 2]
        mixed = fold(dot(jnp.concatenate(split(weights), axis=0), vert_v[rows, :], DOWN))
        mixed = mixed[:, :HEAD_SIZE] + mixed[:, HEAD_SIZE:] + keep * near[:, columns]
        out[0, :, columns] = mixed / total


def attend(q, near, stats, start, first_row, arrays):
    width = q.shape[1]
    heads = width // HEAD_SIZE
    pair = 2
    smem = pl.BlockSpec(memory_space=pltpu.SMEM)
    vmem = pl.BlockSpec(memory_space=pltpu.VMEM)
    base = start // TILE
    wide = (TILE, pair * HEAD_SIZE)
    return pl.pallas_call(
        functools.partial(attend_kernel, start),
        grid=(2, heads // pair),
        out_shape=jax.ShapeDtypeStruct((2, TILE, width), jnp.float32),
        in_specs=[
            smem,
            pl.BlockSpec(wide, lambda t, h: (base + t, h)),
            pl.BlockSpec(wide, lambda t, h: (base + t, h)),
            pl.BlockSpec((TILE, HEAD_SIZE), lambda t, h: (base + t, h)),
        ]
        + [vmem] * len(arrays),
        out_specs=pl.BlockSpec((1, TILE, pair * HEAD_SIZE), lambda t, h: (t, 0, h)),
        scratch_shapes=[pltpu.VMEM((heads * 8 * BLOCK, 2 * HEAD_SIZE), jnp.bfloat16)] * 2,
        compiler_params=pltpu.CompilerParams(vmem_limit_bytes=20 << 20),
        cost_estimate=LARGE,
    )(first_row, q, near, stats, *arrays)


def take_kernel(chips, one, two, three, near, far):
    step = pl.program_id(0)

    @pl.when(step < 4)
    def _():
        near[...], far[...] = one[...], three[...]

    @pl.when(step >= 4)
    def _():
        near[...], far[...] = two[...], two[...]


def take_columns(weight, chips, width):
    rows = weight.shape[0]
    part = width // 4
    out = jax.ShapeDtypeStruct((rows, 2 * width), jnp.float32)
    out_spec = pl.BlockSpec((rows, part), lambda i, o: (0, i))
    early = lambda at: pl.BlockSpec(
        (rows, part), lambda i, o: (0, 4 * o[at] + jnp.minimum(i, 3))
    )
    late = pl.BlockSpec((rows, part), lambda i, o: (0, 4 * o[1] + jnp.maximum(i - 4, 0)))
    return pl.pallas_call(
        take_kernel,
        out_shape=[out, out],
        grid_spec=pltpu.PrefetchScalarGridSpec(
            num_scalar_prefetch=1,
            grid=(8,),
            in_specs=[early(0), late, early(2)],
            out_specs=[out_spec, out_spec],
        ),
        compiler_params=pltpu.CompilerParams(vmem_limit_bytes=58 << 20),
        cost_estimate=SMALL,
    )(chips, weight, weight, weight)


def weight_term(x, block):
    high, low = split(block)
    return fold(dot(x, high, DOWN)) + dot(x[: x.shape[0] // 2], low, DOWN)


def stack(rows):
    return jnp.concatenate(split(rows), axis=0)


def chip_kernel(order, own_a, own_b, w, out, x):
    for kind in range(2):

        @pl.when((pl.program_id(0) == kind) & (pl.program_id(1) == 0))
        def _():
            x[...] = stack(jnp.concatenate([own_a[kind], own_b[kind]], axis=0))

    out[0] = weight_term(x[...], w[...])


def project_chip(own_a, own_b, weight, order):
    _, rows, depth = own_a.shape
    width = depth
    vmem = pl.BlockSpec(memory_space=pltpu.VMEM)
    return pl.pallas_call(
        chip_kernel,
        out_shape=jax.ShapeDtypeStruct((2, 2 * rows, 2 * width), jnp.float32),
        grid_spec=pltpu.PrefetchScalarGridSpec(
            num_scalar_prefetch=1,
            grid=(2, 2),
            in_specs=[vmem, vmem, pl.BlockSpec((depth, width), lambda k, j, o: (0, o[2 * k + j]))],
            out_specs=pl.BlockSpec((1, 2 * rows, width), lambda k, j, o: (k, 0, j)),
            scratch_shapes=[pltpu.VMEM((4 * rows, depth), jnp.bfloat16)],
        ),
        compiler_params=pltpu.CompilerParams(vmem_limit_bytes=20 << 20),
        cost_estimate=LARGE,
    )(order, own_a, own_b, weight)


def pair_kernel(cores, got_a, got_b, near, far, total, *refs):
    *there, here, x = refs
    width = here.shape[2] * 2 // len(there)
    for kind, (got, weight) in enumerate(((got_a, near), (got_b, far))):

        @pl.when((pl.program_id(0) == kind) & (pl.program_id(1) == 0))
        def _():
            x[...] = stack(got[...])

        @pl.when((pl.program_id(0) == kind) & (pl.program_id(1) == 0))
        def _():
            term = total[0] + weight_term(x[...], weight[...])
            mine = there[kind * len(there) // 2 : (kind + 1) * len(there) // 2]
            for at, out in enumerate(mine):
                out[...] = term[:, at * width : (at + 1) * width]

        @pl.when((pl.program_id(0) == kind) & (pl.program_id(1) == 1))
        def _():
            here[0] = total[0] + weight_term(x[...], weight[...])


def project_pair(got, near, far, total, unit, keep, cores):
    rows, depth = got[0].shape
    width = depth
    base = 0 if keep else 2
    vmem = pl.BlockSpec(memory_space=pltpu.VMEM)
    pieces = 4 if keep else 2
    here = jax.ShapeDtypeStruct((2, rows, width), jnp.float32)
    there = jax.ShapeDtypeStruct((rows, 2 * width // pieces), jnp.float32)
    w_spec = lambda side: pl.BlockSpec(
        (depth, width), lambda k, s, c: (0, base + c[side(k, s)])
    )
    *there, here = pl.pallas_call(
        pair_kernel,
        out_shape=[there] * pieces + [here],
        grid_spec=pltpu.PrefetchScalarGridSpec(
            num_scalar_prefetch=1,
            grid=(2, 2),
            in_specs=[
                vmem,
                vmem,
                w_spec(lambda k, s: jnp.where(k == 0, s, 1)),
                w_spec(lambda k, s: jnp.where(k == 0, 0, s)),
                pl.BlockSpec((1, rows, width), lambda k, s, c: (k, unit, s)),
            ],
            out_specs=[pl.BlockSpec(there.shape, lambda k, s, c: (0, 0))] * pieces
            + [pl.BlockSpec((1, rows, width), lambda k, s, c: (k, 0, 0))],
            scratch_shapes=[pltpu.VMEM((2 * rows, depth), jnp.bfloat16)],
        ),
        compiler_params=pltpu.CompilerParams(vmem_limit_bytes=16 << 20),
        cost_estimate=LARGE,
    )(cores, *got, near, far, total)
    return there, here


def body(
    queries, key_rows, value_vectors, vertical_blocks, slash_offsets, prompt_length, out_weight
):
    rows = queries.shape[0]
    blocks = rows // BLOCK
    heads = queries.shape[1] // HEAD_SIZE
    seq_index = lax.axis_index("seq")
    head_index = lax.axis_index("head")
    head_size = lax.axis_size("head")
    core = head_index % 2
    chips = head_size // 2

    x, z = seq_index % 4, seq_index // 4
    ids = range(lax.axis_size("seq"))
    right = [(i, i // 4 * 4 + (i + 1) % 4) for i in ids]
    left = [(i, i // 4 * 4 + (i + 3) % 4) for i in ids]
    over = [(i, i // 4 * 4 + (i + 2) % 4) for i in ids]
    up = [(i, (i + 4) % 16) for i in ids]
    down = [(i, (i + 12) % 16) for i in ids]
    send = lambda a, pairs: lax.ppermute(a, "seq", pairs)
    swapped = lambda a, bits: send(a, [(i, i ^ bits) for i in ids])

    k_left = send(key_rows, right)
    k_right = send(key_rows, left)
    v_below = send(value_vectors, up)

    y = head_index // 2
    over_head = lambda a, bits: lax.ppermute(a, "head", [(i, i ^ bits) for i in range(head_size)])
    width = out_weight.shape[1] // head_size
    near_weight, far_weight = take_columns(out_weight, y ^ jnp.arange(1, 4), 2 * width)
    near_weight, far_weight = over_head(near_weight, 2), over_head(far_weight, 6)

    (k_left, late_values), (vertical_blocks, slash_offsets, prompt_length) = (
        lax.optimization_barrier(
            ((k_left, value_vectors), (vertical_blocks, slash_offsets, prompt_length))
        )
    )
    v_above = send(late_values, down)
    vert = lax.dynamic_slice_in_dim(vertical_blocks, head_index * heads, heads, 0)
    slash = lax.dynamic_slice_in_dim(slash_offsets, head_index * heads, heads, 0)
    prompt = prompt_length[0]
    named = vert.reshape(-1)
    inside = jnp.arange(BLOCK, dtype=jnp.int32)
    vert_pos = vert[:, :, None] * BLOCK + inside
    vert_pos = jnp.where(vert_pos < prompt, -1, vert_pos).reshape(heads, 1, -1)
    offsets = jnp.concatenate([jnp.zeros((heads, 1), jnp.int32), slash + 1], axis=1)
    block_ids = seq_index * blocks + jnp.arange(blocks, dtype=jnp.int32)
    slash_block = block_ids[None, :, None] - offsets[:, None, :]
    repeated = jnp.any(slash_block[:, :, :, None] == vert[:, None, None, :], axis=-1)
    usable = (slash_block >= 0) & jnp.logical_not(repeated)
    slash_pos = slash_block[..., None] * BLOCK + inside
    slash_pos = jnp.where(slash_pos < prompt, -1, slash_pos)
    slash_pos = jnp.where(usable[..., None], slash_pos, FAR).reshape(heads, blocks, 1, -1)
    first_row = (seq_index * rows).reshape(1)
    back = 2 * blocks - offsets
    wraps = jnp.stack([x < 2, x == 0]).astype(jnp.int32)
    cores = jnp.stack([1 - core, core])
    pass_order = jnp.concatenate([2 * chip + cores for chip in (y ^ 3, y ^ 1)])
    keep_order = jnp.concatenate([2 * y + cores] * 2)
    owner = named // blocks
    at = named % blocks
    k_place, k_held = (owner % 4 - x) % 4 * blocks + at, (owner // 4 == z).astype(jnp.int32)
    v_place, v_held = (owner // 4 - z) % 4 * blocks + at, (owner % 4 == x).astype(jnp.int32)
    orders = (pass_order, keep_order, cores)
    small = (vert_pos, slash_pos, first_row, back, wraps, orders, k_place, k_held, v_place, v_held)

    half = rows // 2
    source = jnp.where(x >= 2, v_below, value_vectors)
    v_left = jnp.where(x == 3, v_below, value_vectors)
    moved_left = send(jnp.concatenate([k_right, source[half:]]), left)
    v_beyond = send(v_above, down)
    moved_right = send(jnp.concatenate([v_left, source[:half]]), right)
    k_left_wrap = send(k_left, [(i, i + 4) for i in ids if i % 4 == 0 and i + 4 in ids])
    (moved_left, v_beyond, moved_right, k_left_wrap), small = lax.optimization_barrier(
        ((moved_left, v_beyond, moved_right, k_left_wrap), small)
    )
    vert_pos, slash_pos, first_row, back, wraps, orders, k_place, k_held, v_place, v_held = small
    k_far, v_far_b = moved_left[:rows], moved_left[rows:]
    v_left, v_far_a = moved_right[:rows], moved_right[rows:]

    k_pieces = (key_rows, k_right, k_far, k_left)
    v_pieces = (value_vectors, v_above, v_beyond, v_below)
    named = pick_blocks(k_place, k_held, v_place, v_held, k_pieces, v_pieces)
    v_far_a = send(v_far_a, right)
    v_far_b = send(v_far_b, left)
    k_far_wrap = send(k_far, [(i, i + 4) for i in ids if i % 4 < 2 and i + 4 in ids])
    one, two = (4, 12, 1, 3), (12, 4, 3, 1)
    more = [swapped(a, bits) for a, bits in zip(named, one)]
    q = scaled(queries)
    q, v_far_a, v_far_b, k_far_wrap, *more = lax.optimization_barrier(
        (q, v_far_a, v_far_b, k_far_wrap, *more)
    )
    named = [a + b for a, b in zip(named, more)]
    arrays = (k_far, k_far_wrap, k_left, k_left_wrap, key_rows, v_far_a, v_far_b, v_left)
    near_arrays = (*arrays, value_vectors, slash_pos)
    near = attend_near(q, 0, rows, first_row, back, wraps, near_arrays)
    more = [swapped(a, bits) for a, bits in zip(named, two)]
    near, more = lax.optimization_barrier((near, more))
    arrays = (*(a + b for a, b in zip(named, more)), vert_pos)

    pass_order, keep_order, cores = orders
    meet, end = (2, 6), (6, 2)
    own_a = attend(q, *near, 0, first_row, arrays)
    q, own_a = lax.optimization_barrier((q, own_a))
    meeting = lambda parts: [over_head(parts[i], bits) for i, bits in enumerate(meet)]
    ending = lambda parts: [over_head(parts[i], bits) for i, bits in enumerate(end)]
    got_a = meeting(own_a)
    own_b = attend(q, *near, half, first_row, arrays)
    got_b = meeting(own_b)
    own_b, near_weight, far_weight = lax.optimization_barrier((own_b, near_weight, far_weight))
    total = project_chip(own_a, own_b, out_weight, pass_order)
    total, got_a = lax.optimization_barrier((total, got_a))
    product = lambda got, total, unit, keep: project_pair(
        got, near_weight, far_weight, total, unit, keep, cores
    )
    there_a, here_a = product(got_a, total, 0, False)
    there_a, here_a, got_a, got_b = lax.optimization_barrier((there_a, here_a, got_a, got_b))
    across = lambda parts: [over_head(a, 1) for a in parts]
    moved_a = across(there_a)
    there_b, here_b = product(got_b, total, 1, False)
    there_b, here_b, moved_a = lax.optimization_barrier((there_b, here_b, moved_a))
    moved = zip(moved_a, across(there_b))
    passed = [
        jnp.concatenate([here_a[i] + a, here_b[i] + b]) for i, (a, b) in enumerate(moved)
    ]
    passed, got_a, got_b, own_b = lax.optimization_barrier((passed, got_a, got_b, own_b))
    sent = ending(passed)
    kept_total = project_chip(own_a, own_b, out_weight, keep_order)
    keep_a = product(got_a, kept_total, 0, True)
    keep_b = product(got_b, kept_total, 1, True)
    kept = []
    for there, here in (keep_a, keep_b):
        moved = across(there)
        kept += [here[i] + jnp.concatenate(moved[2 * i : 2 * i + 2], axis=1) for i in range(2)]
    rows = kept[0].shape[0]
    sent = (sent[0][:rows], sent[1][:rows], sent[0][rows:], sent[1][rows:])
    return jnp.concatenate([a + b for a, b in zip(kept, sent)], axis=0)


def solution(mesh):
    placed = (P("seq", "head"), P("seq", "head"), P("seq", "head"), P(), P(), P(), P("head", None))
    return jax.shard_map(
        body, mesh=mesh, in_specs=placed, out_specs=P("seq", "head"), check_vma=False
    )
```

```python
import functools
import math

import jax
import jax.numpy as jnp
from jax import lax
from jax.experimental import pallas as pl
from jax.experimental.pallas import tpu as pltpu
from jax.sharding import PartitionSpec as P

HEAD_SIZE = 128
BLOCK = 64
TILE = 256
FAR = 1 << 30
LOW = -1e30
LARGE = pl.CostEstimate(flops=100000, bytes_accessed=1024, transcendentals=0)
HUGE = pl.CostEstimate(flops=6 << 30, bytes_accessed=1024, transcendentals=0)
SMALL = pl.CostEstimate(flops=1024, bytes_accessed=1024, transcendentals=0)


def pick_kernel(k_place, k_held, v_place, v_held, *refs):
    pieces, outs, rows = refs[:8], refs[8:12], refs[12:]
    size = pieces[0].shape[0]
    slots = outs[0].shape[0] // BLOCK
    for which, (place, held) in enumerate(((k_place, k_held), (v_place, v_held))):
        for at in range(4):
            rows[which][at * size : (at + 1) * size, :] = pieces[4 * which + at][...]
        for slot in range(2 * slots):
            out = outs[2 * which + slot // slots]
            target = pl.ds(slot % slots * BLOCK, BLOCK)

            @pl.when(held[slot] == 1)
            def _():
                start = pl.multiple_of(place[slot] * BLOCK, BLOCK)
                out[target, :] = rows[which][pl.ds(start, BLOCK), :]

            @pl.when(held[slot] == 0)
            def _():
                out[target, :] = jnp.zeros((BLOCK, HEAD_SIZE), jnp.float32)


def pick_blocks(k_place, k_held, v_place, v_held, k_pieces, v_pieces):
    half = k_place.shape[0] // 2 * BLOCK
    smem = pl.BlockSpec(memory_space=pltpu.SMEM)
    vmem = pl.BlockSpec(memory_space=pltpu.VMEM)
    out = jax.ShapeDtypeStruct((half, HEAD_SIZE), jnp.float32)
    size = k_pieces[0].shape[0]
    return pl.pallas_call(
        pick_kernel,
        out_shape=[out] * 4,
        in_specs=[smem] * 4 + [vmem] * 8,
        out_specs=[vmem] * 4,
        scratch_shapes=[pltpu.VMEM((4 * size, HEAD_SIZE), jnp.float32)] * 2,
        compiler_params=pltpu.CompilerParams(vmem_limit_bytes=16 << 20),
        cost_estimate=SMALL,
    )(k_place, k_held, v_place, v_held, *k_pieces, *v_pieces)


def split(x):
    high = x.astype(jnp.bfloat16)
    return high, (x - high.astype(jnp.float32)).astype(jnp.bfloat16)


def fold(x):
    half = x.shape[0] // 2
    return x[:half] + x[half:]


def put_parts(target, first, pieces):
    for piece in pieces:
        count = piece.shape[0]
        high, low = split(piece[...])
        target[first : first + count, 0:HEAD_SIZE] = high
        target[first : first + count, HEAD_SIZE:] = low
        first += count


dot = functools.partial(lax.dot_general, preferred_element_type=jnp.float32)
ACROSS = (((1,), (1,)), ((), ()))
DOWN = (((1,), (0,)), ((), ()))
SCALE = math.log2(math.e) / math.sqrt(HEAD_SIZE)


def query_parts(q):
    return (jnp.concatenate([x, x], axis=1) for x in split(q))


def scale_kernel(q, out):
    out[...] = q[...] * SCALE


def scaled(q):
    rows, width = q.shape
    spec = pl.BlockSpec((TILE, width), lambda i: (i, 0))
    return pl.pallas_call(
        scale_kernel,
        grid=(rows // TILE,),
        out_shape=jax.ShapeDtypeStruct(q.shape, jnp.float32),
        in_specs=[spec],
        out_specs=spec,
        compiler_params=pltpu.CompilerParams(vmem_limit_bytes=8 << 20),
        cost_estimate=HUGE,
    )(q)


def weights_of(scores, top):
    weights = jnp.exp2(scores - top)
    return weights, jnp.sum(weights, axis=1, keepdims=True)


def near_kernel(
    start, first_row, back, wraps, q, k_far, k_far_wrap, k_left, k_left_wrap, k_own,
    v_far_a, v_far_b, v_left, v_own, slash_pos, out, stats, near_k, near_v,
):
    turn = pl.program_id(0)

    @pl.when((turn == 0) & (pl.program_id(1) == 0))
    def _():
        rows = k_own.shape[0]
        for at, (plain, wrapped) in enumerate(((k_far, k_far_wrap), (k_left, k_left_wrap))):

            @pl.when(wraps[at] == 0)
            def _():
                put_parts(near_k, at * rows, (plain,))

            @pl.when(wraps[at] == 1)
            def _():
                put_parts(near_k, at * rows, (wrapped,))

        put_parts(near_k, 2 * rows, (k_own,))
        put_parts(near_v, 0, (v_far_a, v_far_b, v_left, v_own))

    q_pos = first_row[0] + start + turn * TILE + lax.broadcasted_iota(jnp.int32, (TILE, 1), 0)
    per_block = TILE // BLOCK
    pair = q.shape[1] // HEAD_SIZE
    lane = lax.broadcasted_iota(jnp.int32, (TILE, HEAD_SIZE), 1)
    known = jnp.zeros((TILE, HEAD_SIZE), jnp.float32)
    for part in range(pair):
        head = pl.program_id(1) * pair + part
        columns = slice(part * HEAD_SIZE, (part + 1) * HEAD_SIZE)
        high, low = query_parts(q[:, columns])
        scores, near = [], []
        for j in range(per_block):
            block = start // BLOCK + turn * per_block + j
            spots = [
                pl.ds(pl.multiple_of((block + back[head, n]) * BLOCK, BLOCK), BLOCK)
                for n in range(4)
            ]
            near.append(spots)
            keys = jnp.concatenate([near_k[s, :] for s in spots], axis=0)
            mine = slice(j * BLOCK, (j + 1) * BLOCK)
            score = fold(dot(jnp.concatenate([high[mine], low[mine]], axis=0), keys, ACROSS))
            scores.append(jnp.where(slash_pos[head, block] <= q_pos[mine], score, LOW))
        scores = jnp.concatenate(scores, axis=0)
        top = jnp.max(scores, axis=1, keepdims=True)
        weights, total = weights_of(scores, top)
        w_high, w_low = split(weights)
        parts = []
        for j in range(per_block):
            values = jnp.concatenate([near_v[s, :] for s in near[j]], axis=0)
            mine = slice(j * BLOCK, (j + 1) * BLOCK)
            stacked = jnp.concatenate([w_high[mine], w_low[mine]], axis=0)
            parts.append(fold(dot(stacked, values, DOWN)))
        mixed = jnp.concatenate(parts, axis=0)
        out[:, columns] = mixed[:, :HEAD_SIZE] + mixed[:, HEAD_SIZE:]
        known = jnp.where(lane == 2 * part, top, known)
        known = jnp.where(lane == 2 * part + 1, total, known)
    stats[...] = known


def attend_near(q, start, rows, first_row, back, wraps, arrays):
    width = q.shape[1]
    pair = 2
    count = width // (pair * HEAD_SIZE)
    base = start // TILE
    smem = pl.BlockSpec(memory_space=pltpu.SMEM)
    vmem = pl.BlockSpec(memory_space=pltpu.VMEM)
    wide = (TILE, pair * HEAD_SIZE)
    return pl.pallas_call(
        functools.partial(near_kernel, start),
        grid=(rows // TILE, count),
        out_shape=[
            jax.ShapeDtypeStruct((rows, width), jnp.float32),
            jax.ShapeDtypeStruct((rows, count * HEAD_SIZE), jnp.float32),
        ],
        in_specs=[smem, smem, smem, pl.BlockSpec(wide, lambda t, h: (base + t, h))]
        + [vmem] * len(arrays),
        out_specs=[
            pl.BlockSpec(wide, lambda t, h: (t, h)),
            pl.BlockSpec((TILE, HEAD_SIZE), lambda t, h: (t, h)),
        ],
        scratch_shapes=[pltpu.VMEM((3 * q.shape[0], 2 * HEAD_SIZE), jnp.bfloat16)] * 2,
        compiler_params=pltpu.CompilerParams(vmem_limit_bytes=24 << 20),
        cost_estimate=LARGE,
    )(first_row, back, wraps, q, *arrays)


def attend_kernel(
    start, first_row, q, near, stats, k_a, k_b, v_a, v_b, vert_pos, out, vert_k, vert_v
):
    turn = pl.program_id(0)

    @pl.when((turn == 0) & (pl.program_id(1) == 0))
    def _():
        put_parts(vert_k, 0, (k_a, k_b))
        put_parts(vert_v, 0, (v_a, v_b))

    q_pos = first_row[0] + start + turn * TILE + lax.broadcasted_iota(jnp.int32, (TILE, 1), 0)
    vert = vert_pos.shape[2]
    pair = q.shape[1] // HEAD_SIZE
    for part in range(pair):
        head = pl.program_id(1) * pair + part
        columns = slice(part * HEAD_SIZE, (part + 1) * HEAD_SIZE)
        rows = pl.ds(pl.multiple_of(head * vert, vert), vert)
        both = jnp.concatenate(list(query_parts(q[:, columns])), axis=0)
        scores = fold(dot(both, vert_k[rows, :], ACROSS))
        scores = jnp.where(vert_pos[head] <= q_pos, scores, LOW)
        near_top = stats[:, 2 * part : 2 * part + 1]
        top = jnp.maximum(jnp.max(scores, axis=1, keepdims=True), near_top)
        weights, total = weights_of(scores, top)
        keep = jnp.exp2(near_top - top)
        total = total + keep * stats[:, 2 * part + 1 : 2 * part + 2]
        mixed = fold(dot(jnp.concatenate(split(weights), axis=0), vert_v[rows, :], DOWN))
        mixed = mixed[:, :HEAD_SIZE] + mixed[:, HEAD_SIZE:] + keep * near[:, columns]
        out[0, :, columns] = mixed / total


def attend(q, near, stats, start, first_row, arrays):
    width = q.shape[1]
    heads = width // HEAD_SIZE
    pair = 2
    smem = pl.BlockSpec(memory_space=pltpu.SMEM)
    vmem = pl.BlockSpec(memory_space=pltpu.VMEM)
    base = start // TILE
    wide = (TILE, pair * HEAD_SIZE)
    return pl.pallas_call(
        functools.partial(attend_kernel, start),
        grid=(2, heads // pair),
        out_shape=jax.ShapeDtypeStruct((2, TILE, width), jnp.float32),
        in_specs=[
            smem,
            pl.BlockSpec(wide, lambda t, h: (base + t, h)),
            pl.BlockSpec(wide, lambda t, h: (base + t, h)),
            pl.BlockSpec((TILE, HEAD_SIZE), lambda t, h: (base + t, h)),
        ]
        + [vmem] * len(arrays),
        out_specs=pl.BlockSpec((1, TILE, pair * HEAD_SIZE), lambda t, h: (t, 0, h)),
        scratch_shapes=[pltpu.VMEM((heads * 8 * BLOCK, 2 * HEAD_SIZE), jnp.bfloat16)] * 2,
        compiler_params=pltpu.CompilerParams(vmem_limit_bytes=20 << 20),
        cost_estimate=LARGE,
    )(first_row, q, near, stats, *arrays)


def take_kernel(chips, one, two, three, near, far):
    width = one.shape[1]
    near[:, :width], near[:, width:] = one[...], two[...]
    far[:, :width], far[:, width:] = three[...], two[...]


def take_columns(weight, chips, width):
    rows = weight.shape[0]
    step = rows // 8
    out = jax.ShapeDtypeStruct((rows, 2 * width), jnp.float32)
    out_spec = pl.BlockSpec((step, 2 * width), lambda i, o: (i, 0))
    w_spec = lambda at: pl.BlockSpec((step, width), lambda i, o: (i, o[at]))
    return pl.pallas_call(
        take_kernel,
        out_shape=[out, out],
        grid_spec=pltpu.PrefetchScalarGridSpec(
            num_scalar_prefetch=1,
            grid=(rows // step,),
            in_specs=[w_spec(0), w_spec(1), w_spec(2)],
            out_specs=[out_spec, out_spec],
        ),
        compiler_params=pltpu.CompilerParams(vmem_limit_bytes=58 << 20),
        cost_estimate=SMALL,
    )(chips, weight, weight, weight)


def weight_term(x, block):
    high, low = split(block)
    return fold(dot(x, high, DOWN)) + dot(x[: x.shape[0] // 2], low, DOWN)


def stack(rows):
    return jnp.concatenate(split(rows), axis=0)


def chip_kernel(order, own_a, own_b, w, out, x):
    for kind in range(2):

        @pl.when((pl.program_id(0) == kind) & (pl.program_id(1) == 0))
        def _():
            x[...] = stack(jnp.concatenate([own_a[kind], own_b[kind]], axis=0))

    out[0] = weight_term(x[...], w[...])


def project_chip(own_a, own_b, weight, order):
    _, rows, depth = own_a.shape
    width = depth
    vmem = pl.BlockSpec(memory_space=pltpu.VMEM)
    return pl.pallas_call(
        chip_kernel,
        out_shape=jax.ShapeDtypeStruct((2, 2 * rows, 2 * width), jnp.float32),
        grid_spec=pltpu.PrefetchScalarGridSpec(
            num_scalar_prefetch=1,
            grid=(2, 2),
            in_specs=[vmem, vmem, pl.BlockSpec((depth, width), lambda k, j, o: (0, o[2 * k + j]))],
            out_specs=pl.BlockSpec((1, 2 * rows, width), lambda k, j, o: (k, 0, j)),
            scratch_shapes=[pltpu.VMEM((4 * rows, depth), jnp.bfloat16)],
        ),
        compiler_params=pltpu.CompilerParams(vmem_limit_bytes=20 << 20),
        cost_estimate=LARGE,
    )(order, own_a, own_b, weight)


def pair_kernel(pieces, cores, got_a, got_b, near, far, total, *refs):
    *outs, x = refs
    for kind, (got, weight) in enumerate(((got_a, near), (got_b, far))):
        for turn, count in enumerate(pieces):
            start = 2 * sum(pieces[:turn]) + kind * count

            @pl.when((pl.program_id(0) == kind) & (pl.program_id(1) == turn))
            def _():
                if turn == 0:
                    x[...] = stack(got[...])
                term = total[0] + weight_term(x[...], weight[...])
                for at, out in enumerate(outs[start : start + count]):
                    width = out.shape[1]
                    out[...] = term[:, at * width : (at + 1) * width]


def project_pair(got, near, far, total, unit, keep, cores, first=0, pieces=(1, 1)):
    rows, depth = got[0].shape
    width = depth
    base = 0 if keep else 2
    turns = len(pieces)
    vmem = pl.BlockSpec(memory_space=pltpu.VMEM)
    shapes = [
        jax.ShapeDtypeStruct((rows, width // count), jnp.float32)
        for count in pieces
        for _ in range(2 * count)
    ]
    w_spec = lambda place: pl.BlockSpec(
        (depth, width), lambda k, s, c: (0, base + c[first + place(k, s)])
    )
    outs = pl.pallas_call(
        functools.partial(pair_kernel, pieces),
        out_shape=shapes,
        grid_spec=pltpu.PrefetchScalarGridSpec(
            num_scalar_prefetch=1,
            grid=(2, turns),
            in_specs=[
                vmem,
                vmem,
                w_spec(lambda k, s: jnp.where(k == 0, s, turns - 1)),
                w_spec(lambda k, s: jnp.where(k == 0, 0, s)),
                pl.BlockSpec((1, rows, width), lambda k, s, c: (k, unit, first + s)),
            ],
            out_specs=[pl.BlockSpec(x.shape, lambda k, s, c: (0, 0)) for x in shapes],
            scratch_shapes=[pltpu.VMEM((2 * rows, depth), jnp.bfloat16)],
        ),
        compiler_params=pltpu.CompilerParams(vmem_limit_bytes=16 << 20),
        cost_estimate=LARGE,
    )(cores, *got, near, far, total)
    cuts = [2 * sum(pieces[:turn]) for turn in range(turns + 1)]
    return [outs[i:j] for i, j in zip(cuts, cuts[1:])]


def body(
    queries, key_rows, value_vectors, vertical_blocks, slash_offsets, prompt_length, out_weight
):
    rows = queries.shape[0]
    blocks = rows // BLOCK
    heads = queries.shape[1] // HEAD_SIZE
    seq_index = lax.axis_index("seq")
    head_index = lax.axis_index("head")
    head_size = lax.axis_size("head")
    core = head_index % 2
    chips = head_size // 2

    x, z = seq_index % 4, seq_index // 4
    ids = range(lax.axis_size("seq"))
    right = [(i, i // 4 * 4 + (i + 1) % 4) for i in ids]
    left = [(i, i // 4 * 4 + (i + 3) % 4) for i in ids]
    over = [(i, i // 4 * 4 + (i + 2) % 4) for i in ids]
    up = [(i, (i + 4) % 16) for i in ids]
    down = [(i, (i + 12) % 16) for i in ids]
    send = lambda a, pairs: lax.ppermute(a, "seq", pairs)
    swapped = lambda a, bits: send(a, [(i, i ^ bits) for i in ids])

    k_left = send(key_rows, right)
    k_right = send(key_rows, left)
    v_below = send(value_vectors, up)
    v_above = send(value_vectors, down)

    y = head_index // 2
    over_head = lambda a, bits: lax.ppermute(a, "head", [(i, i ^ bits) for i in range(head_size)])
    width = out_weight.shape[1] // head_size
    near_weight, far_weight = take_columns(out_weight, y ^ jnp.arange(1, 4), 2 * width)
    near_weight, far_weight = over_head(near_weight, 2), over_head(far_weight, 6)

    vert = lax.dynamic_slice_in_dim(vertical_blocks, head_index * heads, heads, 0)
    slash = lax.dynamic_slice_in_dim(slash_offsets, head_index * heads, heads, 0)
    prompt = prompt_length[0]
    named = vert.reshape(-1)
    inside = jnp.arange(BLOCK, dtype=jnp.int32)
    vert_pos = vert[:, :, None] * BLOCK + inside
    vert_pos = jnp.where(vert_pos < prompt, -1, vert_pos).reshape(heads, 1, -1)
    offsets = jnp.concatenate([jnp.zeros((heads, 1), jnp.int32), slash + 1], axis=1)
    block_ids = seq_index * blocks + jnp.arange(blocks, dtype=jnp.int32)
    slash_block = block_ids[None, :, None] - offsets[:, None, :]
    repeated = jnp.any(slash_block[:, :, :, None] == vert[:, None, None, :], axis=-1)
    usable = (slash_block >= 0) & jnp.logical_not(repeated)
    slash_pos = slash_block[..., None] * BLOCK + inside
    slash_pos = jnp.where(slash_pos < prompt, -1, slash_pos)
    slash_pos = jnp.where(usable[..., None], slash_pos, FAR).reshape(heads, blocks, 1, -1)
    first_row = (seq_index * rows).reshape(1)
    back = 2 * blocks - offsets
    wraps = jnp.stack([x < 2, x == 0]).astype(jnp.int32)
    cores = jnp.stack([1 - core, core])
    pass_order = jnp.concatenate([2 * chip + cores for chip in (y ^ 3, y ^ 1)])
    keep_order = jnp.concatenate([2 * y + cores] * 2)
    owner = named // blocks
    at = named % blocks
    k_place, k_held = (owner % 4 - x) % 4 * blocks + at, (owner // 4 == z).astype(jnp.int32)
    v_place, v_held = (owner // 4 - z) % 4 * blocks + at, (owner % 4 == x).astype(jnp.int32)
    orders = (pass_order, keep_order, cores)
    small = (vert_pos, slash_pos, first_row, back, wraps, orders, k_place, k_held, v_place, v_held)

    (k_left, k_right, v_below, v_above), small = lax.optimization_barrier(
        ((k_left, k_right, v_below, v_above), small)
    )
    vert_pos, slash_pos, first_row, back, wraps, orders, k_place, k_held, v_place, v_held = small
    half = rows // 2
    source = jnp.where(x >= 2, v_below, value_vectors)
    v_left = jnp.where(x == 3, v_below, value_vectors)
    moved_left = send(jnp.concatenate([k_right, source[half:]]), left)
    v_beyond = send(v_above, down)
    moved_right = send(jnp.concatenate([v_left, source[:half]]), right)
    k_left_wrap = send(k_left, [(i, i + 4) for i in ids if i % 4 == 0 and i + 4 in ids])
    moved_left, v_beyond, moved_right, k_left_wrap = lax.optimization_barrier(
        (moved_left, v_beyond, moved_right, k_left_wrap)
    )
    k_far, v_far_b = moved_left[:rows], moved_left[rows:]
    v_left, v_far_a = moved_right[:rows], moved_right[rows:]

    k_pieces = (key_rows, k_right, k_far, k_left)
    v_pieces = (value_vectors, v_above, v_beyond, v_below)
    named = pick_blocks(k_place, k_held, v_place, v_held, k_pieces, v_pieces)
    v_far_a = send(v_far_a, right)
    v_far_b = send(v_far_b, left)
    k_far_wrap = send(k_far, [(i, i + 4) for i in ids if i % 4 < 2 and i + 4 in ids])
    one, two = (4, 12, 1, 3), (12, 4, 3, 1)
    more = [swapped(a, bits) for a, bits in zip(named, one)]
    q = scaled(queries)
    q, v_far_a, v_far_b, k_far_wrap, *more = lax.optimization_barrier(
        (q, v_far_a, v_far_b, k_far_wrap, *more)
    )
    named = [a + b for a, b in zip(named, more)]
    arrays = (k_far, k_far_wrap, k_left, k_left_wrap, key_rows, v_far_a, v_far_b, v_left)
    near_arrays = (*arrays, value_vectors, slash_pos)
    near = attend_near(q, 0, rows, first_row, back, wraps, near_arrays)
    more = [swapped(a, bits) for a, bits in zip(named, two)]
    near, more = lax.optimization_barrier((near, more))
    arrays = (*(a + b for a, b in zip(named, more)), vert_pos)

    pass_order, keep_order, cores = orders
    meet, end = (2, 6), (6, 2)
    own_a = attend(q, *near, 0, first_row, arrays)
    q, own_a = lax.optimization_barrier((q, own_a))
    meeting = lambda parts: [over_head(parts[i], bits) for i, bits in enumerate(meet)]
    ending = lambda parts: [over_head(parts[i], bits) for i, bits in enumerate(end)]
    got_a = meeting(own_a)
    own_b = attend(q, *near, half, first_row, arrays)
    got_b = meeting(own_b)
    own_b, near_weight, far_weight = lax.optimization_barrier((own_b, near_weight, far_weight))
    own_b, got_a = lax.optimization_barrier((own_b, got_a))
    total = project_chip(own_a, own_b, out_weight, pass_order)
    product = lambda got, total, unit, keep, **kind: project_pair(
        got, near_weight, far_weight, total, unit, keep, cores, **kind
    )
    there_a, here_a = product(got_a, total, 0, False)
    there_a, here_a, got_a, got_b = lax.optimization_barrier((there_a, here_a, got_a, got_b))
    across = lambda parts: [over_head(a, 1) for a in parts]
    moved_a = across(there_a)
    (there_b,) = product(got_b, total, 1, False, pieces=(1,))
    there_b, moved_a, got_b = lax.optimization_barrier((there_b, moved_a, got_b))
    moved_b = across(there_b)
    (here_b,) = product(got_b, total, 1, False, first=1, pieces=(1,))
    here_b, moved_b = lax.optimization_barrier((here_b, moved_b))
    passed = [
        jnp.concatenate([here_a[i] + moved_a[i], here_b[i] + moved_b[i]]) for i in range(2)
    ]
    passed, got_a, got_b, own_b = lax.optimization_barrier((passed, got_a, got_b, own_b))
    sent = ending(passed)
    kept_total = project_chip(own_a, own_b, out_weight, keep_order)
    keep_a = product(got_a, kept_total, 0, True, pieces=(2, 1))
    keep_b = product(got_b, kept_total, 1, True, pieces=(2, 1))
    kept = []
    for there, here in (keep_a, keep_b):
        moved = across(there)
        kept += [here[i] + jnp.concatenate(moved[2 * i : 2 * i + 2], axis=1) for i in range(2)]
    rows = kept[0].shape[0]
    sent = (sent[0][:rows], sent[1][:rows], sent[0][rows:], sent[1][rows:])
    return jnp.concatenate([a + b for a, b in zip(kept, sent)], axis=0)


def solution(mesh):
    placed = (P("seq", "head"), P("seq", "head"), P("seq", "head"), P(), P(), P(), P("head", None))
    return jax.shard_map(
        body, mesh=mesh, in_specs=placed, out_specs=P("seq", "head"), check_vma=False
    )
```

```python
import functools
import math

import jax
import jax.numpy as jnp
from jax import lax
from jax.experimental import pallas as pl
from jax.experimental.pallas import tpu as pltpu
from jax.sharding import PartitionSpec as P

HEAD_SIZE = 128
BLOCK = 64
TILE = 256
FAR = 1 << 30
LOW = -1e30
LARGE = pl.CostEstimate(flops=100000, bytes_accessed=1024, transcendentals=0)
HUGE = pl.CostEstimate(flops=6 << 30, bytes_accessed=1024, transcendentals=0)
SMALL = pl.CostEstimate(flops=1024, bytes_accessed=1024, transcendentals=0)


def pick_kernel(k_place, k_held, v_place, v_held, *refs):
    pieces, outs, rows = refs[:8], refs[8:12], refs[12:]
    size = pieces[0].shape[0]
    slots = outs[0].shape[0] // BLOCK
    for which, (place, held) in enumerate(((k_place, k_held), (v_place, v_held))):
        for at in range(4):
            rows[which][at * size : (at + 1) * size, :] = pieces[4 * which + at][...]
        for slot in range(2 * slots):
            out = outs[2 * which + slot // slots]
            target = pl.ds(slot % slots * BLOCK, BLOCK)

            @pl.when(held[slot] == 1)
            def _():
                start = pl.multiple_of(place[slot] * BLOCK, BLOCK)
                out[target, :] = rows[which][pl.ds(start, BLOCK), :]

            @pl.when(held[slot] == 0)
            def _():
                out[target, :] = jnp.zeros((BLOCK, HEAD_SIZE), jnp.float32)


def pick_blocks(k_place, k_held, v_place, v_held, k_pieces, v_pieces):
    half = k_place.shape[0] // 2 * BLOCK
    smem = pl.BlockSpec(memory_space=pltpu.SMEM)
    vmem = pl.BlockSpec(memory_space=pltpu.VMEM)
    out = jax.ShapeDtypeStruct((half, HEAD_SIZE), jnp.float32)
    size = k_pieces[0].shape[0]
    return pl.pallas_call(
        pick_kernel,
        out_shape=[out] * 4,
        in_specs=[smem] * 4 + [vmem] * 8,
        out_specs=[vmem] * 4,
        scratch_shapes=[pltpu.VMEM((4 * size, HEAD_SIZE), jnp.float32)] * 2,
        compiler_params=pltpu.CompilerParams(vmem_limit_bytes=16 << 20),
        cost_estimate=SMALL,
    )(k_place, k_held, v_place, v_held, *k_pieces, *v_pieces)


def split(x):
    high = x.astype(jnp.bfloat16)
    return high, (x - high.astype(jnp.float32)).astype(jnp.bfloat16)


def fold(x):
    half = x.shape[0] // 2
    return x[:half] + x[half:]


def put_parts(target, first, pieces):
    for piece in pieces:
        count = piece.shape[0]
        high, low = split(piece[...])
        target[first : first + count, 0:HEAD_SIZE] = high
        target[first : first + count, HEAD_SIZE:] = low
        first += count


dot = functools.partial(lax.dot_general, preferred_element_type=jnp.float32)
ACROSS = (((1,), (1,)), ((), ()))
DOWN = (((1,), (0,)), ((), ()))
SCALE = math.log2(math.e) / math.sqrt(HEAD_SIZE)


def query_parts(q):
    return (jnp.concatenate([x, x], axis=1) for x in split(q))


def scale_kernel(q, out):
    out[...] = q[...] * SCALE


def scaled(q):
    rows, width = q.shape
    spec = pl.BlockSpec((TILE, width), lambda i: (i, 0))
    return pl.pallas_call(
        scale_kernel,
        grid=(rows // TILE,),
        out_shape=jax.ShapeDtypeStruct(q.shape, jnp.float32),
        in_specs=[spec],
        out_specs=spec,
        compiler_params=pltpu.CompilerParams(vmem_limit_bytes=8 << 20),
        cost_estimate=HUGE,
    )(q)


def weights_of(scores, top):
    weights = jnp.exp2(scores - top)
    return weights, jnp.sum(weights, axis=1, keepdims=True)


def near_kernel(
    start, first_row, back, wraps, q, k_far, k_far_wrap, k_left, k_left_wrap, k_own,
    v_far_a, v_far_b, v_left, v_own, slash_pos, out, stats, near_k, near_v,
):
    turn = pl.program_id(0)

    @pl.when((turn == 0) & (pl.program_id(1) == 0))
    def _():
        rows = k_own.shape[0]
        for at, (plain, wrapped) in enumerate(((k_far, k_far_wrap), (k_left, k_left_wrap))):

            @pl.when(wraps[at] == 0)
            def _():
                put_parts(near_k, at * rows, (plain,))

            @pl.when(wraps[at] == 1)
            def _():
                put_parts(near_k, at * rows, (wrapped,))

        put_parts(near_k, 2 * rows, (k_own,))
        put_parts(near_v, 0, (v_far_a, v_far_b, v_left, v_own))

    q_pos = first_row[0] + start + turn * TILE + lax.broadcasted_iota(jnp.int32, (TILE, 1), 0)
    per_block = TILE // BLOCK
    pair = q.shape[1] // HEAD_SIZE
    lane = lax.broadcasted_iota(jnp.int32, (TILE, HEAD_SIZE), 1)
    known = jnp.zeros((TILE, HEAD_SIZE), jnp.float32)
    for part in range(pair):
        head = pl.program_id(1) * pair + part
        columns = slice(part * HEAD_SIZE, (part + 1) * HEAD_SIZE)
        high, low = query_parts(q[:, columns])
        scores, near = [], []
        for j in range(per_block):
            block = start // BLOCK + turn * per_block + j
            spots = [
                pl.ds(pl.multiple_of((block + back[head, n]) * BLOCK, BLOCK), BLOCK)
                for n in range(4)
            ]
            near.append(spots)
            keys = jnp.concatenate([near_k[s, :] for s in spots], axis=0)
            mine = slice(j * BLOCK, (j + 1) * BLOCK)
            score = fold(dot(jnp.concatenate([high[mine], low[mine]], axis=0), keys, ACROSS))
            scores.append(jnp.where(slash_pos[head, block] <= q_pos[mine], score, LOW))
        scores = jnp.concatenate(scores, axis=0)
        top = jnp.max(scores, axis=1, keepdims=True)
        weights, total = weights_of(scores, top)
        w_high, w_low = split(weights)
        parts = []
        for j in range(per_block):
            values = jnp.concatenate([near_v[s, :] for s in near[j]], axis=0)
            mine = slice(j * BLOCK, (j + 1) * BLOCK)
            stacked = jnp.concatenate([w_high[mine], w_low[mine]], axis=0)
            parts.append(fold(dot(stacked, values, DOWN)))
        mixed = jnp.concatenate(parts, axis=0)
        out[:, columns] = mixed[:, :HEAD_SIZE] + mixed[:, HEAD_SIZE:]
        known = jnp.where(lane == 2 * part, top, known)
        known = jnp.where(lane == 2 * part + 1, total, known)
    stats[...] = known


def attend_near(q, start, rows, first_row, back, wraps, arrays):
    width = q.shape[1]
    pair = 2
    count = width // (pair * HEAD_SIZE)
    base = start // TILE
    smem = pl.BlockSpec(memory_space=pltpu.SMEM)
    vmem = pl.BlockSpec(memory_space=pltpu.VMEM)
    wide = (TILE, pair * HEAD_SIZE)
    return pl.pallas_call(
        functools.partial(near_kernel, start),
        grid=(rows // TILE, count),
        out_shape=[
            jax.ShapeDtypeStruct((rows, width), jnp.float32),
            jax.ShapeDtypeStruct((rows, count * HEAD_SIZE), jnp.float32),
        ],
        in_specs=[smem, smem, smem, pl.BlockSpec(wide, lambda t, h: (base + t, h))]
        + [vmem] * len(arrays),
        out_specs=[
            pl.BlockSpec(wide, lambda t, h: (t, h)),
            pl.BlockSpec((TILE, HEAD_SIZE), lambda t, h: (t, h)),
        ],
        scratch_shapes=[pltpu.VMEM((3 * q.shape[0], 2 * HEAD_SIZE), jnp.bfloat16)] * 2,
        compiler_params=pltpu.CompilerParams(vmem_limit_bytes=24 << 20),
        cost_estimate=LARGE,
    )(first_row, back, wraps, q, *arrays)


def attend_kernel(
    start, first_row, q, near, stats, k_a, k_b, v_a, v_b, vert_pos, out, vert_k, vert_v
):
    turn = pl.program_id(0)

    @pl.when((turn == 0) & (pl.program_id(1) == 0))
    def _():
        put_parts(vert_k, 0, (k_a, k_b))
        put_parts(vert_v, 0, (v_a, v_b))

    q_pos = first_row[0] + start + turn * TILE + lax.broadcasted_iota(jnp.int32, (TILE, 1), 0)
    vert = vert_pos.shape[2]
    pair = q.shape[1] // HEAD_SIZE
    for part in range(pair):
        head = pl.program_id(1) * pair + part
        columns = slice(part * HEAD_SIZE, (part + 1) * HEAD_SIZE)
        rows = pl.ds(pl.multiple_of(head * vert, vert), vert)
        both = jnp.concatenate(list(query_parts(q[:, columns])), axis=0)
        scores = fold(dot(both, vert_k[rows, :], ACROSS))
        scores = jnp.where(vert_pos[head] <= q_pos, scores, LOW)
        near_top = stats[:, 2 * part : 2 * part + 1]
        top = jnp.maximum(jnp.max(scores, axis=1, keepdims=True), near_top)
        weights, total = weights_of(scores, top)
        keep = jnp.exp2(near_top - top)
        total = total + keep * stats[:, 2 * part + 1 : 2 * part + 2]
        mixed = fold(dot(jnp.concatenate(split(weights), axis=0), vert_v[rows, :], DOWN))
        mixed = mixed[:, :HEAD_SIZE] + mixed[:, HEAD_SIZE:] + keep * near[:, columns]
        out[0, :, columns] = mixed / total


def attend(q, near, stats, start, first_row, arrays):
    width = q.shape[1]
    heads = width // HEAD_SIZE
    pair = 2
    smem = pl.BlockSpec(memory_space=pltpu.SMEM)
    vmem = pl.BlockSpec(memory_space=pltpu.VMEM)
    base = start // TILE
    wide = (TILE, pair * HEAD_SIZE)
    return pl.pallas_call(
        functools.partial(attend_kernel, start),
        grid=(2, heads // pair),
        out_shape=jax.ShapeDtypeStruct((2, TILE, width), jnp.float32),
        in_specs=[
            smem,
            pl.BlockSpec(wide, lambda t, h: (base + t, h)),
            pl.BlockSpec(wide, lambda t, h: (base + t, h)),
            pl.BlockSpec((TILE, HEAD_SIZE), lambda t, h: (base + t, h)),
        ]
        + [vmem] * len(arrays),
        out_specs=pl.BlockSpec((1, TILE, pair * HEAD_SIZE), lambda t, h: (t, 0, h)),
        scratch_shapes=[pltpu.VMEM((heads * 8 * BLOCK, 2 * HEAD_SIZE), jnp.bfloat16)] * 2,
        compiler_params=pltpu.CompilerParams(vmem_limit_bytes=20 << 20),
        cost_estimate=LARGE,
    )(first_row, q, near, stats, *arrays)


def take_kernel(chips, one, two, three, near, far):
    width = one.shape[1]
    near[:, :width], near[:, width:] = one[...], two[...]
    far[:, :width], far[:, width:] = three[...], two[...]


def take_columns(weight, chips, width):
    rows = weight.shape[0]
    step = rows // 8
    out = jax.ShapeDtypeStruct((rows, 2 * width), jnp.float32)
    out_spec = pl.BlockSpec((step, 2 * width), lambda i, o: (i, 0))
    w_spec = lambda at: pl.BlockSpec((step, width), lambda i, o: (i, o[at]))
    return pl.pallas_call(
        take_kernel,
        out_shape=[out, out],
        grid_spec=pltpu.PrefetchScalarGridSpec(
            num_scalar_prefetch=1,
            grid=(rows // step,),
            in_specs=[w_spec(0), w_spec(1), w_spec(2)],
            out_specs=[out_spec, out_spec],
        ),
        compiler_params=pltpu.CompilerParams(vmem_limit_bytes=58 << 20),
        cost_estimate=SMALL,
    )(chips, weight, weight, weight)


def weight_term(x, block):
    high, low = split(block)
    return fold(dot(x, high, DOWN)) + dot(x[: x.shape[0] // 2], low, DOWN)


def stack(rows):
    return jnp.concatenate(split(rows), axis=0)


def chip_kernel(order, own_a, own_b, w, out, x):
    for kind in range(2):

        @pl.when((pl.program_id(0) == kind) & (pl.program_id(1) == 0))
        def _():
            x[...] = stack(jnp.concatenate([own_a[kind], own_b[kind]], axis=0))

    out[0] = weight_term(x[...], w[...])


def project_chip(own_a, own_b, weight, order):
    _, rows, depth = own_a.shape
    width = depth
    vmem = pl.BlockSpec(memory_space=pltpu.VMEM)
    return pl.pallas_call(
        chip_kernel,
        out_shape=jax.ShapeDtypeStruct((2, 2 * rows, 2 * width), jnp.float32),
        grid_spec=pltpu.PrefetchScalarGridSpec(
            num_scalar_prefetch=1,
            grid=(2, 2),
            in_specs=[vmem, vmem, pl.BlockSpec((depth, width), lambda k, j, o: (0, o[2 * k + j]))],
            out_specs=pl.BlockSpec((1, 2 * rows, width), lambda k, j, o: (k, 0, j)),
            scratch_shapes=[pltpu.VMEM((4 * rows, depth), jnp.bfloat16)],
        ),
        compiler_params=pltpu.CompilerParams(vmem_limit_bytes=20 << 20),
        cost_estimate=LARGE,
    )(order, own_a, own_b, weight)


def pair_kernel(pieces, cores, got_a, got_b, near, far, total, *refs):
    *outs, x = refs
    for kind, (got, weight) in enumerate(((got_a, near), (got_b, far))):
        for turn, count in enumerate(pieces):
            start = 2 * sum(pieces[:turn]) + kind * count

            @pl.when((pl.program_id(0) == kind) & (pl.program_id(1) == turn))
            def _():
                if turn == 0:
                    x[...] = stack(got[...])
                term = total[0] + weight_term(x[...], weight[...])
                for at, out in enumerate(outs[start : start + count]):
                    width = out.shape[1]
                    out[...] = term[:, at * width : (at + 1) * width]


def project_pair(got, near, far, total, unit, keep, cores, first=0, pieces=(1, 1)):
    rows, depth = got[0].shape
    width = depth
    base = 0 if keep else 2
    turns = len(pieces)
    vmem = pl.BlockSpec(memory_space=pltpu.VMEM)
    shapes = [
        jax.ShapeDtypeStruct((rows, width // count), jnp.float32)
        for count in pieces
        for _ in range(2 * count)
    ]
    w_spec = lambda place: pl.BlockSpec(
        (depth, width), lambda k, s, c: (0, base + c[first + place(k, s)])
    )
    outs = pl.pallas_call(
        functools.partial(pair_kernel, pieces),
        out_shape=shapes,
        grid_spec=pltpu.PrefetchScalarGridSpec(
            num_scalar_prefetch=1,
            grid=(2, turns),
            in_specs=[
                vmem,
                vmem,
                w_spec(lambda k, s: jnp.where(k == 0, s, turns - 1)),
                w_spec(lambda k, s: jnp.where(k == 0, 0, s)),
                pl.BlockSpec((1, rows, width), lambda k, s, c: (k, unit, first + s)),
            ],
            out_specs=[pl.BlockSpec(x.shape, lambda k, s, c: (0, 0)) for x in shapes],
            scratch_shapes=[pltpu.VMEM((2 * rows, depth), jnp.bfloat16)],
        ),
        compiler_params=pltpu.CompilerParams(vmem_limit_bytes=16 << 20),
        cost_estimate=LARGE,
    )(cores, *got, near, far, total)
    cuts = [2 * sum(pieces[:turn]) for turn in range(turns + 1)]
    return [outs[i:j] for i, j in zip(cuts, cuts[1:])]


def body(
    queries, key_rows, value_vectors, vertical_blocks, slash_offsets, prompt_length, out_weight
):
    rows = queries.shape[0]
    blocks = rows // BLOCK
    heads = queries.shape[1] // HEAD_SIZE
    seq_index = lax.axis_index("seq")
    head_index = lax.axis_index("head")
    head_size = lax.axis_size("head")
    core = head_index % 2
    chips = head_size // 2

    x, z = seq_index % 4, seq_index // 4
    ids = range(lax.axis_size("seq"))
    right = [(i, i // 4 * 4 + (i + 1) % 4) for i in ids]
    left = [(i, i // 4 * 4 + (i + 3) % 4) for i in ids]
    over = [(i, i // 4 * 4 + (i + 2) % 4) for i in ids]
    up = [(i, (i + 4) % 16) for i in ids]
    down = [(i, (i + 12) % 16) for i in ids]
    send = lambda a, pairs: lax.ppermute(a, "seq", pairs)
    swapped = lambda a, bits: send(a, [(i, i ^ bits) for i in ids])

    k_left = send(key_rows, right)
    k_right = send(key_rows, left)
    v_below = send(value_vectors, up)

    y = head_index // 2
    over_head = lambda a, bits: lax.ppermute(a, "head", [(i, i ^ bits) for i in range(head_size)])
    width = out_weight.shape[1] // head_size
    near_weight, far_weight = take_columns(out_weight, y ^ jnp.arange(1, 4), 2 * width)
    near_weight, far_weight = over_head(near_weight, 2), over_head(far_weight, 6)

    vert = lax.dynamic_slice_in_dim(vertical_blocks, head_index * heads, heads, 0)
    slash = lax.dynamic_slice_in_dim(slash_offsets, head_index * heads, heads, 0)
    prompt = prompt_length[0]
    named = vert.reshape(-1)
    inside = jnp.arange(BLOCK, dtype=jnp.int32)
    vert_pos = vert[:, :, None] * BLOCK + inside
    vert_pos = jnp.where(vert_pos < prompt, -1, vert_pos).reshape(heads, 1, -1)
    offsets = jnp.concatenate([jnp.zeros((heads, 1), jnp.int32), slash + 1], axis=1)
    block_ids = seq_index * blocks + jnp.arange(blocks, dtype=jnp.int32)
    slash_block = block_ids[None, :, None] - offsets[:, None, :]
    repeated = jnp.any(slash_block[:, :, :, None] == vert[:, None, None, :], axis=-1)
    usable = (slash_block >= 0) & jnp.logical_not(repeated)
    slash_pos = slash_block[..., None] * BLOCK + inside
    slash_pos = jnp.where(slash_pos < prompt, -1, slash_pos)
    slash_pos = jnp.where(usable[..., None], slash_pos, FAR).reshape(heads, blocks, 1, -1)
    first_row = (seq_index * rows).reshape(1)
    back = 2 * blocks - offsets
    wraps = jnp.stack([x < 2, x == 0]).astype(jnp.int32)
    cores = jnp.stack([1 - core, core])
    pass_order = jnp.concatenate([2 * chip + cores for chip in (y ^ 3, y ^ 1)])
    keep_order = jnp.concatenate([2 * y + cores] * 2)
    owner = named // blocks
    at = named % blocks
    k_place, k_held = (owner % 4 - x) % 4 * blocks + at, (owner // 4 == z).astype(jnp.int32)
    v_place, v_held = (owner // 4 - z) % 4 * blocks + at, (owner % 4 == x).astype(jnp.int32)
    orders = (pass_order, keep_order, cores)
    small = (vert_pos, slash_pos, first_row, back, wraps, orders, k_place, k_held, v_place, v_held)

    k_left, late_values = lax.optimization_barrier((k_left, value_vectors))
    v_above = send(late_values, down)
    (k_left, k_right, v_below), small = lax.optimization_barrier(
        ((k_left, k_right, v_below), small)
    )
    vert_pos, slash_pos, first_row, back, wraps, orders, k_place, k_held, v_place, v_held = small
    half = rows // 2
    source = jnp.where(x >= 2, v_below, value_vectors)
    v_left = jnp.where(x == 3, v_below, value_vectors)
    moved_left = send(jnp.concatenate([k_right, source[half:]]), left)
    v_beyond = send(v_above, down)
    moved_right = send(jnp.concatenate([v_left, source[:half]]), right)
    k_left_wrap = send(k_left, [(i, i + 4) for i in ids if i % 4 == 0 and i + 4 in ids])
    moved_left, v_beyond, moved_right, k_left_wrap = lax.optimization_barrier(
        (moved_left, v_beyond, moved_right, k_left_wrap)
    )
    k_far, v_far_b = moved_left[:rows], moved_left[rows:]
    v_left, v_far_a = moved_right[:rows], moved_right[rows:]

    k_pieces = (key_rows, k_right, k_far, k_left)
    v_pieces = (value_vectors, v_above, v_beyond, v_below)
    named = pick_blocks(k_place, k_held, v_place, v_held, k_pieces, v_pieces)
    v_far_a = send(v_far_a, right)
    v_far_b = send(v_far_b, left)
    k_far_wrap = send(k_far, [(i, i + 4) for i in ids if i % 4 < 2 and i + 4 in ids])
    one, two = (4, 12, 1, 3), (12, 4, 3, 1)
    more = [swapped(a, bits) for a, bits in zip(named, one)]
    q = scaled(queries)
    q, v_far_a, v_far_b, k_far_wrap, *more = lax.optimization_barrier(
        (q, v_far_a, v_far_b, k_far_wrap, *more)
    )
    named = [a + b for a, b in zip(named, more)]
    arrays = (k_far, k_far_wrap, k_left, k_left_wrap, key_rows, v_far_a, v_far_b, v_left)
    near_arrays = (*arrays, value_vectors, slash_pos)
    near = attend_near(q, 0, rows, first_row, back, wraps, near_arrays)
    more = [swapped(a, bits) for a, bits in zip(named, two)]
    near, more = lax.optimization_barrier((near, more))
    arrays = (*(a + b for a, b in zip(named, more)), vert_pos)

    pass_order, keep_order, cores = orders
    meet, end = (2, 6), (6, 2)
    own_a = attend(q, *near, 0, first_row, arrays)
    q, own_a = lax.optimization_barrier((q, own_a))
    meeting = lambda parts: [over_head(parts[i], bits) for i, bits in enumerate(meet)]
    ending = lambda parts: [over_head(parts[i], bits) for i, bits in enumerate(end)]
    got_a = meeting(own_a)
    own_b = attend(q, *near, half, first_row, arrays)
    got_b = meeting(own_b)
    own_b, near_weight, far_weight = lax.optimization_barrier((own_b, near_weight, far_weight))
    total = project_chip(own_a, own_b, out_weight, pass_order)
    total, got_a = lax.optimization_barrier((total, got_a))
    product = lambda got, total, unit, keep, **kind: project_pair(
        got, near_weight, far_weight, total, unit, keep, cores, **kind
    )
    there_a, here_a = product(got_a, total, 0, False)
    there_a, here_a, got_a, got_b = lax.optimization_barrier((there_a, here_a, got_a, got_b))
    across = lambda parts: [over_head(a, 1) for a in parts]
    moved_a = across(there_a)
    (there_b,) = product(got_b, total, 1, False, pieces=(1,))
    there_b, moved_a, got_b = lax.optimization_barrier((there_b, moved_a, got_b))
    moved_b = across(there_b)
    (here_b,) = product(got_b, total, 1, False, first=1, pieces=(1,))
    here_b, moved_b = lax.optimization_barrier((here_b, moved_b))
    passed = [
        jnp.concatenate([here_a[i] + moved_a[i], here_b[i] + moved_b[i]]) for i in range(2)
    ]
    passed, got_a, got_b, own_b = lax.optimization_barrier((passed, got_a, got_b, own_b))
    sent = ending(passed)
    kept_total = project_chip(own_a, own_b, out_weight, keep_order)
    keep_a = product(got_a, kept_total, 0, True, pieces=(2, 1))
    keep_b = product(got_b, kept_total, 1, True, pieces=(2, 1))
    kept = []
    for there, here in (keep_a, keep_b):
        moved = across(there)
        kept += [here[i] + jnp.concatenate(moved[2 * i : 2 * i + 2], axis=1) for i in range(2)]
    rows = kept[0].shape[0]
    sent = (sent[0][:rows], sent[1][:rows], sent[0][rows:], sent[1][rows:])
    return jnp.concatenate([a + b for a, b in zip(kept, sent)], axis=0)


def solution(mesh):
    placed = (P("seq", "head"), P("seq", "head"), P("seq", "head"), P(), P(), P(), P("head", None))
    return jax.shard_map(
        body, mesh=mesh, in_specs=placed, out_specs=P("seq", "head"), check_vma=False
    )
```

```python
import functools
import math

import jax
import jax.numpy as jnp
from jax import lax
from jax.experimental import pallas as pl
from jax.experimental.pallas import tpu as pltpu
from jax.sharding import PartitionSpec as P

HEAD_SIZE = 128
BLOCK = 64
TILE = 256
FAR = 1 << 30
LOW = -1e30
LARGE = pl.CostEstimate(flops=100000, bytes_accessed=1024, transcendentals=0)
HUGE = pl.CostEstimate(flops=6 << 30, bytes_accessed=1024, transcendentals=0)
SMALL = pl.CostEstimate(flops=1024, bytes_accessed=1024, transcendentals=0)


def pick_kernel(k_place, k_held, v_place, v_held, *refs):
    pieces, outs, rows = refs[:8], refs[8:12], refs[12:]
    size = pieces[0].shape[0]
    slots = outs[0].shape[0] // BLOCK
    for which, (place, held) in enumerate(((k_place, k_held), (v_place, v_held))):
        for at in range(4):
            rows[which][at * size : (at + 1) * size, :] = pieces[4 * which + at][...]
        for slot in range(2 * slots):
            out = outs[2 * which + slot // slots]
            target = pl.ds(slot % slots * BLOCK, BLOCK)

            @pl.when(held[slot] == 1)
            def _():
                start = pl.multiple_of(place[slot] * BLOCK, BLOCK)
                out[target, :] = rows[which][pl.ds(start, BLOCK), :]

            @pl.when(held[slot] == 0)
            def _():
                out[target, :] = jnp.zeros((BLOCK, HEAD_SIZE), jnp.float32)


def pick_blocks(k_place, k_held, v_place, v_held, k_pieces, v_pieces):
    half = k_place.shape[0] // 2 * BLOCK
    smem = pl.BlockSpec(memory_space=pltpu.SMEM)
    vmem = pl.BlockSpec(memory_space=pltpu.VMEM)
    out = jax.ShapeDtypeStruct((half, HEAD_SIZE), jnp.float32)
    size = k_pieces[0].shape[0]
    return pl.pallas_call(
        pick_kernel,
        out_shape=[out] * 4,
        in_specs=[smem] * 4 + [vmem] * 8,
        out_specs=[vmem] * 4,
        scratch_shapes=[pltpu.VMEM((4 * size, HEAD_SIZE), jnp.float32)] * 2,
        compiler_params=pltpu.CompilerParams(vmem_limit_bytes=16 << 20),
        cost_estimate=SMALL,
    )(k_place, k_held, v_place, v_held, *k_pieces, *v_pieces)


def split(x):
    high = x.astype(jnp.bfloat16)
    return high, (x - high.astype(jnp.float32)).astype(jnp.bfloat16)


def fold(x):
    half = x.shape[0] // 2
    return x[:half] + x[half:]


def put_parts(target, first, pieces):
    for piece in pieces:
        count = piece.shape[0]
        high, low = split(piece[...])
        target[first : first + count, 0:HEAD_SIZE] = high
        target[first : first + count, HEAD_SIZE:] = low
        first += count


dot = functools.partial(lax.dot_general, preferred_element_type=jnp.float32)
ACROSS = (((1,), (1,)), ((), ()))
DOWN = (((1,), (0,)), ((), ()))
SCALE = math.log2(math.e) / math.sqrt(HEAD_SIZE)


def query_parts(q):
    return (jnp.concatenate([x, x], axis=1) for x in split(q))


def scale_kernel(q, out):
    out[...] = q[...] * SCALE


def scaled(q):
    rows, width = q.shape
    spec = pl.BlockSpec((TILE, width), lambda i: (i, 0))
    return pl.pallas_call(
        scale_kernel,
        grid=(rows // TILE,),
        out_shape=jax.ShapeDtypeStruct(q.shape, jnp.float32),
        in_specs=[spec],
        out_specs=spec,
        compiler_params=pltpu.CompilerParams(vmem_limit_bytes=8 << 20),
        cost_estimate=HUGE,
    )(q)


def weights_of(scores, top):
    weights = jnp.exp2(scores - top)
    return weights, jnp.sum(weights, axis=1, keepdims=True)


def near_kernel(
    start, first_row, back, wraps, q, k_far, k_far_wrap, k_left, k_left_wrap, k_own,
    v_far_a, v_far_b, v_left, v_own, slash_pos, out, stats, near_k, near_v,
):
    turn = pl.program_id(0)

    @pl.when((turn == 0) & (pl.program_id(1) == 0))
    def _():
        rows = k_own.shape[0]
        for at, (plain, wrapped) in enumerate(((k_far, k_far_wrap), (k_left, k_left_wrap))):

            @pl.when(wraps[at] == 0)
            def _():
                put_parts(near_k, at * rows, (plain,))

            @pl.when(wraps[at] == 1)
            def _():
                put_parts(near_k, at * rows, (wrapped,))

        put_parts(near_k, 2 * rows, (k_own,))
        put_parts(near_v, 0, (v_far_a, v_far_b, v_left, v_own))

    q_pos = first_row[0] + start + turn * TILE + lax.broadcasted_iota(jnp.int32, (TILE, 1), 0)
    per_block = TILE // BLOCK
    pair = q.shape[1] // HEAD_SIZE
    lane = lax.broadcasted_iota(jnp.int32, (TILE, HEAD_SIZE), 1)
    known = jnp.zeros((TILE, HEAD_SIZE), jnp.float32)
    for part in range(pair):
        head = pl.program_id(1) * pair + part
        columns = slice(part * HEAD_SIZE, (part + 1) * HEAD_SIZE)
        high, low = query_parts(q[:, columns])
        scores, near = [], []
        for j in range(per_block):
            block = start // BLOCK + turn * per_block + j
            spots = [
                pl.ds(pl.multiple_of((block + back[head, n]) * BLOCK, BLOCK), BLOCK)
                for n in range(4)
            ]
            near.append(spots)
            keys = jnp.concatenate([near_k[s, :] for s in spots], axis=0)
            mine = slice(j * BLOCK, (j + 1) * BLOCK)
            score = fold(dot(jnp.concatenate([high[mine], low[mine]], axis=0), keys, ACROSS))
            scores.append(jnp.where(slash_pos[head, block] <= q_pos[mine], score, LOW))
        scores = jnp.concatenate(scores, axis=0)
        top = jnp.max(scores, axis=1, keepdims=True)
        weights, total = weights_of(scores, top)
        w_high, w_low = split(weights)
        parts = []
        for j in range(per_block):
            values = jnp.concatenate([near_v[s, :] for s in near[j]], axis=0)
            mine = slice(j * BLOCK, (j + 1) * BLOCK)
            stacked = jnp.concatenate([w_high[mine], w_low[mine]], axis=0)
            parts.append(fold(dot(stacked, values, DOWN)))
        mixed = jnp.concatenate(parts, axis=0)
        out[:, columns] = mixed[:, :HEAD_SIZE] + mixed[:, HEAD_SIZE:]
        known = jnp.where(lane == 2 * part, top, known)
        known = jnp.where(lane == 2 * part + 1, total, known)
    stats[...] = known


def attend_near(q, start, rows, first_row, back, wraps, arrays):
    width = q.shape[1]
    pair = 2
    count = width // (pair * HEAD_SIZE)
    base = start // TILE
    smem = pl.BlockSpec(memory_space=pltpu.SMEM)
    vmem = pl.BlockSpec(memory_space=pltpu.VMEM)
    wide = (TILE, pair * HEAD_SIZE)
    return pl.pallas_call(
        functools.partial(near_kernel, start),
        grid=(rows // TILE, count),
        out_shape=[
            jax.ShapeDtypeStruct((rows, width), jnp.float32),
            jax.ShapeDtypeStruct((rows, count * HEAD_SIZE), jnp.float32),
        ],
        in_specs=[smem, smem, smem, pl.BlockSpec(wide, lambda t, h: (base + t, h))]
        + [vmem] * len(arrays),
        out_specs=[
            pl.BlockSpec(wide, lambda t, h: (t, h)),
            pl.BlockSpec((TILE, HEAD_SIZE), lambda t, h: (t, h)),
        ],
        scratch_shapes=[pltpu.VMEM((3 * q.shape[0], 2 * HEAD_SIZE), jnp.bfloat16)] * 2,
        compiler_params=pltpu.CompilerParams(vmem_limit_bytes=24 << 20),
        cost_estimate=LARGE,
    )(first_row, back, wraps, q, *arrays)


def attend_kernel(
    start, first_row, q, near, stats, k_a, k_b, v_a, v_b, vert_pos, out, vert_k, vert_v
):
    turn = pl.program_id(0)

    @pl.when((turn == 0) & (pl.program_id(1) == 0))
    def _():
        put_parts(vert_k, 0, (k_a, k_b))
        put_parts(vert_v, 0, (v_a, v_b))

    q_pos = first_row[0] + start + turn * TILE + lax.broadcasted_iota(jnp.int32, (TILE, 1), 0)
    vert = vert_pos.shape[2]
    pair = q.shape[1] // HEAD_SIZE
    for part in range(pair):
        head = pl.program_id(1) * pair + part
        columns = slice(part * HEAD_SIZE, (part + 1) * HEAD_SIZE)
        rows = pl.ds(pl.multiple_of(head * vert, vert), vert)
        both = jnp.concatenate(list(query_parts(q[:, columns])), axis=0)
        scores = fold(dot(both, vert_k[rows, :], ACROSS))
        scores = jnp.where(vert_pos[head] <= q_pos, scores, LOW)
        near_top = stats[:, 2 * part : 2 * part + 1]
        top = jnp.maximum(jnp.max(scores, axis=1, keepdims=True), near_top)
        weights, total = weights_of(scores, top)
        keep = jnp.exp2(near_top - top)
        total = total + keep * stats[:, 2 * part + 1 : 2 * part + 2]
        mixed = fold(dot(jnp.concatenate(split(weights), axis=0), vert_v[rows, :], DOWN))
        mixed = mixed[:, :HEAD_SIZE] + mixed[:, HEAD_SIZE:] + keep * near[:, columns]
        out[0, :, columns] = mixed / total


def attend(q, near, stats, start, first_row, arrays):
    width = q.shape[1]
    heads = width // HEAD_SIZE
    pair = 2
    smem = pl.BlockSpec(memory_space=pltpu.SMEM)
    vmem = pl.BlockSpec(memory_space=pltpu.VMEM)
    base = start // TILE
    wide = (TILE, pair * HEAD_SIZE)
    return pl.pallas_call(
        functools.partial(attend_kernel, start),
        grid=(2, heads // pair),
        out_shape=jax.ShapeDtypeStruct((2, TILE, width), jnp.float32),
        in_specs=[
            smem,
            pl.BlockSpec(wide, lambda t, h: (base + t, h)),
            pl.BlockSpec(wide, lambda t, h: (base + t, h)),
            pl.BlockSpec((TILE, HEAD_SIZE), lambda t, h: (base + t, h)),
        ]
        + [vmem] * len(arrays),
        out_specs=pl.BlockSpec((1, TILE, pair * HEAD_SIZE), lambda t, h: (t, 0, h)),
        scratch_shapes=[pltpu.VMEM((heads * 8 * BLOCK, 2 * HEAD_SIZE), jnp.bfloat16)] * 2,
        compiler_params=pltpu.CompilerParams(vmem_limit_bytes=20 << 20),
        cost_estimate=LARGE,
    )(first_row, q, near, stats, *arrays)


def take_kernel(chips, one, two, three, near, far):
    width = one.shape[1]
    near[:, :width], near[:, width:] = one[...], two[...]
    far[:, :width], far[:, width:] = three[...], two[...]


def take_columns(weight, chips, width):
    rows = weight.shape[0]
    step = rows // 4
    out = jax.ShapeDtypeStruct((rows, 2 * width), jnp.float32)
    out_spec = pl.BlockSpec((step, 2 * width), lambda i, o: (i, 0))
    w_spec = lambda at: pl.BlockSpec((step, width), lambda i, o: (i, o[at]))
    return pl.pallas_call(
        take_kernel,
        out_shape=[out, out],
        grid_spec=pltpu.PrefetchScalarGridSpec(
            num_scalar_prefetch=1,
            grid=(rows // step,),
            in_specs=[w_spec(0), w_spec(1), w_spec(2)],
            out_specs=[out_spec, out_spec],
        ),
        compiler_params=pltpu.CompilerParams(vmem_limit_bytes=58 << 20),
        cost_estimate=SMALL,
    )(chips, weight, weight, weight)


def weight_term(x, block):
    high, low = split(block)
    return fold(dot(x, high, DOWN)) + dot(x[: x.shape[0] // 2], low, DOWN)


def stack(rows):
    return jnp.concatenate(split(rows), axis=0)


def chip_kernel(order, own_a, own_b, w, out, x):
    for kind in range(2):

        @pl.when((pl.program_id(0) == kind) & (pl.program_id(1) == 0))
        def _():
            x[...] = stack(jnp.concatenate([own_a[kind], own_b[kind]], axis=0))

    out[0] = weight_term(x[...], w[...])


def project_chip(own_a, own_b, weight, order):
    _, rows, depth = own_a.shape
    width = depth
    vmem = pl.BlockSpec(memory_space=pltpu.VMEM)
    return pl.pallas_call(
        chip_kernel,
        out_shape=jax.ShapeDtypeStruct((2, 2 * rows, 2 * width), jnp.float32),
        grid_spec=pltpu.PrefetchScalarGridSpec(
            num_scalar_prefetch=1,
            grid=(2, 2),
            in_specs=[vmem, vmem, pl.BlockSpec((depth, width), lambda k, j, o: (0, o[2 * k + j]))],
            out_specs=pl.BlockSpec((1, 2 * rows, width), lambda k, j, o: (k, 0, j)),
            scratch_shapes=[pltpu.VMEM((4 * rows, depth), jnp.bfloat16)],
        ),
        compiler_params=pltpu.CompilerParams(vmem_limit_bytes=20 << 20),
        cost_estimate=LARGE,
    )(order, own_a, own_b, weight)


def pair_kernel(cores, got_a, got_b, near, far, total, *refs):
    *there, here, x = refs
    width = here.shape[2] * 2 // len(there)
    for kind, (got, weight) in enumerate(((got_a, near), (got_b, far))):

        @pl.when((pl.program_id(0) == kind) & (pl.program_id(1) == 0))
        def _():
            x[...] = stack(got[...])

        @pl.when((pl.program_id(0) == kind) & (pl.program_id(1) == 0))
        def _():
            term = total[0] + weight_term(x[...], weight[...])
            mine = there[kind * len(there) // 2 : (kind + 1) * len(there) // 2]
            for at, out in enumerate(mine):
                out[...] = term[:, at * width : (at + 1) * width]

        @pl.when((pl.program_id(0) == kind) & (pl.program_id(1) == 1))
        def _():
            here[0] = total[0] + weight_term(x[...], weight[...])


def project_pair(got, near, far, total, unit, keep, cores):
    rows, depth = got[0].shape
    width = depth
    base = 0 if keep else 2
    vmem = pl.BlockSpec(memory_space=pltpu.VMEM)
    pieces = 4 if keep else 2
    here = jax.ShapeDtypeStruct((2, rows, width), jnp.float32)
    there = jax.ShapeDtypeStruct((rows, 2 * width // pieces), jnp.float32)
    w_spec = lambda side: pl.BlockSpec(
        (depth, width), lambda k, s, c: (0, base + c[side(k, s)])
    )
    *there, here = pl.pallas_call(
        pair_kernel,
        out_shape=[there] * pieces + [here],
        grid_spec=pltpu.PrefetchScalarGridSpec(
            num_scalar_prefetch=1,
            grid=(2, 2),
            in_specs=[
                vmem,
                vmem,
                w_spec(lambda k, s: jnp.where(k == 0, s, 1)),
                w_spec(lambda k, s: jnp.where(k == 0, 0, s)),
                pl.BlockSpec((1, rows, width), lambda k, s, c: (k, unit, s)),
            ],
            out_specs=[pl.BlockSpec(there.shape, lambda k, s, c: (0, 0))] * pieces
            + [pl.BlockSpec((1, rows, width), lambda k, s, c: (k, 0, 0))],
            scratch_shapes=[pltpu.VMEM((2 * rows, depth), jnp.bfloat16)],
        ),
        compiler_params=pltpu.CompilerParams(vmem_limit_bytes=16 << 20),
        cost_estimate=LARGE,
    )(cores, *got, near, far, total)
    return there, here


def body(
    queries, key_rows, value_vectors, vertical_blocks, slash_offsets, prompt_length, out_weight
):
    rows = queries.shape[0]
    blocks = rows // BLOCK
    heads = queries.shape[1] // HEAD_SIZE
    seq_index = lax.axis_index("seq")
    head_index = lax.axis_index("head")
    head_size = lax.axis_size("head")
    core = head_index % 2
    chips = head_size // 2

    x, z = seq_index % 4, seq_index // 4
    ids = range(lax.axis_size("seq"))
    right = [(i, i // 4 * 4 + (i + 1) % 4) for i in ids]
    left = [(i, i // 4 * 4 + (i + 3) % 4) for i in ids]
    over = [(i, i // 4 * 4 + (i + 2) % 4) for i in ids]
    up = [(i, (i + 4) % 16) for i in ids]
    down = [(i, (i + 12) % 16) for i in ids]
    send = lambda a, pairs: lax.ppermute(a, "seq", pairs)
    swapped = lambda a, bits: send(a, [(i, i ^ bits) for i in ids])

    k_left = send(key_rows, right)
    k_right = send(key_rows, left)
    v_below = send(value_vectors, up)

    y = head_index // 2
    over_head = lambda a, bits: lax.ppermute(a, "head", [(i, i ^ bits) for i in range(head_size)])
    width = out_weight.shape[1] // head_size
    near_weight, far_weight = take_columns(out_weight, y ^ jnp.arange(1, 4), 2 * width)
    near_weight, far_weight = over_head(near_weight, 2), over_head(far_weight, 6)

    vert = lax.dynamic_slice_in_dim(vertical_blocks, head_index * heads, heads, 0)
    slash = lax.dynamic_slice_in_dim(slash_offsets, head_index * heads, heads, 0)
    prompt = prompt_length[0]
    named = vert.reshape(-1)
    inside = jnp.arange(BLOCK, dtype=jnp.int32)
    vert_pos = vert[:, :, None] * BLOCK + inside
    vert_pos = jnp.where(vert_pos < prompt, -1, vert_pos).reshape(heads, 1, -1)
    offsets = jnp.concatenate([jnp.zeros((heads, 1), jnp.int32), slash + 1], axis=1)
    block_ids = seq_index * blocks + jnp.arange(blocks, dtype=jnp.int32)
    slash_block = block_ids[None, :, None] - offsets[:, None, :]
    repeated = jnp.any(slash_block[:, :, :, None] == vert[:, None, None, :], axis=-1)
    usable = (slash_block >= 0) & jnp.logical_not(repeated)
    slash_pos = slash_block[..., None] * BLOCK + inside
    slash_pos = jnp.where(slash_pos < prompt, -1, slash_pos)
    slash_pos = jnp.where(usable[..., None], slash_pos, FAR).reshape(heads, blocks, 1, -1)
    first_row = (seq_index * rows).reshape(1)
    back = 2 * blocks - offsets
    wraps = jnp.stack([x < 2, x == 0]).astype(jnp.int32)
    cores = jnp.stack([1 - core, core])
    pass_order = jnp.concatenate([2 * chip + cores for chip in (y ^ 3, y ^ 1)])
    keep_order = jnp.concatenate([2 * y + cores] * 2)
    owner = named // blocks
    at = named % blocks
    k_place, k_held = (owner % 4 - x) % 4 * blocks + at, (owner // 4 == z).astype(jnp.int32)
    v_place, v_held = (owner // 4 - z) % 4 * blocks + at, (owner % 4 == x).astype(jnp.int32)
    orders = (pass_order, keep_order, cores)
    small = (vert_pos, slash_pos, first_row, back, wraps, orders, k_place, k_held, v_place, v_held)

    k_left, late_values = lax.optimization_barrier((k_left, value_vectors))
    v_above = send(late_values, down)
    (k_left, k_right, v_below), small = lax.optimization_barrier(
        ((k_left, k_right, v_below), small)
    )
    vert_pos, slash_pos, first_row, back, wraps, orders, k_place, k_held, v_place, v_held = small
    half = rows // 2
    source = jnp.where(x >= 2, v_below, value_vectors)
    v_left = jnp.where(x == 3, v_below, value_vectors)
    moved_left = send(jnp.concatenate([k_right, source[half:]]), left)
    v_beyond = send(v_above, down)
    moved_right = send(jnp.concatenate([v_left, source[:half]]), right)
    k_left_wrap = send(k_left, [(i, i + 4) for i in ids if i % 4 == 0 and i + 4 in ids])
    moved_left, v_beyond, moved_right, k_left_wrap = lax.optimization_barrier(
        (moved_left, v_beyond, moved_right, k_left_wrap)
    )
    k_far, v_far_b = moved_left[:rows], moved_left[rows:]
    v_left, v_far_a = moved_right[:rows], moved_right[rows:]

    k_pieces = (key_rows, k_right, k_far, k_left)
    v_pieces = (value_vectors, v_above, v_beyond, v_below)
    named = pick_blocks(k_place, k_held, v_place, v_held, k_pieces, v_pieces)
    v_far_a = send(v_far_a, right)
    v_far_b = send(v_far_b, left)
    k_far_wrap = send(k_far, [(i, i + 4) for i in ids if i % 4 < 2 and i + 4 in ids])
    one, two = (4, 12, 1, 3), (12, 4, 3, 1)
    more = [swapped(a, bits) for a, bits in zip(named, one)]
    q = scaled(queries)
    q, v_far_a, v_far_b, k_far_wrap, *more = lax.optimization_barrier(
        (q, v_far_a, v_far_b, k_far_wrap, *more)
    )
    named = [a + b for a, b in zip(named, more)]
    arrays = (k_far, k_far_wrap, k_left, k_left_wrap, key_rows, v_far_a, v_far_b, v_left)
    near_arrays = (*arrays, value_vectors, slash_pos)
    near = attend_near(q, 0, rows, first_row, back, wraps, near_arrays)
    more = [swapped(a, bits) for a, bits in zip(named, two)]
    near, more = lax.optimization_barrier((near, more))
    arrays = (*(a + b for a, b in zip(named, more)), vert_pos)

    pass_order, keep_order, cores = orders
    meet, end = (2, 6), (6, 2)
    own_a = attend(q, *near, 0, first_row, arrays)
    q, own_a = lax.optimization_barrier((q, own_a))
    meeting = lambda parts: [over_head(parts[i], bits) for i, bits in enumerate(meet)]
    ending = lambda parts: [over_head(parts[i], bits) for i, bits in enumerate(end)]
    got_a = meeting(own_a)
    own_b = attend(q, *near, half, first_row, arrays)
    got_b = meeting(own_b)
    own_b, near_weight, far_weight = lax.optimization_barrier((own_b, near_weight, far_weight))
    total = project_chip(own_a, own_b, out_weight, pass_order)
    total, got_a = lax.optimization_barrier((total, got_a))
    product = lambda got, total, unit, keep: project_pair(
        got, near_weight, far_weight, total, unit, keep, cores
    )
    there_a, here_a = product(got_a, total, 0, False)
    there_a, here_a, got_a, got_b = lax.optimization_barrier((there_a, here_a, got_a, got_b))
    across = lambda parts: [over_head(a, 1) for a in parts]
    moved_a = across(there_a)
    there_b, here_b = product(got_b, total, 1, False)
    there_b, here_b, moved_a = lax.optimization_barrier((there_b, here_b, moved_a))
    moved = zip(moved_a, across(there_b))
    passed = [
        jnp.concatenate([here_a[i] + a, here_b[i] + b]) for i, (a, b) in enumerate(moved)
    ]
    passed, got_a, got_b, own_b = lax.optimization_barrier((passed, got_a, got_b, own_b))
    sent = ending(passed)
    kept_total = project_chip(own_a, own_b, out_weight, keep_order)
    keep_a = product(got_a, kept_total, 0, True)
    keep_b = product(got_b, kept_total, 1, True)
    kept = []
    for there, here in (keep_a, keep_b):
        moved = across(there)
        kept += [here[i] + jnp.concatenate(moved[2 * i : 2 * i + 2], axis=1) for i in range(2)]
    rows = kept[0].shape[0]
    sent = (sent[0][:rows], sent[1][:rows], sent[0][rows:], sent[1][rows:])
    return jnp.concatenate([a + b for a, b in zip(kept, sent)], axis=0)


def solution(mesh):
    placed = (P("seq", "head"), P("seq", "head"), P("seq", "head"), P(), P(), P(), P("head", None))
    return jax.shard_map(
        body, mesh=mesh, in_specs=placed, out_specs=P("seq", "head"), check_vma=False
    )
```
